32 devices in a mesh: grp: 4 (over y, core), shard: 8 (over z, x).
Axes of the slice: x: 2, y: 2, z: 4, core: 2. Of those that a mesh axis runs over, the one named last changes fastest.
Arguments:
- entity_rows: float32 [8192, 400], P('shard'), may hold values from -6 to 6
- entity_first: float32 [8192, 400], P('shard'), may hold values from -1.9073486e-06 to 1.9073486e-06
- entity_second: float32 [8192, 400], P('shard'), may hold values from 1.8335413e-15 to 7.334165e-15
- relation_rows: float32 [6272, 400], P('shard'), may hold values from -6 to 6
- relation_first: float32 [6272, 400], P('shard'), may hold values from -2.3841858e-06 to 2.3841858e-06
- relation_second: float32 [6272, 400], P('shard'), may hold values from 2.2617834e-15 to 9.0471335e-15
- requests: int32 [32, 8, 40], P(('grp', 'shard')), may hold values from 0 to 1807, as said below
- head_slots: int32 [32768], P(('grp', 'shard')), may hold values from 0 to 311, as said below
- relation_slots: int32 [32768], P(('grp', 'shard')), may hold values from 32 to 319, as said below
- tail_slots: int32 [32768], P(('grp', 'shard')), may hold values from 0 to 311, as said below
- neg_offsets: int32 [32768, 16], P(('grp', 'shard')), may hold values from 0 to 127
- valid_counts: int32 [32], P(('grp', 'shard')), may hold values from 1 to 1024
Outputs:
- entity_new: float32 [8192, 400], P('shard')
- entity_moment_one: float32 [8192, 400], P('shard')
- entity_moment_two: float32 [8192, 400], P('shard')
- relation_new: float32 [6272, 400], P('shard')
- relation_moment_one: float32 [6272, 400], P('shard')
- relation_moment_two: float32 [6272, 400], P('shard')
- entity_low: bfloat16 [8192, 400], P('shard')
- relation_low: bfloat16 [6272, 400], P('shard')
- loss_sum: float32 [1], replicated
- pair_count: float32 [1], replicated
The draws below stay inside these ranges and needn't reach their ends.
Inputs may be any that keep to these rules, and one draw needn't show every extreme that they name: Entries 0 to 31 of each requests[d, p] name entity rows (below 1024), entries 32 to 39 name relation rows (1024 plus a relation index); the distinct ones come first, and the remaining slots repeat the first entry of their kind; for each device, the slots of at least one owner are all distinct in each kind. `head_slots`: head slots name distinct entity slots (c below 32) of their owner. `relation_slots`: relation slots name distinct relation slots (c at least 32) of their owner. `tail_slots`: tail slots name distinct entity slots of their owner.
All inputs are finite; a program needn't handle non-finite values.
Results may differ from the reference program's by a relative error of at most 0.001.
Values sent between devices are 32-bit elements; how exact they have to be, the bound alone decides.
A program may use at most 128 MiB of HBM per device.

```python
import math
import jax
import jax.numpy as jnp
from jax import lax

D = 400
E_DEV = 1024
R_DEV = 784
CAP_E = 32
CAP_R = 8
EDGE_DEV = 1024
SEG = 128
NEG = 16
STEP = 10
CAP = 40
ENT = 8192
REL = 6272
EDGES = 32768
N_GRP = 4
N_SHARD = 8
DEVICES = 32


def slot_counts(key):
    key = jax.random.fold_in(key, 11)
    keys = jax.random.split(key, 3)
    entity_count = jax.random.randint(keys[0], (DEVICES, N_SHARD), max(CAP_E // 2, 1), CAP_E + 1)
    relation_count = jax.random.randint(keys[1], (DEVICES, N_SHARD), max(CAP_R // 2, 1), CAP_R + 1)
    full_peer = jax.random.randint(keys[2], (DEVICES, 1), 0, N_SHARD)
    full_peer = full_peer.at[0, 0].set(N_SHARD - 1)
    peer_index = jnp.arange(N_SHARD, dtype=jnp.int32)[None, :]
    entity_count = jnp.where(peer_index == full_peer, CAP_E, entity_count)
    relation_count = jnp.where(peer_index == full_peer, CAP_R, relation_count)
    return (entity_count, relation_count)


def pick_rows(key, count, rows, width, offset):
    order = jnp.broadcast_to(jnp.arange(rows, dtype=jnp.int32), (DEVICES, N_SHARD, rows))
    order = jax.random.permutation(key, order, axis=2, independent=True)[:, :, :width]
    slot_index = jnp.arange(width, dtype=jnp.int32)[None, None, :]
    picked = jnp.where(slot_index < count[:, :, None], order, order[:, :, :1])
    return picked + offset


def draw_requests(key, part):
    entity_count, relation_count = slot_counts(key)
    key = jax.random.fold_in(key, 1)
    key_entity, key_relation = jax.random.split(key)
    entity_ids = pick_rows(key_entity, entity_count, E_DEV, CAP_E, 0)
    relation_ids = pick_rows(key_relation, relation_count, R_DEV, CAP_R, E_DEV)
    return jnp.concatenate([entity_ids, relation_ids], axis=2).astype(jnp.int32)


def pick_slots(key, count, offset):
    key_peer, key_slot = jax.random.split(key)
    peer = jax.random.randint(key_peer, (DEVICES, EDGE_DEV), 0, N_SHARD)
    peer = peer.at[0, 0].set(N_SHARD - 1).at[0, 1].set(0)
    limit = jnp.take_along_axis(count, peer, axis=1)
    within = jax.random.randint(key_slot, (DEVICES, EDGE_DEV), 0, limit)
    within = within.at[0, 0].set(limit[0, 0] - 1).at[0, 1].set(0)
    return (peer * CAP + offset + within).reshape(DEVICES * EDGE_DEV).astype(jnp.int32)


def draw_head_slots(key, part):
    entity_count, relation_count = slot_counts(key)
    key = jax.random.fold_in(key, 2)
    return pick_slots(key, entity_count, 0)


def draw_tail_slots(key, part):
    entity_count, relation_count = slot_counts(key)
    key = jax.random.fold_in(key, 3)
    return pick_slots(key, entity_count, 0)


def draw_relation_slots(key, part):
    entity_count, relation_count = slot_counts(key)
    key = jax.random.fold_in(key, 4)
    return pick_slots(key, relation_count, CAP_E)


def draw_valid_counts(key, part):
    key = jax.random.fold_in(key, 5)
    device_index = jnp.arange(DEVICES, dtype=jnp.int32)
    group_index = device_index // N_SHARD
    shard_index = device_index % N_SHARD
    rise_group = N_GRP - 1 + 2 * group_index
    rise_shard = N_SHARD - 1 + 2 * shard_index
    base = EDGE_DEV * rise_group * rise_shard // (9 * (N_GRP - 1) * (N_SHARD - 1))
    jitter = jax.random.randint(key, (DEVICES,), 0, EDGE_DEV // 16 + 2)
    jitter = jnp.where(device_index < DEVICES - 1, jitter, 0)
    return jnp.clip(base - jitter, 1, EDGE_DEV).astype(jnp.int32)


def plant(values, rng, smallest, largest):
    place = [jax.random.randint(jax.random.fold_in(rng, axis), (), 0, length) for axis, length in enumerate(values.shape)]
    widest = values.shape.index(max(values.shape))
    next_to = place[:widest] + [(place[widest] + 1) % values.shape[widest]] + place[widest + 1:]
    return values.at[tuple(place)].set(smallest).at[tuple(next_to)].set(largest)


def shard_levels(stream_key, extent, pieces, smallest, high):
    level, own = 1.0, jax.random.fold_in(stream_key, 6)
    for position, blocks in pieces:
        heights = jnp.exp(jax.random.uniform(jax.random.fold_in(own, position), (blocks,), jnp.float32, smallest / len(pieces), high / len(pieces)))
        level = level * jnp.repeat(heights, extent[position] // blocks).reshape([-1 if axis == position else 1 for axis in range(len(extent))])
    return level


def normal_values(key, dims, deviation, most, cuts=(), kind=jnp.bfloat16):
    entries = deviation * jax.random.normal(key, dims, jnp.float32)
    if cuts:
        entries = entries * shard_levels(key, dims, cuts, -0.22, 0.18)
    return jnp.clip(entries, -most, most).astype(kind)


def setup_inputs(seed: int = 0) -> dict:
    arg_keys = jax.random.split(jax.random.key(seed), 13)
    entity_rows = normal_values(arg_keys[0], (ENT, D), 1.0, 6.0, ((0, 8),), jnp.float32)
    entity_first = normal_values(arg_keys[1], (ENT, D), (0.1 * (2.8 * (NEG + 2) / (DEVICES * EDGE_DEV * NEG * NEG * N_SHARD * E_DEV * D)) ** 0.5), 1.9073486328125e-06, ((0, 8),), jnp.float32)
    entity_second = jnp.clip(jnp.exp(math.log(7.334165216875237e-15) - 1.3862944 * jax.random.uniform(arg_keys[2], (ENT, D), jnp.float32) ** shard_levels(arg_keys[2], (ENT, D), ((0, 8),), -0.2, 0.2)), 1.833541304218809e-15, 7.334165216875237e-15)
    relation_rows = normal_values(arg_keys[3], (REL, D), 1.0, 6.0, ((0, 8),), jnp.float32)
    relation_first = normal_values(arg_keys[4], (REL, D), (0.1 * (2.8 * (NEG + 1) / (DEVICES * EDGE_DEV * NEG * NEG * N_SHARD * R_DEV * D)) ** 0.5), 2.384185791015625e-06, ((0, 8),), jnp.float32)
    relation_second = jnp.clip(jnp.exp(math.log(9.047133498634764e-15) - 1.3862944 * jax.random.uniform(arg_keys[5], (REL, D), jnp.float32) ** shard_levels(arg_keys[5], (REL, D), ((0, 8),), -0.2, 0.2)), 2.261783374658691e-15, 9.047133498634764e-15)
    requests = draw_requests(jax.random.fold_in(arg_keys[12], 71), 0)
    head_slots = draw_head_slots(jax.random.fold_in(arg_keys[12], 71), 0)
    relation_slots = draw_relation_slots(jax.random.fold_in(arg_keys[12], 71), 0)
    tail_slots = draw_tail_slots(jax.random.fold_in(arg_keys[12], 71), 0)
    neg_offsets = plant(jax.random.randint(arg_keys[10], (EDGES, NEG), 0, SEG), jax.random.fold_in(arg_keys[10], 1), 0, SEG - 1).astype(jnp.int32)
    valid_counts = draw_valid_counts(jax.random.fold_in(arg_keys[12], 71), 0)
    return {"entity_rows": entity_rows, "entity_first": entity_first, "entity_second": entity_second, "relation_rows": relation_rows, "relation_first": relation_first, "relation_second": relation_second, "requests": requests, "head_slots": head_slots, "relation_slots": relation_slots, "tail_slots": tail_slots, "neg_offsets": neg_offsets, "valid_counts": valid_counts}


MARGIN = 0.1
EPS_DIST = 1e-06
BETA_ONE = 0.9
BETA_TWO = 0.999
RATE = 0.5
DECAY = 0.01
EPS_ADAM = 1e-08

@jax.custom_vjp
def low(v):
    return lax.optimization_barrier(v.astype(jnp.bfloat16)).astype(jnp.float32)

@jax.custom_vjp
def low_back(v):
    return v

def low_keep(v):
    return (low(v), None)

def low_pass(kept, grad):
    return (grad,)

def back_keep(v):
    return (v, None)

def back_low(kept, grad):
    return (low(grad),)
low.defvjp(low_keep, low_pass)
low_back.defvjp(back_keep, back_low)

def pair_terms(fetched, head_slot, relation_slot, tail_slot, offsets, valid):
    anchor = fetched[head_slot] + fetched[relation_slot]
    target = fetched[tail_slot]
    dist_pos = jnp.sqrt(lax.optimization_barrier(jnp.sum((anchor - target) ** 2, axis=1)) + EPS_DIST)
    edge_index = jnp.arange(EDGE_DEV, dtype=jnp.int32)
    neg_edge = edge_index[:, None] // SEG * SEG + offsets
    negative = target[neg_edge]
    dist_neg = jnp.sqrt(lax.optimization_barrier(jnp.sum((anchor[:, None, :] - negative) ** 2, axis=2)) + EPS_DIST)
    valid_mask = (edge_index[:, None] < valid) & (neg_edge < valid) & (neg_edge != edge_index[:, None])
    weights = valid_mask.astype(jnp.float32)
    terms = jax.nn.softplus(MARGIN + dist_pos[:, None] - dist_neg) * weights
    return (jnp.sum(terms), jnp.sum(weights))

def adamw(weight, moment_one, moment_two, gradient):
    moment_one = BETA_ONE * moment_one + (1.0 - BETA_ONE) * gradient
    moment_two = BETA_TWO * moment_two + (1.0 - BETA_TWO) * gradient * gradient
    fix_one = 1.0 - BETA_ONE ** STEP
    fix_two = 1.0 - BETA_TWO ** STEP
    direction = moment_one / fix_one / (jnp.sqrt(moment_two / fix_two) + EPS_ADAM)
    return (weight - RATE * (direction + DECAY * weight), moment_one, moment_two)

def reference(entity_rows, entity_first, entity_second, relation_rows, relation_first, relation_second, requests, head_slots, relation_slots, tail_slots, neg_offsets, valid_counts):
    peer_index = jnp.arange(N_SHARD, dtype=jnp.int32)[:, None]
    device_items = (requests, head_slots.reshape(DEVICES, EDGE_DEV), relation_slots.reshape(DEVICES, EDGE_DEV), tail_slots.reshape(DEVICES, EDGE_DEV), neg_offsets.reshape(DEVICES, EDGE_DEV, NEG), valid_counts)

    def total(entity, relation):
        owner_rows = jnp.concatenate([entity.reshape(N_SHARD, E_DEV, D), relation.reshape(N_SHARD, R_DEV, D)], axis=1)

        def per_device(running, items):
            ids, head_slot, relation_slot, tail_slot, offsets, valid = items
            fetched = owner_rows[peer_index, ids].reshape(N_SHARD * CAP, D)
            loss_part, pair_part = pair_terms(fetched, head_slot, relation_slot, tail_slot, offsets, valid)
            return ((running[0] + loss_part, running[1] + pair_part), None)
        start = (jnp.zeros((), jnp.float32), jnp.zeros((), jnp.float32))
        (loss_total, pair_total), _ = lax.scan(jax.checkpoint(per_device), start, device_items)
        return (loss_total / pair_total, (loss_total, pair_total))
    loss_value, backward, (loss_total, pair_total) = jax.vjp(total, entity_rows, relation_rows, has_aux=True)
    entity_grad, relation_grad = backward(jnp.ones((), loss_value.dtype))
    entity_new, entity_one, entity_two = adamw(entity_rows, entity_first, entity_second, entity_grad)
    relation_new, relation_one, relation_two = adamw(relation_rows, relation_first, relation_second, relation_grad)
    return (entity_new, entity_one, entity_two, relation_new, relation_one, relation_two, entity_new.astype(jnp.bfloat16), relation_new.astype(jnp.bfloat16), loss_total.reshape(1), pair_total.reshape(1))
```

```python
import functools

import jax
import jax.numpy as jnp
from jax import lax
from jax.experimental import pallas as pl
from jax.experimental.pallas import tpu as pltpu
from jax.sharding import PartitionSpec as P

CAP_E = 32
SEG = 128
STEP = 10
LANE = 128

MARGIN = 0.1
EPS_DIST = 1e-06
BETA_ONE = 0.9
BETA_TWO = 0.999
RATE = 0.5
DECAY = 0.01
EPS_ADAM = 1e-08

F32 = jnp.float32
BF16 = jnp.bfloat16
I32 = jnp.int32


def mm(a, b):
    return lax.dot_general(a, b, (((1,), (0,)), ((), ())), preferred_element_type=F32)


def mm_nt(a, b):
    return lax.dot_general(a, b, (((1,), (1,)), ((), ())), preferred_element_type=F32)


def halves(x):
    hi = x.astype(BF16)
    return hi, (x - hi.astype(F32)).astype(BF16)


def up(n, m):
    return (n + m - 1) // m * m


def iota(shape, axis):
    return lax.broadcasted_iota(I32, shape, axis)


def far_first(n):
    return sorted(range(1, n), key=lambda k: (abs(k - n // 2), k))


def exchange_kernel(
    ns,
    ng,
    dims,
    valid_ref,
    ent_hbm,
    rel_hbm,
    req_hbm,
    head_hbm,
    rslot_hbm,
    tail_hbm,
    neg_hbm,
    ge_ref,
    gr_ref,
    stat_ref,
    ent_v,
    rel_v,
    req_v,
    slots_v,
    neg_v,
    eth,
    etl,
    rth,
    rtl,
    ids_all,
    idg,
    send_buf,
    recv_buf,
    rows_e,
    rows_r,
    oh_e,
    oh_r,
    hot_h,
    hot_t,
    hot_r,
    hott,
    hott_r,
    wt,
    eh,
    el,
    rr,
    gg_h,
    gg_l,
    gbuf,
    sgt_e,
    sgt_r,
    local_sem,
    ids_send,
    ids_recv,
    idg_send,
    idg_recv,
    f_send,
    f_recv,
    g_send,
    g_recv,
    core_send,
    y_send,
):
    d, ne, nr, cap, edges, neg = dims
    cap_r = cap - CAP_E
    ke, kr = ns * CAP_E, ns * cap_r
    chunks = d // LANE
    rest = d - chunks * LANE
    dp = (chunks + 1) * LANE
    nrp = up(nr, LANE)
    segs = edges // SEG
    copies = LANE // rest
    subs = cap // 8
    ny = ng // 2

    g = lax.axis_index("grp")
    s = lax.axis_index("shard")
    mate = g + 1 - 2 * lax.rem(g, 2)
    order = far_first(ns)

    def shard_at(k):
        return lax.rem(s + k, ns)

    def shard_from(k):
        return lax.rem(s + ns - k, ns)

    barrier = pltpu.get_barrier_semaphore()
    for k in range(1, ns):
        pl.semaphore_signal(barrier, inc=1, device_id={"shard": shard_at(k)})
    for k in range(1, ng):
        pl.semaphore_signal(barrier, inc=1, device_id={"grp": lax.rem(g + k, ng)})

    local = [
        pltpu.make_async_copy(src, dst, local_sem.at[i])
        for i, (src, dst) in enumerate(
            [
                (req_hbm, req_v),
                (ent_hbm, ent_v),
                (rel_hbm, rel_v),
                (head_hbm, slots_v.at[0]),
                (rslot_hbm, slots_v.at[1]),
                (tail_hbm, slots_v.at[2]),
                (neg_hbm, neg_v),
            ]
        )
    ]
    for copy in local:
        copy.start()
    local[0].wait()
    pl.semaphore_wait(barrier, ns - 1 + ng - 1)

    def ids_copy(k):
        return pltpu.make_async_remote_copy(
            src_ref=req_v,
            dst_ref=ids_all.at[s],
            send_sem=ids_send.at[k],
            recv_sem=ids_recv.at[s],
            device_id={"shard": shard_at(k)},
        )

    def ids_arrival(k):
        return pltpu.make_async_remote_copy(
            src_ref=req_v,
            dst_ref=ids_all.at[shard_from(k)],
            send_sem=ids_send.at[k],
            recv_sem=ids_recv.at[shard_from(k)],
            device_id={"shard": shard_from(k)},
        )

    for k in order:
        ids_copy(k).start()
    ids_all[s] = req_v[...]

    local[1].wait()
    local[2].wait()

    def split_rows(i, _):
        at = pl.ds(pl.multiple_of(i * 16, 16), 16)
        hi, lo = halves(ent_v[at, :])
        eth[at, :] = hi
        etl[at, :] = lo
        hi, lo = halves(rel_v[at, :])
        rth[at, 0:nr] = hi
        rtl[at, 0:nr] = lo
        return 0

    if nrp > nr:
        rth[:, nr:nrp] = jnp.zeros((dp, nrp - nr), BF16)
        rtl[:, nr:nrp] = jnp.zeros((dp, nrp - nr), BF16)
    lax.fori_loop(0, d // 16, split_rows, 0)
    for table in (eth, etl, rth, rtl):
        tail_rows = table[chunks * LANE : d, :]
        for c in range(1, copies):
            table[chunks * LANE + c * rest : chunks * LANE + (c + 1) * rest, :] = tail_rows

    for k in order:
        ids_arrival(k).wait_recv()
    for r in range(ns):
        idg[g, r : r + 1, :] = ids_all[r, pl.ds(s, 1), :]

    def idg_copy(k):
        return pltpu.make_async_remote_copy(
            src_ref=idg.at[g],
            dst_ref=idg.at[g],
            send_sem=idg_send.at[k],
            recv_sem=idg_recv.at[g],
            device_id={"grp": lax.rem(g + k, ng)},
        )

    def idg_arrival(k):
        other = lax.rem(g + ng - k, ng)
        return pltpu.make_async_remote_copy(
            src_ref=idg.at[other],
            dst_ref=idg.at[other],
            send_sem=idg_send.at[k],
            recv_sem=idg_recv.at[other],
            device_id={"grp": other},
        )

    def one_hots(grp):
        wide = jnp.concatenate([idg[grp].astype(F32), jnp.zeros((ns, LANE - cap), F32)], axis=1)
        columns = jnp.concatenate([wide] + [jnp.zeros((LANE - ns, LANE), F32)], axis=0).T
        lanes_e = iota((CAP_E, ne), 1).astype(F32)
        lanes_r = iota((cap_r, nrp), 1).astype(F32) + float(ne)
        pieces = []
        for r in range(ns):
            column = columns[:, r : r + 1]
            hit = jnp.where(column[0:CAP_E] == lanes_e, 1.0, 0.0).astype(BF16)
            oh_e[r * CAP_E : (r + 1) * CAP_E, :] = hit
            pieces.append(jnp.where(column[CAP_E:cap] == lanes_r, 1.0, 0.0))
        for r in range(0, ns, 2):
            oh_r[r * cap_r : (r + 2) * cap_r, :] = jnp.concatenate(pieces[r : r + 2], axis=0).astype(BF16)

    one_hots(g)
    rows_e[...] = mm_nt(oh_e[...], eth[...]) + mm_nt(oh_e[...], etl[...])
    rows_r[...] = mm_nt(oh_r[...], rth[...]) + mm_nt(oh_r[...], rtl[...])

    lane8 = iota((8, LANE), 1)

    def pack(r, roll, extra):
        for c in range(chunks):
            at = slice(c * LANE, (c + 1) * LANE)
            send_buf[r, c * cap : c * cap + CAP_E, :] = rows_e[r * CAP_E : (r + 1) * CAP_E, at]
            send_buf[r, c * cap + CAP_E : (c + 1) * cap, :] = rows_r[r * cap_r : (r + 1) * cap_r, at]
        last = slice(chunks * LANE, dp)
        out = extra
        for j in range(subs):
            if j * 8 < CAP_E:
                piece = rows_e[r * CAP_E + j * 8 : r * CAP_E + j * 8 + 8, last]
            else:
                piece = rows_r[r * cap_r + j * 8 - CAP_E : r * cap_r + j * 8 - CAP_E + 8, last]
            if roll and j:
                piece = pltpu.roll(piece, j * rest, 1)
            out = jnp.where((lane8 >= j * rest) & (lane8 < (j + 1) * rest), piece, out)
        send_buf[r, chunks * cap : chunks * cap + 8, :] = out

    def last_columns(tile):
        pieces = []
        for j in range(subs):
            piece = pltpu.roll(tile, LANE - j * rest, 1) if j else tile
            pieces.append(jnp.where(lane8 < rest, piece, 0.0))
        return jnp.concatenate(pieces[: CAP_E // 8], axis=0), jnp.concatenate(pieces[CAP_E // 8 :], axis=0)

    def fetch_copy(k):
        peer = shard_at(k)
        return pltpu.make_async_remote_copy(
            src_ref=send_buf.at[peer],
            dst_ref=recv_buf.at[s],
            send_sem=f_send.at[k],
            recv_sem=f_recv.at[s],
            device_id={"shard": peer},
        )

    def fetch_arrival(k):
        peer = shard_from(k)
        return pltpu.make_async_remote_copy(
            src_ref=send_buf.at[peer],
            dst_ref=recv_buf.at[peer],
            send_sem=f_send.at[k],
            recv_sem=f_recv.at[peer],
            device_id={"shard": peer},
        )

    for r in range(ns):
        pack(r, False, jnp.zeros((8, LANE), F32))
    for k in order:
        fetch_copy(k).start()
    recv_buf[s] = send_buf[s]
    for k in range(1, ng):
        idg_copy(k).start()

    for copy in local[3:]:
        copy.wait()
    slots = slots_v[...]
    owner = lax.shift_right_logical(slots * ((1 << 16) // cap + 1), 16)
    within = slots - owner * cap
    head_k = owner[0] * CAP_E + within[0]
    rel_k = owner[1] * cap_r + within[1] - CAP_E
    tail_k = owner[2] * CAP_E + within[2]
    for i in range(segs):
        at = slice(i * SEG, (i + 1) * SEG)
        head_row, rel_row, tail_row = (v[i : i + 1, :] for v in (head_k, rel_k, tail_k))
        hott[:, at] = jnp.where(iota((ke, SEG), 0) == head_row, 1.0, 0.0).astype(BF16)
        hott[:, edges + i * SEG : edges + (i + 1) * SEG] = jnp.where(
            iota((ke, SEG), 0) == tail_row, 1.0, 0.0
        ).astype(BF16)
        hott_r[:, at] = jnp.where(iota((kr, SEG), 0) == rel_row, 1.0, 0.0).astype(BF16)
        head_col, rel_col, tail_col = (
            jnp.broadcast_to(v.astype(F32), (SEG, SEG)).T[:, 0:1] for v in (head_row, rel_row, tail_row)
        )
        lanes_e = iota((SEG, ke), 1).astype(F32)
        lanes_r = iota((SEG, kr), 1).astype(F32)
        hot_h[at, :] = jnp.where(lanes_e == head_col, 1.0, 0.0).astype(BF16)
        hot_t[at, :] = jnp.where(lanes_e == tail_col, 1.0, 0.0).astype(BF16)
        hit = jnp.where(lanes_r == rel_col, 1.0, 0.0)
        hot_r[at, :] = jnp.concatenate([hit, hit], axis=1).astype(BF16)

    valid = valid_ref[0]
    sub = iota((SEG, SEG), 0)
    lane = iota((SEG, SEG), 1)

    def count(i, total):
        start = pl.multiple_of(i * SEG, SEG)
        hits = jnp.zeros((SEG, SEG), F32)
        for k in range(neg):
            hits += jnp.where(neg_v[k : k + 1, pl.ds(start, SEG)] == sub, 1.0, 0.0)
        keep = (lane + start < valid) & (sub + start < valid) & (sub != lane)
        hits = jnp.where(keep, hits, 0.0)
        wt[i] = hits
        return total + hits

    pairs = jnp.sum(lax.fori_loop(0, segs, count, jnp.zeros((SEG, SEG), F32)))

    recv = [(s, None)] + [(shard_from(k), k) for k in order]
    for src, k in recv:
        if k is not None:
            fetch_arrival(k).wait_recv()
    for p in range(ns):
        ends_e, ends_r = last_columns(recv_buf[p, chunks * cap : chunks * cap + 8, :])
        e = jnp.concatenate(
            [recv_buf[p, c * cap : c * cap + CAP_E, :] for c in range(chunks)] + [ends_e], axis=1
        )
        r = jnp.concatenate(
            [recv_buf[p, c * cap + CAP_E : (c + 1) * cap, :] for c in range(chunks)] + [ends_r], axis=1
        )
        at = slice(p * CAP_E, (p + 1) * CAP_E)
        eh[at, :], el[at, :] = halves(e)
        rows_r[p * cap_r : (p + 1) * cap_r, :] = r
    hi, lo = halves(rows_r[...])
    rr[0:kr, :] = hi
    rr[kr : 2 * kr, :] = lo

    def lane_fold(x):
        out = x[:, 0:LANE]
        for c in range(1, dp // LANE):
            out += x[:, c * LANE : (c + 1) * LANE]
        return out

    def edge_step(i, loss):
        at = pl.ds(pl.multiple_of(i * SEG, SEG), SEG)
        at_t = pl.ds(pl.multiple_of(edges + i * SEG, SEG), SEG)
        a = mm(hot_h[at, :], eh[...]) + mm(hot_h[at, :], el[...]) + mm(hot_r[at, :], rr[...])
        t = mm(hot_t[at, :], eh[...]) + mm(hot_t[at, :], el[...])
        ah, al = halves(a)
        th, tl = halves(t)
        aa = jnp.concatenate([ah, al], axis=0)
        tt = jnp.concatenate([th, tl], axis=0)
        offset = a - t
        dist_pos = jnp.sqrt(jnp.sum(lane_fold(offset * offset).T, axis=0, keepdims=True) + EPS_DIST)
        anchor_sq = jnp.sum(lane_fold(a * a).T, axis=0, keepdims=True)
        target_sq = jnp.sum(lane_fold(t * t), axis=1, keepdims=True)
        near = mm_nt(th, aa)
        far = mm_nt(tl, aa)
        gram = near[:, 0:SEG] + (near[:, SEG:] + far[:, 0:SEG] + far[:, SEG:])
        square = jnp.maximum(anchor_sq + target_sq - 2.0 * gram, 0.0) + EPS_DIST
        inv = lax.rsqrt(square)
        m = MARGIN + dist_pos - square * inv
        w = wt[i]
        small = jnp.exp(-jnp.abs(m))
        loss += w * (jnp.maximum(m, 0.0) + jnp.log1p(small))
        slope = w * (jnp.where(m >= 0.0, 1.0, small) / (1.0 + small))
        ratio = jnp.sum(slope, axis=0, keepdims=True) / dist_pos
        pt = slope * inv - jnp.where(sub == lane, ratio, 0.0)
        pa = pt.T
        row_t = jnp.sum(pt, axis=1, keepdims=True)
        row_a = jnp.sum(pa, axis=1, keepdims=True)
        pth, ptl = halves(pt)
        pah, pal = halves(pa)
        grad_t = mm(jnp.concatenate([pth, pth], axis=1), aa) + mm(ptl, ah) - row_t * t
        grad_a = mm(jnp.concatenate([pah, pah], axis=1), tt) + mm(pal, th) - row_a * a
        gg_h[at, :], gg_l[at, :] = halves(grad_a)
        gg_h[at_t, :], gg_l[at_t, :] = halves(grad_t)
        return loss

    loss = jnp.sum(lax.fori_loop(0, segs, edge_step, jnp.zeros((SEG, SEG), F32)))

    rows_e[...] = mm(hott[...], gg_h[...]) + mm(hott[...], gg_l[...])
    rows_r[...] = mm(hott_r[...], gg_h[0:edges, :]) + mm(hott_r[...], gg_l[0:edges, :])
    at_loss = copies * rest - 2
    extra = jnp.where(lane8 == at_loss, loss, jnp.where(lane8 == at_loss + 1, pairs, 0.0))

    def grad_copy(k):
        peer = shard_at(k)
        return pltpu.make_async_remote_copy(
            src_ref=send_buf.at[peer],
            dst_ref=gbuf.at[g, s],
            send_sem=g_send.at[k],
            recv_sem=g_recv.at[g, s],
            device_id={"shard": peer},
        )

    def block_copy(grp, src, to, send_sem):
        return pltpu.make_async_remote_copy(
            src_ref=gbuf.at[grp, src],
            dst_ref=gbuf.at[grp, src],
            send_sem=send_sem,
            recv_sem=g_recv.at[grp, src],
            device_id={"grp": to},
        )

    def arrived(grp, src):
        block_copy(grp, src, mate, core_send.at[0, 0]).wait_recv()

    for k in order:
        fetch_copy(k).wait_send()
    for r in range(ns):
        pack(r, True, extra)
    for k in order:
        grad_copy(k).start()
    gbuf[g, s] = send_buf[s]

    def group_up(dy):
        return lax.rem(g + 2 * dy, ng)

    def group_down(dy):
        return lax.rem(g + ng - 2 * dy, ng)

    def forward(src):
        out = [block_copy(g, src, mate, core_send.at[0, src])]
        for dy in range(1, ny):
            out.append(block_copy(g, src, group_up(dy), y_send.at[dy - 1, src]))
        return out

    def hand_over(dy, src):
        return block_copy(group_down(dy), src, mate, core_send.at[dy, src])

    sequence = [0] + order
    lag = 2

    def hand_over_all(idx):
        src = shard_from(sequence[idx])
        for dy in range(1, ny):
            arrived(group_down(dy), src)
            hand_over(dy, src).start()

    for idx, k in enumerate(sequence):
        src = shard_from(k)
        if k:
            arrived(g, src)
        for copy in forward(src):
            copy.start()
        if idx >= lag:
            hand_over_all(idx - lag)

    def gather_blocks(grp):
        for r in range(ns):
            ends_e, ends_r = last_columns(gbuf[grp, r, chunks * cap : chunks * cap + 8, :])
            rows_e[r * CAP_E : (r + 1) * CAP_E, chunks * LANE : dp] = ends_e
            rows_r[r * cap_r : (r + 1) * cap_r, chunks * LANE : dp] = ends_r
            for c in range(chunks):
                at = slice(c * LANE, (c + 1) * LANE)
                rows_e[r * CAP_E : (r + 1) * CAP_E, at] = gbuf[grp, r, c * cap : c * cap + CAP_E, :]
                rows_r[r * cap_r : (r + 1) * cap_r, at] = gbuf[grp, r, c * cap + CAP_E : (c + 1) * cap, :]
        for c in range(chunks + 1):
            at = slice(c * LANE, (c + 1) * LANE)
            size = LANE if c < chunks else rest
            put = slice(c * LANE, c * LANE + size)
            hi, lo = halves(rows_e[:, at].T[0:size, :])
            sgt_e[put, 0:ke] = hi
            sgt_e[put, ke : 2 * ke] = lo
            hi, lo = halves(rows_r[:, at].T[0:size, :])
            sgt_r[put, 0:kr] = hi
            sgt_r[put, kr : 2 * kr] = lo

    def add_group(grp, first):
        gather_blocks(grp)
        part_e = mm(sgt_e[:, 0:ke], oh_e[...]) + mm(sgt_e[:, ke : 2 * ke], oh_e[...])
        part_r = mm(sgt_r[:, 0:kr], oh_r[...]) + mm(sgt_r[:, kr : 2 * kr], oh_r[...])
        if first:
            ge_ref[...] = part_e
            gr_ref[...] = part_r[:, 0:nr]
        else:
            ge_ref[...] += part_e
            gr_ref[...] += part_r[:, 0:nr]

    one_hots(g)
    add_group(g, True)
    for idx in range(max(len(sequence) - lag, 0), len(sequence)):
        hand_over_all(idx)
    for k in range(1, ng):
        idg_arrival(k).wait_recv()
    one_hots(mate)
    for k in sequence:
        arrived(mate, shard_from(k))
    add_group(mate, False)
    for dy in range(1, ny):
        one_hots(group_down(dy))
        add_group(group_down(dy), False)
        other = lax.rem(mate + ng - 2 * dy, ng)
        one_hots(other)
        for k in sequence:
            arrived(other, shard_from(k))
        add_group(other, False)

    def stat(i, total):
        for r in range(ns):
            total += gbuf[i, r, chunks * cap : chunks * cap + 8, :]
        return total

    stat_ref[...] = lax.fori_loop(0, ng, stat, jnp.zeros((8, LANE), F32))

    for k in order:
        ids_copy(k).wait_send()
        grad_copy(k).wait_send()
    for k in range(1, ng):
        idg_copy(k).wait_send()
    for k in sequence:
        src = shard_from(k)
        for copy in forward(src):
            copy.wait_send()
        for dy in range(1, ny):
            hand_over(dy, src).wait_send()


def adamw_kernel(at_pairs, stat_ref, *refs):
    factor = 1.0 / stat_ref[0:1, at_pairs : at_pairs + 1]
    fix_one = 1.0 - BETA_ONE**STEP
    fix_two = 1.0 - BETA_TWO**STEP
    for i in range(2):
        g_ref, w_ref, one_ref, two_ref = refs[4 * i : 4 * i + 4]
        w_out, one_out, two_out, low_out = refs[8 + 4 * i : 12 + 4 * i]
        gradient = g_ref[...] * factor
        weight = w_ref[...]
        one = BETA_ONE * one_ref[...] + (1.0 - BETA_ONE) * gradient
        two = BETA_TWO * two_ref[...] + (1.0 - BETA_TWO) * gradient * gradient
        direction = one / fix_one / (jnp.sqrt(two / fix_two) + EPS_ADAM)
        new = weight - RATE * (direction + DECAY * weight)
        w_out[...] = new
        one_out[...] = one
        two_out[...] = two
        low_out[...] = new.astype(BF16)


def per_device(
    ns,
    ng,
    entity_rows,
    entity_first,
    entity_second,
    relation_rows,
    relation_first,
    relation_second,
    requests,
    head_slots,
    relation_slots,
    tail_slots,
    neg_offsets,
    valid_counts,
):
    ne, d = entity_rows.shape
    nr = relation_rows.shape[0]
    cap = requests.shape[2]
    cap_r = cap - CAP_E
    edges, neg = neg_offsets.shape
    segs = edges // SEG
    ke, kr = ns * CAP_E, ns * cap_r
    chunks = d // LANE
    rest = d - chunks * LANE
    dp = (chunks + 1) * LANE
    nrp = up(nr, LANE)
    ny = ng // 2
    block = (LANE, LANE)
    any_space = pl.BlockSpec(memory_space=pl.ANY)
    vmem = pl.BlockSpec(memory_space=pltpu.VMEM)
    smem = pl.BlockSpec(memory_space=pltpu.SMEM)
    dma = pltpu.SemaphoreType.DMA
    ge, gr, stat = pl.pallas_call(
        functools.partial(exchange_kernel, ns, ng, (d, ne, nr, cap, edges, neg)),
        out_shape=(
            jax.ShapeDtypeStruct((d, ne), F32),
            jax.ShapeDtypeStruct((d, nr), F32),
            jax.ShapeDtypeStruct((8, LANE), F32),
        ),
        in_specs=[smem] + [any_space] * 7,
        out_specs=(vmem, vmem, vmem),
        scratch_shapes=[
            pltpu.VMEM((d, ne), F32),
            pltpu.VMEM((d, nr), F32),
            pltpu.VMEM((ns, cap), I32),
            pltpu.VMEM((3, segs, SEG), I32),
            pltpu.VMEM((neg, edges), I32),
            pltpu.VMEM((dp, ne), BF16),
            pltpu.VMEM((dp, ne), BF16),
            pltpu.VMEM((dp, nrp), BF16),
            pltpu.VMEM((dp, nrp), BF16),
            pltpu.VMEM((ns, ns, cap), I32),
            pltpu.VMEM((ng, ns, cap), I32),
            pltpu.VMEM((ns, *block), F32),
            pltpu.VMEM((ns, *block), F32),
            pltpu.VMEM((ke, dp), F32),
            pltpu.VMEM((kr, dp), F32),
            pltpu.VMEM((ke, ne), BF16),
            pltpu.VMEM((kr, nrp), BF16),
            pltpu.VMEM((edges, ke), BF16),
            pltpu.VMEM((edges, ke), BF16),
            pltpu.VMEM((edges, 2 * kr), BF16),
            pltpu.VMEM((ke, 2 * edges), BF16),
            pltpu.VMEM((kr, edges), BF16),
            pltpu.VMEM((segs, SEG, SEG), F32),
            pltpu.VMEM((ke, dp), BF16),
            pltpu.VMEM((ke, dp), BF16),
            pltpu.VMEM((2 * kr, dp), BF16),
            pltpu.VMEM((2 * edges, dp), BF16),
            pltpu.VMEM((2 * edges, dp), BF16),
            pltpu.VMEM((ng, ns, *block), F32),
            pltpu.VMEM((d, 2 * ke), BF16),
            pltpu.VMEM((d, 2 * kr), BF16),
            dma((7,)),
            dma((ns,)),
            dma((ns,)),
            dma((ng,)),
            dma((ng,)),
            dma((ns,)),
            dma((ns,)),
            dma((ns,)),
            dma((ng, ns)),
            dma((ny, ns)),
            dma((max(ny - 1, 1), ns)),
        ],
        compiler_params=pltpu.CompilerParams(
            collective_id=0, has_side_effects=True, vmem_limit_bytes=60 * 1024 * 1024
        ),
    )(
        valid_counts,
        entity_rows.T,
        relation_rows.T,
        requests[0],
        head_slots.reshape(segs, SEG),
        relation_slots.reshape(segs, SEG),
        tail_slots.reshape(segs, SEG),
        neg_offsets.T,
    )
    steps = d // 80
    at_loss = LANE // rest * rest - 2

    def rows(n):
        return pl.BlockSpec((d // steps, n), lambda i: (i, 0))

    outs = pl.pallas_call(
        functools.partial(adamw_kernel, at_loss + 1),
        grid=(steps,),
        out_shape=[jax.ShapeDtypeStruct((d, n), t) for n in (ne, nr) for t in (F32, F32, F32, BF16)],
        in_specs=[pl.BlockSpec((8, LANE), lambda i: (0, 0))] + [rows(ne)] * 4 + [rows(nr)] * 4,
        out_specs=[rows(ne)] * 4 + [rows(nr)] * 4,
        compiler_params=pltpu.CompilerParams(vmem_limit_bytes=32 * 1024 * 1024),
    )(
        stat,
        ge,
        entity_rows.T,
        entity_first.T,
        entity_second.T,
        gr,
        relation_rows.T,
        relation_first.T,
        relation_second.T,
    )
    e_new, e_one, e_two, e_low, r_new, r_one, r_two, r_low = (x.T for x in outs)
    return (
        e_new,
        e_one,
        e_two,
        r_new,
        r_one,
        r_two,
        e_low,
        r_low,
        stat[0, at_loss : at_loss + 1],
        stat[0, at_loss + 1 : at_loss + 2],
    )


def solution(mesh):
    rows = P("shard", None)
    both = ("grp", "shard")
    return jax.shard_map(
        functools.partial(per_device, mesh.shape["shard"], mesh.shape["grp"]),
        mesh=mesh,
        in_specs=(
            rows,
            rows,
            rows,
            rows,
            rows,
            rows,
            P(both, None, None),
            P(both),
            P(both),
            P(both),
            P(both, None),
            P(both),
        ),
        out_specs=(rows,) * 8 + (P(), P()),
        check_vma=False,
    )
```

```python
import functools
import math

import jax
import jax.numpy as jnp
from jax import lax
from jax.experimental import pallas as pl
from jax.experimental.pallas import tpu as pltpu
from jax.sharding import PartitionSpec as P

CAP_E = 32
SEG = 128
STEP = 10
LANE = 128

MARGIN = 0.1
EPS_DIST = 1e-06
BETA_ONE = 0.9
BETA_TWO = 0.999
RATE = 0.5
DECAY = 0.01
EPS_ADAM = 1e-08

F32 = jnp.float32
BF16 = jnp.bfloat16
I32 = jnp.int32


def mm(a, b):
    return lax.dot_general(a, b, (((1,), (0,)), ((), ())), preferred_element_type=F32)


def mm_nt(a, b):
    return lax.dot_general(a, b, (((1,), (1,)), ((), ())), preferred_element_type=F32)


def halves(x):
    hi = x.astype(BF16)
    return hi, (x - hi.astype(F32)).astype(BF16)


def up(n, m):
    return (n + m - 1) // m * m


def iota(shape, axis):
    return lax.broadcasted_iota(I32, shape, axis)


def padded(ref):
    *lead, rows, cols = ref.shape
    size = jnp.dtype(ref.dtype).itemsize
    return math.prod(lead) * up(rows, 32 // size) * up(cols, LANE) * size


def exchange_kernel(
    ns,
    ng,
    dims,
    valid_ref,
    ent_hbm,
    one_e_hbm,
    two_e_hbm,
    rel_hbm,
    one_r_hbm,
    two_r_hbm,
    req_hbm,
    head_hbm,
    rslot_hbm,
    tail_hbm,
    neg_hbm,
    ge_ref,
    gr_ref,
    stat_ref,
    ent_v,
    one_e_v,
    two_e_v,
    rel_v,
    one_r_v,
    two_r_v,
    req_v,
    slots_v,
    neg_v,
    eth,
    etl,
    rth,
    rtl,
    ids_all,
    idg,
    send_buf,
    recv_buf,
    rows_e,
    rows_r,
    oh_e,
    oh_r,
    hot_h,
    hot_t,
    hot_r,
    hott,
    hott_r,
    wt,
    eh,
    el,
    rr,
    gg_h,
    gg_l,
    gbuf,
    sgt_e,
    sgt_r,
    local_sem,
    ids_send,
    ids_recv,
    idg_send,
    idg_recv,
    f_send,
    f_recv,
    g_send,
    g_recv,
    core_send,
    y_send,
):
    d, ne, nr, cap, edges, neg = dims
    cap_r = cap - CAP_E
    ke, kr = ns * CAP_E, ns * cap_r
    chunks = d // LANE
    rest = d - chunks * LANE
    dp = (chunks + 1) * LANE
    nrp = up(nr, LANE)
    segs = edges // SEG
    copies = LANE // rest
    subs = cap // 8
    ny = ng // 2

    g = lax.axis_index("grp")
    s = lax.axis_index("shard")
    mate = g + 1 - 2 * lax.rem(g, 2)
    near = list(range(1, ns))
    order = near[ns // 2 - 1 :] + near[: ns // 2 - 1]

    def shard_at(k):
        partner, bit = s, 1
        while bit < ns:
            if k & bit:
                partner = partner + bit * (1 - 2 * lax.rem(s // bit, 2))
            bit *= 2
        return partner

    shard_from = shard_at

    barrier = pltpu.get_barrier_semaphore()
    for k in range(1, ns):
        pl.semaphore_signal(barrier, inc=1, device_id={"shard": shard_at(k)})
    for k in range(1, ng):
        pl.semaphore_signal(barrier, inc=1, device_id={"grp": lax.rem(g + k, ng)})

    local = [
        pltpu.make_async_copy(src, dst, local_sem.at[i])
        for i, (src, dst) in enumerate(
            [
                (req_hbm, req_v),
                (ent_hbm, ent_v),
                (rel_hbm, rel_v),
                (head_hbm, slots_v.at[0]),
                (rslot_hbm, slots_v.at[1]),
                (tail_hbm, slots_v.at[2]),
                (neg_hbm, neg_v),
                (one_e_hbm, one_e_v),
                (two_e_hbm, two_e_v),
                (one_r_hbm, one_r_v),
                (two_r_hbm, two_r_v),
            ]
        )
    ]
    for copy in local:
        copy.start()
    local[0].wait()
    pl.semaphore_wait(barrier, ns - 1 + ng - 1)

    def ids_copy(k):
        return pltpu.make_async_remote_copy(
            src_ref=req_v,
            dst_ref=ids_all.at[s],
            send_sem=ids_send.at[k],
            recv_sem=ids_recv.at[s],
            device_id={"shard": shard_at(k)},
        )

    def ids_arrival(k):
        return pltpu.make_async_remote_copy(
            src_ref=req_v,
            dst_ref=ids_all.at[shard_from(k)],
            send_sem=ids_send.at[k],
            recv_sem=ids_recv.at[shard_from(k)],
            device_id={"shard": shard_from(k)},
        )

    for k in order:
        ids_copy(k).start()
    ids_all[s] = req_v[...]

    local[1].wait()
    local[2].wait()

    def split_rows(i, _):
        at = pl.ds(pl.multiple_of(i * 16, 16), 16)
        hi, lo = halves(ent_v[at, :])
        eth[at, :] = hi
        etl[at, :] = lo
        hi, lo = halves(rel_v[at, :])
        rth[at, 0:nr] = hi
        rtl[at, 0:nr] = lo
        return 0

    if nrp > nr:
        rth[:, nr:nrp] = jnp.zeros((dp, nrp - nr), BF16)
        rtl[:, nr:nrp] = jnp.zeros((dp, nrp - nr), BF16)
    lax.fori_loop(0, d // 16, split_rows, 0)
    for table in (eth, etl, rth, rtl):
        tail_rows = table[chunks * LANE : d, :]
        for c in range(1, copies):
            table[chunks * LANE + c * rest : chunks * LANE + (c + 1) * rest, :] = tail_rows

    for k in order:
        ids_arrival(k).wait_recv()
    for r in range(ns):
        idg[g, r : r + 1, :] = ids_all[r, pl.ds(s, 1), :]

    def idg_copy(k):
        return pltpu.make_async_remote_copy(
            src_ref=idg.at[g],
            dst_ref=idg.at[g],
            send_sem=idg_send.at[k],
            recv_sem=idg_recv.at[g],
            device_id={"grp": lax.rem(g + k, ng)},
        )

    def idg_arrival(k):
        other = lax.rem(g + ng - k, ng)
        return pltpu.make_async_remote_copy(
            src_ref=idg.at[other],
            dst_ref=idg.at[other],
            send_sem=idg_send.at[k],
            recv_sem=idg_recv.at[other],
            device_id={"grp": other},
        )

    def one_hots(grp):
        wide = jnp.concatenate([idg[grp].astype(F32), jnp.zeros((ns, LANE - cap), F32)], axis=1)
        columns = jnp.concatenate([wide] + [jnp.zeros((LANE - ns, LANE), F32)], axis=0).T
        lanes_e = iota((CAP_E, ne), 1).astype(F32)
        lanes_r = iota((cap_r, nrp), 1).astype(F32) + float(ne)
        pieces = []
        for r in range(ns):
            column = columns[:, r : r + 1]
            hit = jnp.where(column[0:CAP_E] == lanes_e, 1.0, 0.0).astype(BF16)
            oh_e[r * CAP_E : (r + 1) * CAP_E, :] = hit
            pieces.append(jnp.where(column[CAP_E:cap] == lanes_r, 1.0, 0.0))
        for r in range(0, ns, 2):
            oh_r[r * cap_r : (r + 2) * cap_r, :] = jnp.concatenate(pieces[r : r + 2], axis=0).astype(BF16)

    one_hots(g)
    rows_e[...] = mm_nt(oh_e[...], eth[...]) + mm_nt(oh_e[...], etl[...])
    rows_r[...] = mm_nt(oh_r[...], rth[...]) + mm_nt(oh_r[...], rtl[...])

    lane8 = iota((8, LANE), 1)

    def pack(r, roll, extra):
        for c in range(chunks):
            at = slice(c * LANE, (c + 1) * LANE)
            send_buf[r, c * cap : c * cap + CAP_E, :] = rows_e[r * CAP_E : (r + 1) * CAP_E, at]
            send_buf[r, c * cap + CAP_E : (c + 1) * cap, :] = rows_r[r * cap_r : (r + 1) * cap_r, at]
        last = slice(chunks * LANE, dp)
        out = extra
        for j in range(subs):
            if j * 8 < CAP_E:
                piece = rows_e[r * CAP_E + j * 8 : r * CAP_E + j * 8 + 8, last]
            else:
                piece = rows_r[r * cap_r + j * 8 - CAP_E : r * cap_r + j * 8 - CAP_E + 8, last]
            if roll and j:
                piece = pltpu.roll(piece, j * rest, 1)
            out = jnp.where((lane8 >= j * rest) & (lane8 < (j + 1) * rest), piece, out)
        send_buf[r, chunks * cap : chunks * cap + 8, :] = out

    def last_columns(tile):
        pieces = []
        for j in range(subs):
            piece = pltpu.roll(tile, LANE - j * rest, 1) if j else tile
            pieces.append(jnp.where(lane8 < rest, piece, 0.0))
        return jnp.concatenate(pieces[: CAP_E // 8], axis=0), jnp.concatenate(pieces[CAP_E // 8 :], axis=0)

    def fetch_copy(k):
        peer = shard_at(k)
        return pltpu.make_async_remote_copy(
            src_ref=send_buf.at[peer],
            dst_ref=recv_buf.at[s],
            send_sem=f_send.at[k],
            recv_sem=f_recv.at[s],
            device_id={"shard": peer},
        )

    def fetch_arrival(k):
        peer = shard_from(k)
        return pltpu.make_async_remote_copy(
            src_ref=send_buf.at[peer],
            dst_ref=recv_buf.at[peer],
            send_sem=f_send.at[k],
            recv_sem=f_recv.at[peer],
            device_id={"shard": peer},
        )

    for r in range(ns):
        pack(r, False, jnp.zeros((8, LANE), F32))
    for k in order:
        fetch_copy(k).start()
    recv_buf[s] = send_buf[s]
    for k in range(1, ng):
        idg_copy(k).start()

    for copy in local[3:7]:
        copy.wait()
    slots = slots_v[...]
    owner = lax.shift_right_logical(slots * ((1 << 16) // cap + 1), 16)
    within = slots - owner * cap
    head_k = owner[0] * CAP_E + within[0]
    rel_k = owner[1] * cap_r + within[1] - CAP_E
    tail_k = owner[2] * CAP_E + within[2]
    for i in range(segs):
        at = slice(i * SEG, (i + 1) * SEG)
        head_row, rel_row, tail_row = (v[i : i + 1, :] for v in (head_k, rel_k, tail_k))
        hott[:, at] = jnp.where(iota((ke, SEG), 0) == head_row, 1.0, 0.0).astype(BF16)
        hott[:, edges + i * SEG : edges + (i + 1) * SEG] = jnp.where(
            iota((ke, SEG), 0) == tail_row, 1.0, 0.0
        ).astype(BF16)
        hott_r[:, at] = jnp.where(iota((kr, SEG), 0) == rel_row, 1.0, 0.0).astype(BF16)
        head_col, rel_col, tail_col = (
            jnp.broadcast_to(v.astype(F32), (SEG, SEG)).T[:, 0:1] for v in (head_row, rel_row, tail_row)
        )
        lanes_e = iota((SEG, ke), 1).astype(F32)
        lanes_r = iota((SEG, kr), 1).astype(F32)
        hot_h[at, :] = jnp.where(lanes_e == head_col, 1.0, 0.0).astype(BF16)
        hot_t[at, :] = jnp.where(lanes_e == tail_col, 1.0, 0.0).astype(BF16)
        hit = jnp.where(lanes_r == rel_col, 1.0, 0.0)
        hot_r[at, :] = jnp.concatenate([hit, hit], axis=1).astype(BF16)

    valid = valid_ref[0]
    sub = iota((SEG, SEG), 0)
    lane = iota((SEG, SEG), 1)

    def count(i, total):
        start = pl.multiple_of(i * SEG, SEG)
        hits = jnp.zeros((SEG, SEG), F32)
        for k in range(neg):
            hits += jnp.where(neg_v[k : k + 1, pl.ds(start, SEG)] == sub, 1.0, 0.0)
        keep = (lane + start < valid) & (sub + start < valid) & (sub != lane)
        hits = jnp.where(keep, hits, 0.0)
        wt[i] = hits
        return total + hits

    pairs = jnp.sum(lax.fori_loop(0, segs, count, jnp.zeros((SEG, SEG), F32)))

    recv = [(s, None)] + [(shard_from(k), k) for k in order]
    for src, k in recv:
        if k is not None:
            fetch_arrival(k).wait_recv()
    for p in range(ns):
        ends_e, ends_r = last_columns(recv_buf[p, chunks * cap : chunks * cap + 8, :])
        e = jnp.concatenate(
            [recv_buf[p, c * cap : c * cap + CAP_E, :] for c in range(chunks)] + [ends_e], axis=1
        )
        r = jnp.concatenate(
            [recv_buf[p, c * cap + CAP_E : (c + 1) * cap, :] for c in range(chunks)] + [ends_r], axis=1
        )
        at = slice(p * CAP_E, (p + 1) * CAP_E)
        eh[at, :], el[at, :] = halves(e)
        rows_r[p * cap_r : (p + 1) * cap_r, :] = r
    hi, lo = halves(rows_r[...])
    rr[0:kr, :] = hi
    rr[kr : 2 * kr, :] = lo

    def lane_fold(x):
        out = x[:, 0:LANE]
        for c in range(1, dp // LANE):
            out += x[:, c * LANE : (c + 1) * LANE]
        return out

    def edge_step(i, loss):
        at = pl.ds(pl.multiple_of(i * SEG, SEG), SEG)
        at_t = pl.ds(pl.multiple_of(edges + i * SEG, SEG), SEG)
        a = mm(hot_h[at, :], eh[...]) + mm(hot_h[at, :], el[...]) + mm(hot_r[at, :], rr[...])
        t = mm(hot_t[at, :], eh[...]) + mm(hot_t[at, :], el[...])
        ah, al = halves(a)
        th, tl = halves(t)
        aa = jnp.concatenate([ah, al], axis=0)
        tt = jnp.concatenate([th, tl], axis=0)
        offset = a - t
        dist_pos = jnp.sqrt(jnp.sum(lane_fold(offset * offset).T, axis=0, keepdims=True) + EPS_DIST)
        anchor_sq = jnp.sum(lane_fold(a * a).T, axis=0, keepdims=True)
        target_sq = jnp.sum(lane_fold(t * t), axis=1, keepdims=True)
        near = mm_nt(th, aa)
        far = mm_nt(tl, aa)
        gram = near[:, 0:SEG] + (near[:, SEG:] + far[:, 0:SEG] + far[:, SEG:])
        square = jnp.maximum(anchor_sq + target_sq - 2.0 * gram, 0.0) + EPS_DIST
        inv = lax.rsqrt(square)
        m = MARGIN + dist_pos - square * inv
        w = wt[i]
        small = jnp.exp(-jnp.abs(m))
        loss += w * (jnp.maximum(m, 0.0) + jnp.log1p(small))
        slope = w * (jnp.where(m >= 0.0, 1.0, small) / (1.0 + small))
        ratio = jnp.sum(slope, axis=0, keepdims=True) / dist_pos
        pt = slope * inv - jnp.where(sub == lane, ratio, 0.0)
        pa = pt.T
        row_t = jnp.sum(pt, axis=1, keepdims=True)
        row_a = jnp.sum(pa, axis=1, keepdims=True)
        pth, ptl = halves(pt)
        pah, pal = halves(pa)
        grad_t = mm(jnp.concatenate([pth, pth], axis=1), aa) + mm(ptl, ah) - row_t * t
        grad_a = mm(jnp.concatenate([pah, pah], axis=1), tt) + mm(pal, th) - row_a * a
        gg_h[at, :], gg_l[at, :] = halves(grad_a)
        gg_h[at_t, :], gg_l[at_t, :] = halves(grad_t)
        return loss

    loss = jnp.sum(lax.fori_loop(0, segs, edge_step, jnp.zeros((SEG, SEG), F32)))

    rows_e[...] = mm(hott[...], gg_h[...]) + mm(hott[...], gg_l[...])
    rows_r[...] = mm(hott_r[...], gg_h[0:edges, :]) + mm(hott_r[...], gg_l[0:edges, :])
    at_loss = copies * rest - 2
    extra = jnp.where(lane8 == at_loss, loss, jnp.where(lane8 == at_loss + 1, pairs, 0.0))

    def grad_copy(k):
        peer = shard_at(k)
        return pltpu.make_async_remote_copy(
            src_ref=send_buf.at[peer],
            dst_ref=gbuf.at[g, s],
            send_sem=g_send.at[k],
            recv_sem=g_recv.at[g, s],
            device_id={"shard": peer},
        )

    def block_copy(grp, src, to, send_sem):
        return pltpu.make_async_remote_copy(
            src_ref=gbuf.at[grp, src],
            dst_ref=gbuf.at[grp, src],
            send_sem=send_sem,
            recv_sem=g_recv.at[grp, src],
            device_id={"grp": to},
        )

    def arrived(grp, src):
        block_copy(grp, src, mate, core_send.at[0, 0]).wait_recv()

    for k in order:
        fetch_copy(k).wait_send()
    for r in range(ns):
        pack(r, True, extra)
    for k in near:
        grad_copy(k).start()
    gbuf[g, s] = send_buf[s]

    def group_up(dy):
        return lax.rem(g + 2 * dy, ng)

    def group_down(dy):
        return lax.rem(g + ng - 2 * dy, ng)

    def forward(src):
        out = [block_copy(g, src, mate, core_send.at[0, src])]
        for dy in range(1, ny):
            out.append(block_copy(g, src, group_up(dy), y_send.at[dy - 1, src]))
        return out

    def hand_over(dy, src):
        return block_copy(group_down(dy), src, mate, core_send.at[dy, src])

    sequence = [0] + near
    lag = 2

    def hand_over_all(idx):
        src = shard_from(sequence[idx])
        for dy in range(1, ny):
            arrived(group_down(dy), src)
            hand_over(dy, src).start()

    for idx, k in enumerate(sequence):
        src = shard_from(k)
        if k:
            arrived(g, src)
        for copy in forward(src):
            copy.start()
        if idx >= lag:
            hand_over_all(idx - lag)

    def gather_blocks(grp):
        for r in range(ns):
            ends_e, ends_r = last_columns(gbuf[grp, r, chunks * cap : chunks * cap + 8, :])
            rows_e[r * CAP_E : (r + 1) * CAP_E, chunks * LANE : dp] = ends_e
            rows_r[r * cap_r : (r + 1) * cap_r, chunks * LANE : dp] = ends_r
            for c in range(chunks):
                at = slice(c * LANE, (c + 1) * LANE)
                rows_e[r * CAP_E : (r + 1) * CAP_E, at] = gbuf[grp, r, c * cap : c * cap + CAP_E, :]
                rows_r[r * cap_r : (r + 1) * cap_r, at] = gbuf[grp, r, c * cap + CAP_E : (c + 1) * cap, :]
        for c in range(chunks + 1):
            at = slice(c * LANE, (c + 1) * LANE)
            size = LANE if c < chunks else rest
            put = slice(c * LANE, c * LANE + size)
            hi, lo = halves(rows_e[:, at].T[0:size, :])
            sgt_e[put, 0:ke] = hi
            sgt_e[put, ke : 2 * ke] = lo
            hi, lo = halves(rows_r[:, at].T[0:size, :])
            sgt_r[put, 0:kr] = hi
            sgt_r[put, kr : 2 * kr] = lo

    def add_group(grp, first):
        gather_blocks(grp)
        part_e = mm(sgt_e[:, 0:ke], oh_e[...]) + mm(sgt_e[:, ke : 2 * ke], oh_e[...])
        part_r = mm(sgt_r[:, 0:kr], oh_r[...]) + mm(sgt_r[:, kr : 2 * kr], oh_r[...])
        if first:
            ge_ref[...] = part_e
            gr_ref[...] = part_r[:, 0:nr]
        else:
            ge_ref[...] += part_e
            gr_ref[...] += part_r[:, 0:nr]

    one_hots(g)
    add_group(g, True)
    for idx in range(max(len(sequence) - lag, 0), len(sequence)):
        hand_over_all(idx)
    for k in range(1, ng):
        idg_arrival(k).wait_recv()
    one_hots(mate)
    for k in sequence:
        arrived(mate, shard_from(k))
    add_group(mate, False)
    for dy in range(1, ny):
        one_hots(group_down(dy))
        add_group(group_down(dy), False)
        other = lax.rem(mate + ng - 2 * dy, ng)
        one_hots(other)
        for k in sequence:
            arrived(other, shard_from(k))
        add_group(other, False)

    def stat(i, total):
        for r in range(ns):
            total += gbuf[i, r, chunks * cap : chunks * cap + 8, :]
        return total

    stat_ref[...] = lax.fori_loop(0, ng, stat, jnp.zeros((8, LANE), F32))

    for copy in local[7:]:
        copy.wait()
    for k in order:
        ids_copy(k).wait_send()
        grad_copy(k).wait_send()
    for k in range(1, ng):
        idg_copy(k).wait_send()
    for k in sequence:
        src = shard_from(k)
        for copy in forward(src):
            copy.wait_send()
        for dy in range(1, ny):
            hand_over(dy, src).wait_send()


def adamw_kernel(
    at_loss,
    strip,
    stat_ref,
    ge_ref,
    gr_ref,
    w_e,
    one_e,
    two_e,
    w_r,
    one_r,
    two_r,
    e_new,
    e_one,
    e_two,
    e_low,
    r_new,
    r_one,
    r_two,
    r_low,
    loss_ref,
    pairs_ref,
    *scratch,
):
    d = ge_ref.shape[0]
    sems = scratch[-1]
    total = stat_ref[0:1, :]
    loss_ref[0] = total[0, at_loss]
    pairs_ref[0] = total[0, at_loss + 1]
    factor = ((1.0 - BETA_ONE) / total)[0, at_loss + 1]
    square = (1.0 - BETA_TWO) / (1.0 - BETA_ONE) ** 2
    fix_two = 1.0 / (1.0 - BETA_TWO**STEP)
    rate = RATE / (1.0 - BETA_ONE**STEP)
    tables = (
        (ge_ref, w_e, one_e, two_e, (e_new, e_one, e_two, e_low), scratch[0:4]),
        (gr_ref, w_r, one_r, two_r, (r_new, r_one, r_two, r_low), scratch[4:8]),
    )

    def copies(i):
        at = pl.ds(pl.multiple_of(i * strip, strip), strip)
        out = []
        for n, (_, _, _, _, outs, bufs) in enumerate(tables):
            for m, (hbm, buf) in enumerate(zip(outs, bufs)):
                out.append(pltpu.make_async_copy(buf.at[at, :], hbm.at[at, :], sems.at[n * 4 + m, i]))
        return out

    def step(i, _):
        for g_ref, w_ref, one_ref, two_ref, _, bufs in tables:

            def rows(j, _):
                at = pl.ds(pl.multiple_of(i * strip + j * 16, 16), 16)
                gradient = g_ref[at, :] * factor
                weight = w_ref[at, :]
                one = BETA_ONE * one_ref[at, :] + gradient
                two = BETA_TWO * two_ref[at, :] + square * gradient * gradient
                scaled = two * fix_two
                root = scaled * lax.rsqrt(scaled) + EPS_ADAM
                new = weight * (1.0 - RATE * DECAY) - rate * one / root
                bufs[0][at, :] = new
                bufs[1][at, :] = one
                bufs[2][at, :] = two
                bufs[3][at, :] = new.astype(BF16)
                return 0

            lax.fori_loop(0, strip // 16, rows, 0, unroll=True)
        for copy in copies(i):
            copy.start()
        return 0

    steps = d // strip
    lax.fori_loop(0, steps, step, 0)
    for i in range(steps):
        for copy in copies(i):
            copy.wait()


def per_device(
    ns,
    ng,
    entity_rows,
    entity_first,
    entity_second,
    relation_rows,
    relation_first,
    relation_second,
    requests,
    head_slots,
    relation_slots,
    tail_slots,
    neg_offsets,
    valid_counts,
):
    ne, d = entity_rows.shape
    nr = relation_rows.shape[0]
    cap = requests.shape[2]
    cap_r = cap - CAP_E
    edges, neg = neg_offsets.shape
    segs = edges // SEG
    ke, kr = ns * CAP_E, ns * cap_r
    chunks = d // LANE
    rest = d - chunks * LANE
    dp = (chunks + 1) * LANE
    nrp = up(nr, LANE)
    ny = ng // 2
    block = (LANE, LANE)
    any_space = pl.BlockSpec(memory_space=pl.ANY)
    vmem = pl.BlockSpec(memory_space=pltpu.VMEM)
    smem = pl.BlockSpec(memory_space=pltpu.SMEM)
    dma = pltpu.SemaphoreType.DMA
    hbm = functools.partial(pltpu.with_memory_space_constraint, memory_space=pltpu.HBM)
    scratch = [
        pltpu.VMEM((ns, cap), I32),
        pltpu.VMEM((3, segs, SEG), I32),
        pltpu.VMEM((neg, edges), I32),
        pltpu.VMEM((dp, ne), BF16),
        pltpu.VMEM((dp, ne), BF16),
        pltpu.VMEM((dp, nrp), BF16),
        pltpu.VMEM((dp, nrp), BF16),
        pltpu.VMEM((ns, ns, cap), I32),
        pltpu.VMEM((ng, ns, cap), I32),
        pltpu.VMEM((ns, *block), F32),
        pltpu.VMEM((ns, *block), F32),
        pltpu.VMEM((ke, dp), F32),
        pltpu.VMEM((kr, dp), F32),
        pltpu.VMEM((ke, ne), BF16),
        pltpu.VMEM((kr, nrp), BF16),
        pltpu.VMEM((edges, ke), BF16),
        pltpu.VMEM((edges, ke), BF16),
        pltpu.VMEM((edges, 2 * kr), BF16),
        pltpu.VMEM((ke, 2 * edges), BF16),
        pltpu.VMEM((kr, edges), BF16),
        pltpu.VMEM((segs, SEG, SEG), F32),
        pltpu.VMEM((ke, dp), BF16),
        pltpu.VMEM((ke, dp), BF16),
        pltpu.VMEM((2 * kr, dp), BF16),
        pltpu.VMEM((2 * edges, dp), BF16),
        pltpu.VMEM((2 * edges, dp), BF16),
        pltpu.VMEM((ng, ns, *block), F32),
        pltpu.VMEM((d, 2 * ke), BF16),
        pltpu.VMEM((d, 2 * kr), BF16),
        dma((11,)),
        dma((ns,)),
        dma((ns,)),
        dma((ng,)),
        dma((ng,)),
        dma((ns,)),
        dma((ns,)),
        dma((ns,)),
        dma((ng, ns)),
        dma((ny, ns)),
        dma((max(ny - 1, 1), ns)),
    ]
    limit = sum(padded(x) for x in scratch[: scratch.index(dma((11,)))]) + (2 << 20)
    passed = pl.pallas_call(
        functools.partial(exchange_kernel, ns, ng, (d, ne, nr, cap, edges, neg)),
        out_shape=(
            pltpu.VMEM((d, ne), F32),
            pltpu.VMEM((d, nr), F32),
            pltpu.VMEM((8, LANE), F32),
        )
        + (pltpu.VMEM((d, ne), F32),) * 3
        + (pltpu.VMEM((d, nr), F32),) * 3,
        in_specs=[smem] + [any_space] * 11,
        out_specs=(vmem,) * 9,
        scratch_shapes=scratch,
        compiler_params=pltpu.CompilerParams(
            collective_id=0, has_side_effects=True, vmem_limit_bytes=limit
        ),
    )(
        valid_counts,
        hbm(entity_rows.T),
        hbm(entity_first.T),
        hbm(entity_second.T),
        hbm(relation_rows.T),
        hbm(relation_first.T),
        hbm(relation_second.T),
        hbm(requests[0]),
        hbm(head_slots.reshape(segs, SEG)),
        hbm(relation_slots.reshape(segs, SEG)),
        hbm(tail_slots.reshape(segs, SEG)),
        hbm(neg_offsets.T),
    )
    ge, gr, stat, *tables = passed
    at_loss = LANE // rest * rest - 2
    strip = 80
    shapes = [(jax.ShapeDtypeStruct((d, n), t)) for n in (ne, nr) for t in (F32, F32, F32, BF16)]
    one = jax.ShapeDtypeStruct((1,), F32)
    *outs, loss, pairs = pl.pallas_call(
        functools.partial(adamw_kernel, at_loss, strip),
        out_shape=shapes + [one, one],
        in_specs=[vmem] * 9,
        out_specs=[any_space] * 8 + [smem, smem],
        scratch_shapes=[pltpu.VMEM(x.shape, x.dtype) for x in shapes] + [dma((8, d // strip))],
        compiler_params=pltpu.CompilerParams(vmem_limit_bytes=32 * 1024 * 1024),
    )(stat, ge, gr, *tables)
    e_new, e_one, e_two, e_low, r_new, r_one, r_two, r_low = (x.T for x in outs)
    return (e_new, e_one, e_two, r_new, r_one, r_two, e_low, r_low, loss, pairs)


def solution(mesh):
    rows = P("shard", None)
    both = ("grp", "shard")
    return jax.shard_map(
        functools.partial(per_device, mesh.shape["shard"], mesh.shape["grp"]),
        mesh=mesh,
        in_specs=(
            rows,
            rows,
            rows,
            rows,
            rows,
            rows,
            P(both, None, None),
            P(both),
            P(both),
            P(both),
            P(both, None),
            P(both),
        ),
        out_specs=(rows,) * 8 + (P(), P()),
        check_vma=False,
    )
```

```python
import functools
import math

import jax
import jax.numpy as jnp
from jax import lax
from jax.experimental import pallas as pl
from jax.experimental.pallas import tpu as pltpu
from jax.sharding import PartitionSpec as P

CAP_E = 32
SEG = 128
STEP = 10
LANE = 128

MARGIN = 0.1
EPS_DIST = 1e-06
BETA_ONE = 0.9
BETA_TWO = 0.999
RATE = 0.5
DECAY = 0.01
EPS_ADAM = 1e-08

F32 = jnp.float32
BF16 = jnp.bfloat16
I32 = jnp.int32


def mm(a, b):
    return lax.dot_general(a, b, (((1,), (0,)), ((), ())), preferred_element_type=F32)


def mm_nt(a, b):
    return lax.dot_general(a, b, (((1,), (1,)), ((), ())), preferred_element_type=F32)


def halves(x):
    hi = x.astype(BF16)
    return hi, (x - hi.astype(F32)).astype(BF16)


def up(n, m):
    return (n + m - 1) // m * m


def iota(shape, axis):
    return lax.broadcasted_iota(I32, shape, axis)


def padded(ref):
    *lead, rows, cols = ref.shape
    size = jnp.dtype(ref.dtype).itemsize
    return math.prod(lead) * up(rows, 32 // size) * up(cols, LANE) * size


def exchange_kernel(
    ns,
    ng,
    dims,
    keep,
    valid_ref,
    req_hbm,
    head_hbm,
    rslot_hbm,
    tail_hbm,
    neg_hbm,
    ent_hbm,
    rel_hbm,
    *refs,
):
    rest_hbm, refs = refs[: 4 * keep], refs[4 * keep :]
    ge_ref, gr_ref, stat_ref, ent_v, rel_v, *refs = refs
    rest_v, refs = refs[: 4 * keep], refs[4 * keep :]
    exchange(ns, ng, dims, valid_ref, (req_hbm, head_hbm, rslot_hbm, tail_hbm, neg_hbm), (ent_hbm, rel_hbm, *rest_hbm), ge_ref, gr_ref, stat_ref, (ent_v, rel_v, *rest_v), *refs)


def exchange(
    ns,
    ng,
    dims,
    valid_ref,
    small_hbm,
    tables_hbm,
    ge_ref,
    gr_ref,
    stat_ref,
    tables,
    req_v,
    slots_v,
    neg_v,
    eth,
    etl,
    rth,
    rtl,
    ids_all,
    idg,
    send_buf,
    recv_buf,
    rows_e,
    rows_r,
    oh_e,
    oh_r,
    hot_h,
    hot_t,
    hot_r,
    hotx,
    hott,
    wt,
    eh,
    el,
    rr,
    targets,
    anchors,
    folds,
    squares,
    edge_rows,
    form,
    y_h,
    y_l,
    gbuf,
    sgt_e,
    sgt_r,
    local_sem,
    ids_send,
    ids_recv,
    idg_send,
    idg_recv,
    f_send,
    f_recv,
    g_send,
    g_recv,
    core_send,
    y_send,
):
    d, ne, nr, cap, edges, neg = dims
    ent_v, rel_v = tables[:2]
    req_hbm, head_hbm, rslot_hbm, tail_hbm, neg_hbm = small_hbm
    ent_hbm, rel_hbm = tables_hbm[:2]
    cap_r = cap - CAP_E
    ke, kr = ns * CAP_E, ns * cap_r
    chunks = d // LANE
    rest = d - chunks * LANE
    dp = (chunks + 1) * LANE
    nrp = up(nr, LANE)
    segs = edges // SEG
    copies = LANE // rest
    subs = cap // 8
    ny = ng // 2

    g = lax.axis_index("grp")
    s = lax.axis_index("shard")
    mate = g + 1 - 2 * lax.rem(g, 2)
    near = list(range(1, ns))
    order = near[ns // 2 - 1 :] + near[: ns // 2 - 1]

    def shard_at(k):
        partner, bit = s, 1
        while bit < ns:
            if k & bit:
                partner = partner + bit * (1 - 2 * lax.rem(s // bit, 2))
            bit *= 2
        return partner

    shard_from = shard_at

    barrier = pltpu.get_barrier_semaphore()
    for k in range(1, ns):
        pl.semaphore_signal(barrier, inc=1, device_id={"shard": shard_at(k)})
    for k in range(1, ng):
        pl.semaphore_signal(barrier, inc=1, device_id={"grp": lax.rem(g + k, ng)})

    local = [
        pltpu.make_async_copy(src, dst, local_sem.at[i])
        for i, (src, dst) in enumerate(
            [
                (req_hbm, req_v),
                (ent_hbm, ent_v),
                (rel_hbm, rel_v),
                (head_hbm, slots_v.at[0]),
                (rslot_hbm, slots_v.at[1]),
                (tail_hbm, slots_v.at[2]),
                (neg_hbm, neg_v),
                *zip(tables_hbm[2:], tables[2:]),
            ]
        )
    ]
    for copy in local:
        copy.start()
    local[0].wait()
    pl.semaphore_wait(barrier, ns - 1 + ng - 1)

    def ids_copy(k):
        return pltpu.make_async_remote_copy(
            src_ref=req_v,
            dst_ref=ids_all.at[s],
            send_sem=ids_send.at[k],
            recv_sem=ids_recv.at[s],
            device_id={"shard": shard_at(k)},
        )

    def ids_arrival(k):
        return pltpu.make_async_remote_copy(
            src_ref=req_v,
            dst_ref=ids_all.at[shard_from(k)],
            send_sem=ids_send.at[k],
            recv_sem=ids_recv.at[shard_from(k)],
            device_id={"shard": shard_from(k)},
        )

    for k in order:
        ids_copy(k).start()
    ids_all[s] = req_v[...]

    local[1].wait()
    local[2].wait()

    def split_rows(i, _):
        at = pl.ds(pl.multiple_of(i * 16, 16), 16)
        hi, lo = halves(ent_v[at, :])
        eth[at, :] = hi
        etl[at, :] = lo
        hi, lo = halves(rel_v[at, :])
        rth[at, 0:nr] = hi
        rtl[at, 0:nr] = lo
        return 0

    if nrp > nr:
        rth[:, nr:nrp] = jnp.zeros((dp, nrp - nr), BF16)
        rtl[:, nr:nrp] = jnp.zeros((dp, nrp - nr), BF16)
    lax.fori_loop(0, d // 16, split_rows, 0)
    for table in (eth, etl, rth, rtl):
        tail_rows = table[chunks * LANE : d, :]
        for c in range(1, copies):
            table[chunks * LANE + c * rest : chunks * LANE + (c + 1) * rest, :] = tail_rows

    for k in order:
        ids_arrival(k).wait_recv()
    for r in range(ns):
        idg[g, r : r + 1, :] = ids_all[r, pl.ds(s, 1), :]

    def idg_copy(k):
        return pltpu.make_async_remote_copy(
            src_ref=idg.at[g],
            dst_ref=idg.at[g],
            send_sem=idg_send.at[k],
            recv_sem=idg_recv.at[g],
            device_id={"grp": lax.rem(g + k, ng)},
        )

    def idg_arrival(k):
        other = lax.rem(g + ng - k, ng)
        return pltpu.make_async_remote_copy(
            src_ref=idg.at[other],
            dst_ref=idg.at[other],
            send_sem=idg_send.at[k],
            recv_sem=idg_recv.at[other],
            device_id={"grp": other},
        )

    def one_hots(grp):
        wide = jnp.concatenate([idg[grp].astype(F32), jnp.zeros((ns, LANE - cap), F32)], axis=1)
        columns = jnp.concatenate([wide] + [jnp.zeros((LANE - ns, LANE), F32)], axis=0).T
        lanes_e = iota((CAP_E, ne), 1).astype(F32)
        lanes_r = iota((cap_r, nrp), 1).astype(F32) + float(ne)
        pieces = []
        for r in range(ns):
            column = columns[:, r : r + 1]
            hit = jnp.where(column[0:CAP_E] == lanes_e, 1.0, 0.0).astype(BF16)
            oh_e[r * CAP_E : (r + 1) * CAP_E, :] = hit
            pieces.append(jnp.where(column[CAP_E:cap] == lanes_r, 1.0, 0.0))
        for r in range(0, ns, 2):
            oh_r[r * cap_r : (r + 2) * cap_r, :] = jnp.concatenate(pieces[r : r + 2], axis=0).astype(BF16)

    one_hots(g)
    rows_e[...] = mm_nt(oh_e[...], eth[...]) + mm_nt(oh_e[...], etl[...])
    rows_r[...] = mm_nt(oh_r[...], rth[...]) + mm_nt(oh_r[...], rtl[...])

    lane8 = iota((8, LANE), 1)

    def pack(r, roll, extra):
        for c in range(chunks):
            at = slice(c * LANE, (c + 1) * LANE)
            send_buf[r, c * cap : c * cap + CAP_E, :] = rows_e[r * CAP_E : (r + 1) * CAP_E, at]
            send_buf[r, c * cap + CAP_E : (c + 1) * cap, :] = rows_r[r * cap_r : (r + 1) * cap_r, at]
        last = slice(chunks * LANE, dp)
        out = extra
        for j in range(subs):
            if j * 8 < CAP_E:
                piece = rows_e[r * CAP_E + j * 8 : r * CAP_E + j * 8 + 8, last]
            else:
                piece = rows_r[r * cap_r + j * 8 - CAP_E : r * cap_r + j * 8 - CAP_E + 8, last]
            if roll and j:
                piece = pltpu.roll(piece, j * rest, 1)
            out = jnp.where((lane8 >= j * rest) & (lane8 < (j + 1) * rest), piece, out)
        send_buf[r, chunks * cap : chunks * cap + 8, :] = out

    def last_columns(tile):
        pieces = []
        for j in range(subs):
            piece = pltpu.roll(tile, LANE - j * rest, 1) if j else tile
            pieces.append(jnp.where(lane8 < rest, piece, 0.0))
        return jnp.concatenate(pieces[: CAP_E // 8], axis=0), jnp.concatenate(pieces[CAP_E // 8 :], axis=0)

    def fetch_copy(k):
        peer = shard_at(k)
        return pltpu.make_async_remote_copy(
            src_ref=send_buf.at[peer],
            dst_ref=recv_buf.at[s],
            send_sem=f_send.at[k],
            recv_sem=f_recv.at[s],
            device_id={"shard": peer},
        )

    def fetch_arrival(k):
        peer = shard_from(k)
        return pltpu.make_async_remote_copy(
            src_ref=send_buf.at[peer],
            dst_ref=recv_buf.at[peer],
            send_sem=f_send.at[k],
            recv_sem=f_recv.at[peer],
            device_id={"shard": peer},
        )

    for r in range(ns):
        pack(r, False, jnp.zeros((8, LANE), F32))
    for k in order:
        fetch_copy(k).start()
    recv_buf[s] = send_buf[s]
    for k in range(1, ng):
        idg_copy(k).start()

    for copy in local[3:7]:
        copy.wait()
    slots = slots_v[...]
    owner = lax.shift_right_logical(slots * ((1 << 16) // cap + 1), 16)
    within = slots - owner * cap
    head_k = owner[0] * CAP_E + within[0]
    rel_k = owner[1] * cap_r + within[1] - CAP_E
    tail_k = owner[2] * CAP_E + within[2]
    for i in range(segs):
        at = slice(i * SEG, (i + 1) * SEG)
        head_row, rel_row, tail_row = (v[i : i + 1, :] for v in (head_k, rel_k, tail_k))
        hotx[0:ke, at] = jnp.where(iota((ke, SEG), 0) == head_row, 1.0, 0.0).astype(BF16)
        hott[:, at] = jnp.where(iota((ke, SEG), 0) == tail_row, 1.0, 0.0).astype(BF16)
        hotx[ke:, at] = jnp.where(iota((kr, SEG), 0) == rel_row, 1.0, 0.0).astype(BF16)
        head_col, rel_col, tail_col = (
            jnp.broadcast_to(v.astype(F32), (SEG, SEG)).T[:, 0:1] for v in (head_row, rel_row, tail_row)
        )
        lanes_e = iota((SEG, ke), 1).astype(F32)
        lanes_r = iota((SEG, kr), 1).astype(F32)
        hot_h[at, :] = jnp.where(lanes_e == head_col, 1.0, 0.0).astype(BF16)
        hot_t[at, :] = jnp.where(lanes_e == tail_col, 1.0, 0.0).astype(BF16)
        hit = jnp.where(lanes_r == rel_col, 1.0, 0.0)
        hot_r[at, :] = jnp.concatenate([hit, hit], axis=1).astype(BF16)

    valid = valid_ref[0]
    sub = iota((SEG, SEG), 0)
    lane = iota((SEG, SEG), 1)

    def count(i, total):
        start = pl.multiple_of(i * SEG, SEG)
        hits = jnp.zeros((SEG, SEG), F32)
        for k in range(neg):
            hits += jnp.where(neg_v[k : k + 1, pl.ds(start, SEG)] == sub, 1.0, 0.0)
        keep = (lane + start < valid) & (sub + start < valid) & (sub != lane)
        hits = jnp.where(keep, hits, 0.0)
        wt[i] = hits
        return total + hits

    pairs = jnp.sum(lax.fori_loop(0, segs, count, jnp.zeros((SEG, SEG), F32)))

    recv = [(s, None)] + [(shard_from(k), k) for k in order]
    for src, k in recv:
        if k is not None:
            fetch_arrival(k).wait_recv()
    for p in range(ns):
        ends_e, ends_r = last_columns(recv_buf[p, chunks * cap : chunks * cap + 8, :])
        e = jnp.concatenate(
            [recv_buf[p, c * cap : c * cap + CAP_E, :] for c in range(chunks)] + [ends_e], axis=1
        )
        r = jnp.concatenate(
            [recv_buf[p, c * cap + CAP_E : (c + 1) * cap, :] for c in range(chunks)] + [ends_r], axis=1
        )
        at = slice(p * CAP_E, (p + 1) * CAP_E)
        eh[at, :], el[at, :] = halves(e)
        rows_r[p * cap_r : (p + 1) * cap_r, :] = r
    hi, lo = halves(rows_r[...])
    rr[0:kr, :] = hi
    rr[kr : 2 * kr, :] = lo

    def lane_fold(x):
        out = x[:, 0:LANE]
        for c in range(1, dp // LANE):
            out += x[:, c * LANE : (c + 1) * LANE]
        return out

    def seg(i):
        return slice(i * SEG, (i + 1) * SEG)

    def pair(i):
        return slice(2 * i * SEG, 2 * (i + 1) * SEG)

    for i in range(segs):
        hots = jnp.concatenate([hot_h[seg(i), :], hot_t[seg(i), :]], axis=0)
        both_h = mm(hots, eh[...])
        both_l = mm(hots, el[...])
        a = both_h[0:SEG] + both_l[0:SEG] + mm(hot_r[seg(i), :], rr[...])
        t = both_h[SEG:] + both_l[SEG:]
        targets[pair(i), :] = jnp.concatenate([both_h[SEG:].astype(BF16), both_l[SEG:].astype(BF16)], axis=0)
        anchors[pair(i), :] = jnp.concatenate(halves(a), axis=0)
        offset = a - t
        folds[0, i] = lane_fold(offset * offset)
        folds[1, i] = lane_fold(a * a)
        folds[2, i] = lane_fold(t * t)

    for i in range(segs):
        terms = mm_nt(targets[pair(i), :], anchors[pair(i), :])
        gram = terms[0:SEG, 0:SEG] + (terms[0:SEG, SEG:] + terms[SEG:, 0:SEG] + terms[SEG:, SEG:])
        square_pos = jnp.sum(folds[0, i].T, axis=0, keepdims=True)
        edge_rows[0:1, seg(i)] = jnp.sqrt(square_pos + EPS_DIST)
        anchor_sq = jnp.sum(folds[1, i].T, axis=0, keepdims=True)
        target_sq = jnp.sum(folds[2, i], axis=1, keepdims=True)
        squares[i] = anchor_sq + target_sq - 2.0 * gram

    loss = jnp.zeros((SEG, SEG), F32)
    for i in range(segs):
        square = jnp.maximum(squares[i], 0.0) + EPS_DIST
        dist_pos = edge_rows[0:1, seg(i)]
        inv = lax.rsqrt(square)
        m = MARGIN + dist_pos - square * inv
        w = wt[i]
        small = jnp.exp(-jnp.abs(m))
        loss += w * (jnp.maximum(m, 0.0) + jnp.log1p(small))
        slope = w * (jnp.where(m >= 0.0, 1.0, small) / (1.0 + small))
        ratio = jnp.sum(slope, axis=0, keepdims=True) / dist_pos
        pt = slope * inv - jnp.where(sub == lane, ratio, 0.0)
        pa = pt.T
        sum_a = jnp.sum(pt, axis=0, keepdims=True)
        edge_rows[1:2, seg(i)] = sum_a
        edge_rows[2:3, seg(i)] = jnp.sum(pa, axis=0, keepdims=True)
        own_h, own_l = halves(jnp.where(sub == lane, -sum_a, 0.0))
        pa_h, pa_l = halves(pa)
        form[pair(i), 0:SEG] = jnp.concatenate([pa_h, pa_l], axis=0)
        form[pair(i), SEG:] = jnp.concatenate([own_h, own_l], axis=0)
    loss = jnp.sum(loss)

    for i in range(segs):
        hots = jnp.concatenate([hot_t[seg(i), :], hot_h[seg(i), :]], axis=0)
        y = mm(form[pair(i), :], hots)
        y_h[seg(i), :], y_l[seg(i), :] = halves(y[0:SEG] + y[SEG:])
    crossed = mm(hotx[...], y_h[...]) + mm(hotx[...], y_l[...])
    form_re = crossed[ke:]
    own_e = jnp.zeros((ke, LANE), F32)
    own_r = jnp.zeros((kr, LANE), F32)
    for i in range(segs):
        sum_a = edge_rows[1:2, seg(i)]
        sum_t = edge_rows[2:3, seg(i)]
        own_e += hotx[0:ke, seg(i)].astype(F32) * sum_a - hott[:, seg(i)].astype(F32) * sum_t
        own_r -= hotx[ke:, seg(i)].astype(F32) * sum_a
    own_e = jnp.sum(own_e, axis=1, keepdims=True)
    own_r = jnp.sum(own_r, axis=1, keepdims=True)
    diagonal = iota((ke, ke), 0) == iota((ke, ke), 1)
    form_ee = crossed[0:ke] + crossed[0:ke].T + jnp.where(diagonal, own_e, 0.0)

    ee_h, ee_l = halves(form_ee)
    re_h, re_l = halves(form_re)
    er_h, er_l = halves(form_re.T)
    rows_e[...] = (
        mm(ee_h, eh[...])
        + (mm(ee_h, el[...]) + mm(ee_l, eh[...]))
        + (mm(jnp.concatenate([er_h, er_h], axis=1), rr[...]) + mm(er_l, rr[0:kr, :]))
    )
    rows_r[...] = (
        mm(re_h, eh[...])
        + (mm(re_h, el[...]) + mm(re_l, eh[...]))
        + own_r * (rr[0:kr, :].astype(F32) + rr[kr : 2 * kr, :].astype(F32))
    )
    at_loss = copies * rest - 2
    extra = jnp.where(lane8 == at_loss, loss, jnp.where(lane8 == at_loss + 1, pairs, 0.0))

    def grad_copy(k):
        peer = shard_at(k)
        return pltpu.make_async_remote_copy(
            src_ref=send_buf.at[peer],
            dst_ref=gbuf.at[g, s],
            send_sem=g_send.at[k],
            recv_sem=g_recv.at[g, s],
            device_id={"shard": peer},
        )

    def block_copy(grp, src, to, send_sem):
        return pltpu.make_async_remote_copy(
            src_ref=gbuf.at[grp, src],
            dst_ref=gbuf.at[grp, src],
            send_sem=send_sem,
            recv_sem=g_recv.at[grp, src],
            device_id={"grp": to},
        )

    def arrived(grp, src):
        block_copy(grp, src, mate, core_send.at[0, 0]).wait_recv()

    for k in order:
        fetch_copy(k).wait_send()
    for r in range(ns):
        pack(r, True, extra)
    for k in near:
        grad_copy(k).start()
    gbuf[g, s] = send_buf[s]

    def group_up(dy):
        return lax.rem(g + 2 * dy, ng)

    def group_down(dy):
        return lax.rem(g + ng - 2 * dy, ng)

    def forward(src):
        out = [block_copy(g, src, mate, core_send.at[0, src])]
        for dy in range(1, ny):
            out.append(block_copy(g, src, group_up(dy), y_send.at[dy - 1, src]))
        return out

    def hand_over(dy, src):
        return block_copy(group_down(dy), src, mate, core_send.at[dy, src])

    sequence = [0] + near
    lag = 2

    def hand_over_all(idx):
        src = shard_from(sequence[idx])
        for dy in range(1, ny):
            arrived(group_down(dy), src)
            hand_over(dy, src).start()

    for idx, k in enumerate(sequence):
        src = shard_from(k)
        if k:
            arrived(g, src)
        for copy in forward(src):
            copy.start()
        if idx >= lag:
            hand_over_all(idx - lag)

    def gather_blocks(grp):
        for r in range(ns):
            ends_e, ends_r = last_columns(gbuf[grp, r, chunks * cap : chunks * cap + 8, :])
            rows_e[r * CAP_E : (r + 1) * CAP_E, chunks * LANE : dp] = ends_e
            rows_r[r * cap_r : (r + 1) * cap_r, chunks * LANE : dp] = ends_r
            for c in range(chunks):
                at = slice(c * LANE, (c + 1) * LANE)
                rows_e[r * CAP_E : (r + 1) * CAP_E, at] = gbuf[grp, r, c * cap : c * cap + CAP_E, :]
                rows_r[r * cap_r : (r + 1) * cap_r, at] = gbuf[grp, r, c * cap + CAP_E : (c + 1) * cap, :]
        for c in range(chunks + 1):
            at = slice(c * LANE, (c + 1) * LANE)
            size = LANE if c < chunks else rest
            put = slice(c * LANE, c * LANE + size)
            hi, lo = halves(rows_e[:, at].T[0:size, :])
            sgt_e[put, 0:ke] = hi
            sgt_e[put, ke : 2 * ke] = lo
            hi, lo = halves(rows_r[:, at].T[0:size, :])
            sgt_r[put, 0:kr] = hi
            sgt_r[put, kr : 2 * kr] = lo

    def add_group(grp, first):
        gather_blocks(grp)
        part_e = mm(sgt_e[:, 0:ke], oh_e[...]) + mm(sgt_e[:, ke : 2 * ke], oh_e[...])
        part_r = mm(sgt_r[:, 0:kr], oh_r[...]) + mm(sgt_r[:, kr : 2 * kr], oh_r[...])
        if first:
            ge_ref[...] = part_e
            gr_ref[...] = part_r[:, 0:nr]
        else:
            ge_ref[...] += part_e
            gr_ref[...] += part_r[:, 0:nr]

    one_hots(g)
    add_group(g, True)
    for idx in range(max(len(sequence) - lag, 0), len(sequence)):
        hand_over_all(idx)
    for k in range(1, ng):
        idg_arrival(k).wait_recv()
    one_hots(mate)
    for k in sequence:
        arrived(mate, shard_from(k))
    add_group(mate, False)
    for dy in range(1, ny):
        one_hots(group_down(dy))
        add_group(group_down(dy), False)
        other = lax.rem(mate + ng - 2 * dy, ng)
        one_hots(other)
        for k in sequence:
            arrived(other, shard_from(k))
        add_group(other, False)

    def stat(i, total):
        for r in range(ns):
            total += gbuf[i, r, chunks * cap : chunks * cap + 8, :]
        return total

    stat_ref[...] = lax.fori_loop(0, ng, stat, jnp.zeros((8, LANE), F32))

    for copy in local[7:]:
        copy.wait()
    for k in order:
        ids_copy(k).wait_send()
        grad_copy(k).wait_send()
    for k in range(1, ng):
        idg_copy(k).wait_send()
    for k in sequence:
        src = shard_from(k)
        for copy in forward(src):
            copy.wait_send()
        for dy in range(1, ny):
            hand_over(dy, src).wait_send()


def adamw_kernel(
    at_loss,
    strip,
    stat_ref,
    ge_ref,
    gr_ref,
    w_e,
    one_e,
    two_e,
    w_r,
    one_r,
    two_r,
    e_new,
    e_one,
    e_two,
    e_low,
    r_new,
    r_one,
    r_two,
    r_low,
    loss_ref,
    pairs_ref,
    *scratch,
):
    d = ge_ref.shape[0]
    sems = scratch[-1]
    total = stat_ref[0:1, :]
    loss_ref[0] = total[0, at_loss]
    pairs_ref[0] = total[0, at_loss + 1]
    factor = ((1.0 - BETA_ONE) / total)[0, at_loss + 1]
    square = (1.0 - BETA_TWO) / (1.0 - BETA_ONE) ** 2
    fix_two = 1.0 / (1.0 - BETA_TWO**STEP)
    rate = RATE / (1.0 - BETA_ONE**STEP)
    tables = (
        (ge_ref, w_e, one_e, two_e, (e_new, e_one, e_two, e_low), scratch[0:4]),
        (gr_ref, w_r, one_r, two_r, (r_new, r_one, r_two, r_low), scratch[4:8]),
    )

    def copies(i):
        at = pl.ds(pl.multiple_of(i * strip, strip), strip)
        out = []
        for n, (_, _, _, _, outs, bufs) in enumerate(tables):
            for m, (hbm, buf) in enumerate(zip(outs, bufs)):
                out.append(pltpu.make_async_copy(buf.at[at, :], hbm.at[at, :], sems.at[n * 4 + m, i]))
        return out

    def step(i, _):
        for g_ref, w_ref, one_ref, two_ref, _, bufs in tables:

            def rows(j, _):
                at = pl.ds(pl.multiple_of(i * strip + j * 16, 16), 16)
                gradient = g_ref[at, :] * factor
                weight = w_ref[at, :]
                one = BETA_ONE * one_ref[at, :] + gradient
                two = BETA_TWO * two_ref[at, :] + square * gradient * gradient
                scaled = two * fix_two
                root = scaled * lax.rsqrt(scaled) + EPS_ADAM
                new = weight * (1.0 - RATE * DECAY) - rate * one / root
                bufs[0][at, :] = new
                bufs[1][at, :] = one
                bufs[2][at, :] = two
                bufs[3][at, :] = new.astype(BF16)
                return 0

            lax.fori_loop(0, strip // 16, rows, 0, unroll=True)
        for copy in copies(i):
            copy.start()
        return 0

    steps = d // strip
    lax.fori_loop(0, steps, step, 0)
    for i in range(steps):
        for copy in copies(i):
            copy.wait()


def per_device(
    ns,
    ng,
    entity_rows,
    entity_first,
    entity_second,
    relation_rows,
    relation_first,
    relation_second,
    requests,
    head_slots,
    relation_slots,
    tail_slots,
    neg_offsets,
    valid_counts,
):
    ne, d = entity_rows.shape
    nr = relation_rows.shape[0]
    cap = requests.shape[2]
    cap_r = cap - CAP_E
    edges, neg = neg_offsets.shape
    segs = edges // SEG
    ke, kr = ns * CAP_E, ns * cap_r
    chunks = d // LANE
    rest = d - chunks * LANE
    dp = (chunks + 1) * LANE
    nrp = up(nr, LANE)
    ny = ng // 2
    block = (LANE, LANE)
    any_space = pl.BlockSpec(memory_space=pl.ANY)
    vmem = pl.BlockSpec(memory_space=pltpu.VMEM)
    smem = pl.BlockSpec(memory_space=pltpu.SMEM)
    dma = pltpu.SemaphoreType.DMA
    hbm = functools.partial(pltpu.with_memory_space_constraint, memory_space=pltpu.HBM)
    scratch = [
        pltpu.VMEM((ns, cap), I32),
        pltpu.VMEM((3, segs, SEG), I32),
        pltpu.VMEM((neg, edges), I32),
        pltpu.VMEM((dp, ne), BF16),
        pltpu.VMEM((dp, ne), BF16),
        pltpu.VMEM((dp, nrp), BF16),
        pltpu.VMEM((dp, nrp), BF16),
        pltpu.VMEM((ns, ns, cap), I32),
        pltpu.VMEM((ng, ns, cap), I32),
        pltpu.VMEM((ns, *block), F32),
        pltpu.VMEM((ns, *block), F32),
        pltpu.VMEM((ke, dp), F32),
        pltpu.VMEM((kr, dp), F32),
        pltpu.VMEM((ke, ne), BF16),
        pltpu.VMEM((kr, nrp), BF16),
        pltpu.VMEM((edges, ke), BF16),
        pltpu.VMEM((edges, ke), BF16),
        pltpu.VMEM((edges, 2 * kr), BF16),
        pltpu.VMEM((ke + kr, edges), BF16),
        pltpu.VMEM((ke, edges), BF16),
        pltpu.VMEM((segs, SEG, SEG), F32),
        pltpu.VMEM((ke, dp), BF16),
        pltpu.VMEM((ke, dp), BF16),
        pltpu.VMEM((2 * kr, dp), BF16),
        pltpu.VMEM((2 * edges, dp), BF16),
        pltpu.VMEM((2 * edges, dp), BF16),
        pltpu.VMEM((3, segs, SEG, SEG), F32),
        pltpu.VMEM((segs, SEG, SEG), F32),
        pltpu.VMEM((8, edges), F32),
        pltpu.VMEM((2 * edges, 2 * SEG), BF16),
        pltpu.VMEM((edges, ke), BF16),
        pltpu.VMEM((edges, ke), BF16),
        pltpu.VMEM((ng, ns, *block), F32),
        pltpu.VMEM((d, 2 * ke), BF16),
        pltpu.VMEM((d, 2 * kr), BF16),
        dma((11,)),
        dma((ns,)),
        dma((ns,)),
        dma((ng,)),
        dma((ng,)),
        dma((ns,)),
        dma((ns,)),
        dma((ns,)),
        dma((ng, ns)),
        dma((ny, ns)),
        dma((max(ny - 1, 1), ns)),
    ]
    small = [
        requests[0],
        head_slots.reshape(segs, SEG),
        relation_slots.reshape(segs, SEG),
        tail_slots.reshape(segs, SEG),
        neg_offsets.T,
    ]
    rows = [entity_rows.T, relation_rows.T]
    moments = [entity_first.T, entity_second.T, relation_first.T, relation_second.T]
    sums = [pltpu.VMEM((d, ne), F32), pltpu.VMEM((d, nr), F32), pltpu.VMEM((8, LANE), F32)]
    held_rows = [pltpu.VMEM(x.shape, F32) for x in rows]
    held_moments = [pltpu.VMEM(x.shape, F32) for x in moments]
    need = sum(padded(x) for x in scratch[: scratch.index(dma((11,)))]) + (2 << 20)
    keep = need + sum(padded(x) for x in sums + held_rows + held_moments) < (62 << 20)
    if keep:
        outs, held = sums + held_rows + held_moments, []
    else:
        outs, held = sums, held_rows
        need += sum(padded(x) for x in held)
    operands = small + rows + (moments if keep else [])
    ge, gr, stat, *passed = pl.pallas_call(
        functools.partial(exchange_kernel, ns, ng, (d, ne, nr, cap, edges, neg), int(keep)),
        out_shape=outs,
        in_specs=[smem] + [any_space] * len(operands),
        out_specs=[vmem] * len(outs),
        scratch_shapes=held + scratch,
        compiler_params=pltpu.CompilerParams(
            collective_id=0, has_side_effects=True, vmem_limit_bytes=need
        ),
    )(valid_counts, *[hbm(x) for x in operands])
    if not keep:
        passed = rows + moments
    w_e, w_r, one_e, two_e, one_r, two_r = passed
    tables = (w_e, one_e, two_e, w_r, one_r, two_r)
    at_loss = LANE // rest * rest - 2
    strip = 80
    shapes = [(jax.ShapeDtypeStruct((d, n), t)) for n in (ne, nr) for t in (F32, F32, F32, BF16)]
    one = jax.ShapeDtypeStruct((1,), F32)
    *outs, loss, pairs = pl.pallas_call(
        functools.partial(adamw_kernel, at_loss, strip),
        out_shape=shapes + [one, one],
        in_specs=[vmem] * 9,
        out_specs=[any_space] * 8 + [smem, smem],
        scratch_shapes=[pltpu.VMEM(x.shape, x.dtype) for x in shapes] + [dma((8, d // strip))],
        compiler_params=pltpu.CompilerParams(vmem_limit_bytes=32 * 1024 * 1024),
    )(stat, ge, gr, *tables)
    e_new, e_one, e_two, e_low, r_new, r_one, r_two, r_low = (x.T for x in outs)
    return (e_new, e_one, e_two, r_new, r_one, r_two, e_low, r_low, loss, pairs)


def solution(mesh):
    rows = P("shard", None)
    both = ("grp", "shard")
    return jax.shard_map(
        functools.partial(per_device, mesh.shape["shard"], mesh.shape["grp"]),
        mesh=mesh,
        in_specs=(
            rows,
            rows,
            rows,
            rows,
            rows,
            rows,
            P(both, None, None),
            P(both),
            P(both),
            P(both),
            P(both, None),
            P(both),
        ),
        out_specs=(rows,) * 8 + (P(), P()),
        check_vma=False,
    )
```

```python
import functools
import math

import jax
import jax.numpy as jnp
from jax import lax
from jax.experimental import pallas as pl
from jax.experimental.pallas import tpu as pltpu
from jax.sharding import PartitionSpec as P

CAP_E = 32
SEG = 128
STEP = 10
LANE = 128

MARGIN = 0.1
EPS_DIST = 1e-06
BETA_ONE = 0.9
BETA_TWO = 0.999
RATE = 0.5
DECAY = 0.01
EPS_ADAM = 1e-08

F32 = jnp.float32
BF16 = jnp.bfloat16
I32 = jnp.int32


def mm(a, b):
    return lax.dot_general(a, b, (((1,), (0,)), ((), ())), preferred_element_type=F32)


def mm_nt(a, b):
    return lax.dot_general(a, b, (((1,), (1,)), ((), ())), preferred_element_type=F32)


def halves(x):
    hi = x.astype(BF16)
    return hi, (x - hi.astype(F32)).astype(BF16)


def up(n, m):
    return (n + m - 1) // m * m


def iota(shape, axis):
    return lax.broadcasted_iota(I32, shape, axis)


def padded(ref):
    *lead, rows, cols = ref.shape
    size = jnp.dtype(ref.dtype).itemsize
    return math.prod(lead) * up(rows, 32 // size) * up(cols, LANE) * size


def exchange_kernel(
    ns,
    ng,
    dims,
    keep,
    early,
    valid_ref,
    req_hbm,
    head_hbm,
    rslot_hbm,
    tail_hbm,
    neg_hbm,
    ent_hbm,
    rel_hbm,
    *refs,
):
    rest_hbm, refs = refs[: 4 * keep], refs[4 * keep :]
    ge_ref, gr_ref, stat_ref, ent_v, rel_v, *refs = refs
    rest_v, refs = refs[: 4 * keep], refs[4 * keep :]
    exchange(ns, ng, dims, early, valid_ref, (req_hbm, head_hbm, rslot_hbm, tail_hbm, neg_hbm), (ent_hbm, rel_hbm, *rest_hbm), ge_ref, gr_ref, stat_ref, (ent_v, rel_v, *rest_v), *refs)


def exchange(
    ns,
    ng,
    dims,
    early,
    valid_ref,
    small_hbm,
    tables_hbm,
    ge_ref,
    gr_ref,
    stat_ref,
    tables,
    req_v,
    slots_v,
    neg_v,
    eth,
    etl,
    rth,
    rtl,
    ids_all,
    idg,
    send_buf,
    recv_buf,
    rows_e,
    rows_r,
    oh_e,
    oh_r,
    hot_h,
    hot_t,
    hot_r,
    hotx,
    hott,
    wt,
    eh,
    el,
    rr,
    targets,
    anchors,
    folds,
    squares,
    edge_rows,
    form,
    y_h,
    y_l,
    gbuf,
    sgt_e,
    sgt_r,
    local_sem,
    ids_send,
    ids_recv,
    idg_send,
    idg_recv,
    f_send,
    f_recv,
    g_send,
    g_recv,
    core_send,
    y_send,
    turn_sem,
):
    d, ne, nr, cap, edges, neg = dims
    ent_v, rel_v = tables[:2]
    req_hbm, head_hbm, rslot_hbm, tail_hbm, neg_hbm = small_hbm
    ent_hbm, rel_hbm = tables_hbm[:2]
    cap_r = cap - CAP_E
    ke, kr = ns * CAP_E, ns * cap_r
    chunks = d // LANE
    rest = d - chunks * LANE
    dp = (chunks + 1) * LANE
    nrp = up(nr, LANE)
    segs = edges // SEG
    copies = LANE // rest
    subs = cap // 8
    ny = ng // 2

    g = lax.axis_index("grp")
    s = lax.axis_index("shard")
    parity = lax.rem(g, 2)
    mate = g + 1 - 2 * parity
    near = list(range(1, ns))
    order = near

    def shard_at(k):
        partner, bit = s, 1
        while bit < ns:
            if k & bit:
                partner = partner + bit * (1 - 2 * lax.rem(s // bit, 2))
            bit *= 2
        return partner

    shard_from = shard_at

    barrier = pltpu.get_barrier_semaphore()
    for k in range(1, ns):
        pl.semaphore_signal(barrier, inc=1, device_id={"shard": shard_at(k)})
    for k in range(1, ng):
        pl.semaphore_signal(barrier, inc=1, device_id={"grp": lax.rem(g + k, ng)})

    local = [
        pltpu.make_async_copy(src, dst, local_sem.at[i])
        for i, (src, dst) in enumerate(
            [
                (req_hbm, req_v),
                (ent_hbm, ent_v),
                (rel_hbm, rel_v),
                (head_hbm, slots_v.at[0]),
                (rslot_hbm, slots_v.at[1]),
                (tail_hbm, slots_v.at[2]),
                (neg_hbm, neg_v),
                *zip(tables_hbm[2:], tables[2:]),
            ]
        )
    ]
    for copy in local[:7]:
        copy.start()
    local[0].wait()
    pl.semaphore_wait(barrier, ns - 1 + ng - 1)

    def ids_copy(k):
        return pltpu.make_async_remote_copy(
            src_ref=req_v,
            dst_ref=ids_all.at[s],
            send_sem=ids_send.at[k],
            recv_sem=ids_recv.at[s],
            device_id={"shard": shard_at(k)},
        )

    def ids_arrival(k):
        return pltpu.make_async_remote_copy(
            src_ref=req_v,
            dst_ref=ids_all.at[shard_from(k)],
            send_sem=ids_send.at[k],
            recv_sem=ids_recv.at[shard_from(k)],
            device_id={"shard": shard_from(k)},
        )

    for k in order:
        ids_copy(k).start()
    ids_all[s] = req_v[...]

    local[1].wait()
    local[2].wait()

    for start in range(0, d, 80):
        at = slice(start, start + 80)
        eth[at, :], etl[at, :] = halves(ent_v[at, :])
        rth[at, 0:nr], rtl[at, 0:nr] = halves(rel_v[at, :])
    if nrp > nr:
        rth[:, nr:nrp] = jnp.zeros((dp, nrp - nr), BF16)
        rtl[:, nr:nrp] = jnp.zeros((dp, nrp - nr), BF16)
    for table in (eth, etl, rth, rtl):
        tail_rows = table[chunks * LANE : d, :]
        for c in range(1, copies):
            table[chunks * LANE + c * rest : chunks * LANE + (c + 1) * rest, :] = tail_rows

    for k in order:
        ids_arrival(k).wait_recv()
    for r in range(ns):
        idg[g, r : r + 1, :] = ids_all[r, pl.ds(s, 1), :]

    def idg_copy(k):
        return pltpu.make_async_remote_copy(
            src_ref=idg.at[g],
            dst_ref=idg.at[g],
            send_sem=idg_send.at[k],
            recv_sem=idg_recv.at[g],
            device_id={"grp": lax.rem(g + k, ng)},
        )

    def idg_arrival(k):
        other = lax.rem(g + ng - k, ng)
        return pltpu.make_async_remote_copy(
            src_ref=idg.at[other],
            dst_ref=idg.at[other],
            send_sem=idg_send.at[k],
            recv_sem=idg_recv.at[other],
            device_id={"grp": other},
        )

    lanes_e = iota((CAP_E, ne), 1).astype(F32)
    lanes_r = iota((cap_r, nrp), 1).astype(F32) + float(ne)

    def one_hots(at, blocks, columns):
        pieces = []
        for n, (grp, src) in enumerate(blocks):
            column = columns[grp][:, src : src + 1]
            hit = jnp.where(column[0:CAP_E] == lanes_e, 1.0, 0.0).astype(BF16)
            oh_e[at, n * CAP_E : (n + 1) * CAP_E, :] = hit
            pieces.append(jnp.where(column[CAP_E:cap] == lanes_r, 1.0, 0.0))
        hit = jnp.concatenate(pieces, axis=0).astype(BF16)
        oh_r[at, 0:kr, :] = hit
        oh_r[at, kr : 2 * kr, :] = hit

    def columns_of(grp):
        wide = jnp.concatenate([idg[grp].astype(F32), jnp.zeros((ns, LANE - cap), F32)], axis=1)
        return jnp.concatenate([wide, jnp.zeros((LANE - ns, LANE), F32)], axis=0).T

    one_hots(0, [(0, src) for src in range(ns)], [columns_of(g)])
    rows_e[...] = mm_nt(oh_e[0], eth[...]) + mm_nt(oh_e[0], etl[...])
    rows_r[...] = mm_nt(oh_r[0, 0:kr], rth[...]) + mm_nt(oh_r[0, 0:kr], rtl[...])

    lane8 = iota((8, LANE), 1)

    def pack(r, roll, extra):
        for c in range(chunks):
            at = slice(c * LANE, (c + 1) * LANE)
            send_buf[r, c * cap : c * cap + CAP_E, :] = rows_e[r * CAP_E : (r + 1) * CAP_E, at]
            send_buf[r, c * cap + CAP_E : (c + 1) * cap, :] = rows_r[r * cap_r : (r + 1) * cap_r, at]
        last = slice(chunks * LANE, dp)
        out = extra
        for j in range(subs):
            if j * 8 < CAP_E:
                piece = rows_e[r * CAP_E + j * 8 : r * CAP_E + j * 8 + 8, last]
            else:
                piece = rows_r[r * cap_r + j * 8 - CAP_E : r * cap_r + j * 8 - CAP_E + 8, last]
            if roll and j:
                piece = pltpu.roll(piece, j * rest, 1)
            out = jnp.where((lane8 >= j * rest) & (lane8 < (j + 1) * rest), piece, out)
        send_buf[r, chunks * cap : chunks * cap + 8, :] = out

    def last_columns(tile):
        pieces = []
        for j in range(subs):
            piece = pltpu.roll(tile, LANE - j * rest, 1) if j else tile
            pieces.append(jnp.where(lane8 < rest, piece, 0.0))
        return jnp.concatenate(pieces[: CAP_E // 8], axis=0), jnp.concatenate(pieces[CAP_E // 8 :], axis=0)

    def fetch_copy(k):
        peer = shard_at(k)
        return pltpu.make_async_remote_copy(
            src_ref=send_buf.at[peer],
            dst_ref=recv_buf.at[s],
            send_sem=f_send.at[k],
            recv_sem=f_recv.at[s],
            device_id={"shard": peer},
        )

    def fetch_arrival(k):
        peer = shard_from(k)
        return pltpu.make_async_remote_copy(
            src_ref=send_buf.at[peer],
            dst_ref=recv_buf.at[peer],
            send_sem=f_send.at[k],
            recv_sem=f_recv.at[peer],
            device_id={"shard": peer},
        )

    for r in range(ns):
        pack(r, False, jnp.zeros((8, LANE), F32))
    @pl.when(parity == 0)
    def _():
        for k in order:
            fetch_copy(k).start()

    recv_buf[s] = send_buf[s]
    for k in range(1, ng):
        idg_copy(k).start()
    for copy in local[7:]:
        copy.start()

    for copy in local[3:7]:
        copy.wait()
    slots = slots_v[...]
    owner = lax.shift_right_logical(slots * ((1 << 16) // cap + 1), 16)
    within = slots - owner * cap
    head_k = owner[0] * CAP_E + within[0]
    rel_k = owner[1] * cap_r + within[1] - CAP_E
    tail_k = owner[2] * CAP_E + within[2]
    for i in range(segs):
        at = slice(i * SEG, (i + 1) * SEG)
        head_row, rel_row, tail_row = (v[i : i + 1, :] for v in (head_k, rel_k, tail_k))
        hotx[0:ke, at] = jnp.where(iota((ke, SEG), 0) == head_row, 1.0, 0.0).astype(BF16)
        hott[:, at] = jnp.where(iota((ke, SEG), 0) == tail_row, 1.0, 0.0).astype(BF16)
        hotx[ke:, at] = jnp.where(iota((kr, SEG), 0) == rel_row, 1.0, 0.0).astype(BF16)
        head_col, rel_col, tail_col = (
            jnp.broadcast_to(v.astype(F32), (SEG, SEG)).T[:, 0:1] for v in (head_row, rel_row, tail_row)
        )
        slots_e = iota((SEG, ke), 1).astype(F32)
        slots_r = iota((SEG, kr), 1).astype(F32)
        hot_h[at, :] = jnp.where(slots_e == head_col, 1.0, 0.0).astype(BF16)
        hot_t[at, :] = jnp.where(slots_e == tail_col, 1.0, 0.0).astype(BF16)
        hit = jnp.where(slots_r == rel_col, 1.0, 0.0)
        hot_r[at, :] = jnp.concatenate([hit, hit], axis=1).astype(BF16)

    part = ns // 2
    batches = [
        ((core + 4 * pair_of, core + 4 * pair_of + 2), core, b * part)
        for core in range(2)
        for b in range(2)
        for pair_of in range(ny // 2)
    ]

    def batch_one_hots(n):
        groups, _, start = batches[n]
        columns = []
        for grp in groups:
            wide = jnp.concatenate([idg[grp, pl.ds(shard_at(k), 1), :].astype(F32) for k in range(start, start + part)], axis=0)
            wide = jnp.concatenate([wide, jnp.zeros((part, LANE - cap), F32)], axis=1)
            columns.append(jnp.concatenate([wide, jnp.zeros((LANE - part, LANE), F32)], axis=0).T)
        one_hots(n if early else 0, [(c, k) for c in range(2) for k in range(part)], columns)

    for k in range(1, ng):
        idg_arrival(k).wait_recv()
    if early:
        for n in range(len(batches)):
            batch_one_hots(n)

    valid = valid_ref[0]
    sub = iota((SEG, SEG), 0)
    lane = iota((SEG, SEG), 1)

    def count(i, total):
        start = pl.multiple_of(i * SEG, SEG)
        hits = jnp.zeros((SEG, SEG), F32)
        for k in range(neg):
            hits += jnp.where(neg_v[k : k + 1, pl.ds(start, SEG)] == sub, 1.0, 0.0)
        keep = (lane + start < valid) & (sub + start < valid) & (sub != lane)
        hits = jnp.where(keep, hits, 0.0)
        wt[i] = hits
        return total + hits

    pairs = jnp.sum(lax.fori_loop(0, segs, count, jnp.zeros((SEG, SEG), F32)))

    most = 4

    @pl.when(parity == 0)
    def _():
        for k in order[:most]:
            fetch_arrival(k).wait_recv()
        pl.semaphore_signal(turn_sem, inc=1, device_id={"grp": mate})
        for k in order[most:]:
            fetch_arrival(k).wait_recv()

    @pl.when(parity == 1)
    def _():
        pl.semaphore_wait(turn_sem, 1)
        for k in order:
            fetch_copy(k).start()
        for k in order:
            fetch_arrival(k).wait_recv()

    for p in range(ns):
        ends_e, ends_r = last_columns(recv_buf[p, chunks * cap : chunks * cap + 8, :])
        e = jnp.concatenate(
            [recv_buf[p, c * cap : c * cap + CAP_E, :] for c in range(chunks)] + [ends_e], axis=1
        )
        r = jnp.concatenate(
            [recv_buf[p, c * cap + CAP_E : (c + 1) * cap, :] for c in range(chunks)] + [ends_r], axis=1
        )
        at = slice(p * CAP_E, (p + 1) * CAP_E)
        eh[at, :], el[at, :] = halves(e)
        rows_r[p * cap_r : (p + 1) * cap_r, :] = r
    hi, lo = halves(rows_r[...])
    rr[0:kr, :] = hi
    rr[kr : 2 * kr, :] = lo

    def lane_fold(x):
        out = x[:, 0:LANE]
        for c in range(1, dp // LANE):
            out += x[:, c * LANE : (c + 1) * LANE]
        return out

    def seg(i):
        return slice(i * SEG, (i + 1) * SEG)

    def pair(i):
        return slice(2 * i * SEG, 2 * (i + 1) * SEG)

    for i in range(segs):
        hots = jnp.concatenate([hot_h[seg(i), :], hot_t[seg(i), :]], axis=0)
        both_h = mm(hots, eh[...])
        both_l = mm(hots, el[...])
        a = both_h[0:SEG] + both_l[0:SEG] + mm(hot_r[seg(i), :], rr[...])
        t = both_h[SEG:] + both_l[SEG:]
        targets[pair(i), :] = jnp.concatenate([both_h[SEG:].astype(BF16), both_l[SEG:].astype(BF16)], axis=0)
        anchors[pair(i), :] = jnp.concatenate(halves(a), axis=0)
        offset = a - t
        folds[0, i] = lane_fold(offset * offset)
        folds[1, i] = lane_fold(a * a)
        folds[2, i] = lane_fold(t * t)

    for i in range(segs):
        terms = mm_nt(targets[pair(i), :], anchors[pair(i), :])
        gram = terms[0:SEG, 0:SEG] + (terms[0:SEG, SEG:] + terms[SEG:, 0:SEG] + terms[SEG:, SEG:])
        square_pos = jnp.sum(folds[0, i].T, axis=0, keepdims=True)
        edge_rows[0:1, seg(i)] = jnp.sqrt(square_pos + EPS_DIST)
        anchor_sq = jnp.sum(folds[1, i].T, axis=0, keepdims=True)
        target_sq = jnp.sum(folds[2, i], axis=1, keepdims=True)
        squares[i] = anchor_sq + target_sq - 2.0 * gram

    loss = jnp.zeros((SEG, SEG), F32)
    for i in range(segs):
        square = jnp.maximum(squares[i], 0.0) + EPS_DIST
        dist_pos = edge_rows[0:1, seg(i)]
        inv = lax.rsqrt(square)
        m = MARGIN + dist_pos - square * inv
        w = wt[i]
        small = jnp.exp(-jnp.abs(m))
        loss += w * (jnp.maximum(m, 0.0) + jnp.log1p(small))
        slope = w * (jnp.where(m >= 0.0, 1.0, small) / (1.0 + small))
        ratio = jnp.sum(slope, axis=0, keepdims=True) / dist_pos
        pt = slope * inv - jnp.where(sub == lane, ratio, 0.0)
        pa = pt.T
        sum_a = jnp.sum(pt, axis=0, keepdims=True)
        edge_rows[1:2, seg(i)] = sum_a
        edge_rows[2:3, seg(i)] = jnp.sum(pa, axis=0, keepdims=True)
        own_h, own_l = halves(jnp.where(sub == lane, -sum_a, 0.0))
        pa_h, pa_l = halves(pa)
        form[pair(i), 0:SEG] = jnp.concatenate([pa_h, pa_l], axis=0)
        form[pair(i), SEG:] = jnp.concatenate([own_h, own_l], axis=0)
    loss = jnp.sum(loss)

    for i in range(segs):
        hots = jnp.concatenate([hot_t[seg(i), :], hot_h[seg(i), :]], axis=0)
        y = mm(form[pair(i), :], hots)
        y_h[seg(i), :], y_l[seg(i), :] = halves(y[0:SEG] + y[SEG:])
    crossed = mm(hotx[...], y_h[...]) + mm(hotx[...], y_l[...])
    form_re = crossed[ke:]
    own_e = jnp.zeros((ke, LANE), F32)
    own_r = jnp.zeros((kr, LANE), F32)
    for i in range(segs):
        sum_a = edge_rows[1:2, seg(i)]
        sum_t = edge_rows[2:3, seg(i)]
        own_e += hotx[0:ke, seg(i)].astype(F32) * sum_a - hott[:, seg(i)].astype(F32) * sum_t
        own_r -= hotx[ke:, seg(i)].astype(F32) * sum_a
    own_e = jnp.sum(own_e, axis=1, keepdims=True)
    own_r = jnp.sum(own_r, axis=1, keepdims=True)
    diagonal = iota((ke, ke), 0) == iota((ke, ke), 1)
    form_ee = crossed[0:ke] + crossed[0:ke].T + jnp.where(diagonal, own_e, 0.0)

    ee_h, ee_l = halves(form_ee)
    re_h, re_l = halves(form_re)
    er_h, er_l = halves(form_re.T)
    rows_e[...] = (
        mm(ee_h, eh[...])
        + (mm(ee_h, el[...]) + mm(ee_l, eh[...]))
        + (mm(jnp.concatenate([er_h, er_h], axis=1), rr[...]) + mm(er_l, rr[0:kr, :]))
    )
    rows_r[...] = (
        mm(re_h, eh[...])
        + (mm(re_h, el[...]) + mm(re_l, eh[...]))
        + own_r * (rr[0:kr, :].astype(F32) + rr[kr : 2 * kr, :].astype(F32))
    )
    at_loss = copies * rest - 2
    extra = jnp.where(lane8 == at_loss, loss, jnp.where(lane8 == at_loss + 1, pairs, 0.0))

    def grad_copy(k):
        peer = shard_at(k)
        return pltpu.make_async_remote_copy(
            src_ref=send_buf.at[peer],
            dst_ref=gbuf.at[g, s],
            send_sem=g_send.at[k],
            recv_sem=g_recv.at[g, s],
            device_id={"shard": peer},
        )

    def block_copy(grp, src, to, send_sem):
        return pltpu.make_async_remote_copy(
            src_ref=gbuf.at[grp, src],
            dst_ref=gbuf.at[grp, src],
            send_sem=send_sem,
            recv_sem=g_recv.at[grp, src],
            device_id={"grp": to},
        )

    def arrived(grp, src):
        block_copy(grp, src, mate, core_send.at[0, 0]).wait_recv()

    for k in order:
        fetch_copy(k).wait_send()
    for r in range(ns):
        pack(r, True, extra)
    for k in near:
        grad_copy(k).start()
    gbuf[g, s] = send_buf[s]

    def group_up(dy):
        return lax.rem(g + 2 * dy, ng)

    def group_down(dy):
        return lax.rem(g + ng - 2 * dy, ng)

    def forward(src):
        out = [block_copy(g, src, group_up(dy), y_send.at[dy - 1, src]) for dy in range(1, ny)]
        return out + [block_copy(g, src, mate, core_send.at[0, src])]

    def hand_over(dy, src):
        return block_copy(group_down(dy), src, mate, core_send.at[dy, src])

    sequence = [0] + near
    lag = 2
    handed = [0]

    def hand_over_to(end):
        end = max(end, handed[0])
        for k in sequence[handed[0] : end]:
            for dy in range(1, ny):
                arrived(group_down(dy), shard_at(k))
                hand_over(dy, shard_at(k)).start()
        handed[0] = end

    def hand_over_last():
        for dy in range(1, ny):
            arrived(group_down(dy), shard_at(sequence[-1]))
            hand_over(dy, shard_at(sequence[-1])).start()

    def add_batch(n):
        groups, core, start = batches[n]

        @pl.when(parity != core)
        def _():
            for k in range(start, start + part):
                for grp in groups:
                    arrived(grp, shard_at(k))

        if not early:
            batch_one_hots(n)
        at = n if early else 0
        blocks = [(grp, shard_at(k)) for grp in groups for k in range(start, start + part)]
        ends = [last_columns(gbuf[grp, src, chunks * cap : chunks * cap + 8, :]) for grp, src in blocks]
        for c in range(chunks + 1):
            size = LANE if c < chunks else rest
            put = slice(c * LANE, c * LANE + size)
            if c < chunks:
                e = [gbuf[grp, src, c * cap : c * cap + CAP_E, :] for grp, src in blocks]
                r = [gbuf[grp, src, c * cap + CAP_E : (c + 1) * cap, :] for grp, src in blocks]
            else:
                e, r = [x[0] for x in ends], [x[1] for x in ends]
            hi, lo = halves(jnp.concatenate(e, axis=0).T[0:size, :])
            sgt_e[put, 0:ke] = hi
            sgt_e[put, ke : 2 * ke] = lo
            hi, lo = halves(jnp.concatenate(r, axis=0).T[0:size, :])
            sgt_r[put, 0:kr] = hi
            sgt_r[put, kr : 2 * kr] = lo
        part_e = mm(sgt_e[:, 0:ke], oh_e[at]) + mm(sgt_e[:, ke : 2 * ke], oh_e[at])
        part_r = mm(sgt_r[...], oh_r[at])
        if n:
            ge_ref[...] += part_e
            gr_ref[...] += part_r[:, 0:nr]
        else:
            ge_ref[...] = part_e
            gr_ref[...] = part_r[:, 0:nr]

    def pass_on(idx):
        k = sequence[idx]
        if k:
            arrived(g, shard_at(k))
        for copy in forward(shard_at(k)):
            copy.start()

    for idx in range(ns):
        pass_on(idx)
        hand_over_to(idx + 1 - lag)
    for copy in local[7:]:
        copy.wait()
    for k in near:
        ids_copy(k).wait_send()
        grad_copy(k).wait_send()
    for k in range(1, ng):
        idg_copy(k).wait_send()
    quarter = len(batches) // 4
    for n in range(quarter):
        add_batch(n)
    hand_over_to(ns - 1)

    @pl.when(parity == 0)
    def _():
        hand_over_last()

    for n in range(quarter, 2 * quarter):
        add_batch(n)

    @pl.when(parity == 1)
    def _():
        hand_over_last()

    for n in range(2 * quarter, 4 * quarter):
        add_batch(n)

    def stat(i, total):
        for r in range(ns):
            total += gbuf[i, r, chunks * cap : chunks * cap + 8, :]
        return total

    stat_ref[...] = lax.fori_loop(0, ng, stat, jnp.zeros((8, LANE), F32))

    for k in sequence:
        src = shard_from(k)
        for copy in forward(src):
            copy.wait_send()
        for dy in range(1, ny):
            hand_over(dy, src).wait_send()


def adamw_kernel(
    at_loss,
    strip,
    stat_ref,
    ge_ref,
    gr_ref,
    w_e,
    one_e,
    two_e,
    w_r,
    one_r,
    two_r,
    e_new,
    e_one,
    e_two,
    e_low,
    r_new,
    r_one,
    r_two,
    r_low,
    loss_ref,
    pairs_ref,
    *scratch,
):
    d = ge_ref.shape[0]
    sems = scratch[-1]
    total = stat_ref[0:1, :]
    sums = [
        pltpu.make_async_copy(buf, out, sems.at[n, 0])
        for n, (buf, out) in enumerate(zip(scratch[8:10], (loss_ref, pairs_ref)), 8)
    ]
    for n, copy in enumerate(sums):
        scratch[8 + n][0] = total[0, at_loss + n]
        copy.start()
    factor = ((1.0 - BETA_ONE) / total)[0, at_loss + 1]
    square = (1.0 - BETA_TWO) / (1.0 - BETA_ONE) ** 2
    fix_two = 1.0 / (1.0 - BETA_TWO**STEP)
    rate = RATE / (1.0 - BETA_ONE**STEP)
    tables = (
        (ge_ref, w_e, one_e, two_e, (e_new, e_one, e_two, e_low), scratch[0:4]),
        (gr_ref, w_r, one_r, two_r, (r_new, r_one, r_two, r_low), scratch[4:8]),
    )

    def copies(i):
        at = pl.ds(pl.multiple_of(i * strip, strip), strip)
        out = []
        for n, (_, _, _, _, outs, bufs) in enumerate(tables):
            for m, (hbm, buf) in enumerate(zip(outs, bufs)):
                out.append(pltpu.make_async_copy(buf.at[at, :], hbm.at[at, :], sems.at[n * 4 + m, i]))
        return out

    def step(i, _):
        for g_ref, w_ref, one_ref, two_ref, _, bufs in tables:

            def rows(j, _):
                at = pl.ds(pl.multiple_of(i * strip, 16), strip)
                gradient = g_ref[at, :] * factor
                weight = w_ref[at, :]
                one = BETA_ONE * one_ref[at, :] + gradient
                two = BETA_TWO * two_ref[at, :] + square * gradient * gradient
                scaled = two * fix_two
                root = scaled * lax.rsqrt(scaled) + EPS_ADAM
                new = weight * (1.0 - RATE * DECAY) - rate * one / root
                bufs[0][at, :] = new
                bufs[1][at, :] = one
                bufs[2][at, :] = two
                bufs[3][at, :] = new.astype(BF16)
                return 0

            rows(0, 0)
        for copy in copies(i):
            copy.start()
        return 0

    steps = d // strip
    lax.fori_loop(0, steps, step, 0)
    for i in range(steps):
        for copy in copies(i):
            copy.wait()
    for copy in sums:
        copy.wait()


def per_device(
    ns,
    ng,
    entity_rows,
    entity_first,
    entity_second,
    relation_rows,
    relation_first,
    relation_second,
    requests,
    head_slots,
    relation_slots,
    tail_slots,
    neg_offsets,
    valid_counts,
):
    ne, d = entity_rows.shape
    nr = relation_rows.shape[0]
    cap = requests.shape[2]
    cap_r = cap - CAP_E
    edges, neg = neg_offsets.shape
    segs = edges // SEG
    ke, kr = ns * CAP_E, ns * cap_r
    chunks = d // LANE
    rest = d - chunks * LANE
    dp = (chunks + 1) * LANE
    nrp = up(nr, LANE)
    ny = ng // 2
    block = (LANE, LANE)
    any_space = pl.BlockSpec(memory_space=pl.ANY)
    vmem = pl.BlockSpec(memory_space=pltpu.VMEM)
    smem = pl.BlockSpec(memory_space=pltpu.SMEM)
    dma = pltpu.SemaphoreType.DMA
    hbm = functools.partial(pltpu.with_memory_space_constraint, memory_space=pltpu.HBM)
    batches = ng if ng <= 4 else 1
    scratch = [
        pltpu.VMEM((ns, cap), I32),
        pltpu.VMEM((3, segs, SEG), I32),
        pltpu.VMEM((neg, edges), I32),
        pltpu.VMEM((dp, ne), BF16),
        pltpu.VMEM((dp, ne), BF16),
        pltpu.VMEM((dp, nrp), BF16),
        pltpu.VMEM((dp, nrp), BF16),
        pltpu.VMEM((ns, ns, cap), I32),
        pltpu.VMEM((ng, ns, cap), I32),
        pltpu.VMEM((ns, *block), F32),
        pltpu.VMEM((ns, *block), F32),
        pltpu.VMEM((ke, dp), F32),
        pltpu.VMEM((kr, dp), F32),
        pltpu.VMEM((batches, ke, ne), BF16),
        pltpu.VMEM((batches, 2 * kr, nrp), BF16),
        pltpu.VMEM((edges, ke), BF16),
        pltpu.VMEM((edges, ke), BF16),
        pltpu.VMEM((edges, 2 * kr), BF16),
        pltpu.VMEM((ke + kr, edges), BF16),
        pltpu.VMEM((ke, edges), BF16),
        pltpu.VMEM((segs, SEG, SEG), F32),
        pltpu.VMEM((ke, dp), BF16),
        pltpu.VMEM((ke, dp), BF16),
        pltpu.VMEM((2 * kr, dp), BF16),
        pltpu.VMEM((2 * edges, dp), BF16),
        pltpu.VMEM((2 * edges, dp), BF16),
        pltpu.VMEM((3, segs, SEG, SEG), F32),
        pltpu.VMEM((segs, SEG, SEG), F32),
        pltpu.VMEM((8, edges), F32),
        pltpu.VMEM((2 * edges, 2 * SEG), BF16),
        pltpu.VMEM((edges, ke), BF16),
        pltpu.VMEM((edges, ke), BF16),
        pltpu.VMEM((ng, ns, *block), F32),
        pltpu.VMEM((d, 2 * ke), BF16),
        pltpu.VMEM((d, 2 * kr), BF16),
        dma((11,)),
        dma((ns,)),
        dma((ns,)),
        dma((ng,)),
        dma((ng,)),
        dma((ns,)),
        dma((ns,)),
        dma((ns,)),
        dma((ng, ns)),
        dma((ny, ns)),
        dma((max(ny - 1, 1), ns)),
        pltpu.SemaphoreType.REGULAR,
    ]
    small = [
        requests[0],
        head_slots.reshape(segs, SEG),
        relation_slots.reshape(segs, SEG),
        tail_slots.reshape(segs, SEG),
        neg_offsets.T,
    ]
    rows = [entity_rows.T, relation_rows.T]
    moments = [entity_first.T, entity_second.T, relation_first.T, relation_second.T]
    sums = [pltpu.VMEM((d, ne), F32), pltpu.VMEM((d, nr), F32), pltpu.VMEM((8, LANE), F32)]
    held_rows = [pltpu.VMEM(x.shape, F32) for x in rows]
    held_moments = [pltpu.VMEM(x.shape, F32) for x in moments]
    need = sum(padded(x) for x in scratch[: scratch.index(dma((11,)))]) + (2 << 20)
    keep = need + sum(padded(x) for x in sums + held_rows + held_moments) < (62 << 20)
    if keep:
        outs, held = sums + held_rows + held_moments, []
    else:
        outs, held = sums, held_rows
        need += sum(padded(x) for x in held)
    operands = small + rows + (moments if keep else [])
    ge, gr, stat, *passed = pl.pallas_call(
        functools.partial(exchange_kernel, ns, ng, (d, ne, nr, cap, edges, neg), int(keep), batches > 1),
        out_shape=outs,
        in_specs=[smem] + [any_space] * len(operands),
        out_specs=[vmem] * len(outs),
        scratch_shapes=held + scratch,
        compiler_params=pltpu.CompilerParams(
            collective_id=0, has_side_effects=True, vmem_limit_bytes=need
        ),
    )(valid_counts, *[hbm(x) for x in operands])
    if not keep:
        passed = rows + moments
    w_e, w_r, one_e, two_e, one_r, two_r = passed
    tables = (w_e, one_e, two_e, w_r, one_r, two_r)
    at_loss = LANE // rest * rest - 2
    strip = 80
    shapes = [(jax.ShapeDtypeStruct((d, n), t)) for n in (ne, nr) for t in (F32, F32, F32, BF16)]
    one = jax.ShapeDtypeStruct((1,), F32)
    *outs, loss, pairs = pl.pallas_call(
        functools.partial(adamw_kernel, at_loss, strip),
        out_shape=shapes + [one, one],
        in_specs=[vmem] * 9,
        out_specs=[any_space] * 10,
        scratch_shapes=[pltpu.VMEM(x.shape, x.dtype) for x in shapes] + [pltpu.SMEM((1,), F32)] * 2 + [dma((10, d // strip))],
        compiler_params=pltpu.CompilerParams(vmem_limit_bytes=32 * 1024 * 1024),
    )(stat, ge, gr, *tables)
    e_new, e_one, e_two, e_low, r_new, r_one, r_two, r_low = (x.T for x in outs)
    return (e_new, e_one, e_two, r_new, r_one, r_two, e_low, r_low, loss, pairs)


def solution(mesh):
    rows = P("shard", None)
    both = ("grp", "shard")
    return jax.shard_map(
        functools.partial(per_device, mesh.shape["shard"], mesh.shape["grp"]),
        mesh=mesh,
        in_specs=(
            rows,
            rows,
            rows,
            rows,
            rows,
            rows,
            P(both, None, None),
            P(both),
            P(both),
            P(both),
            P(both, None),
            P(both),
        ),
        out_specs=(rows,) * 8 + (P(), P()),
        check_vma=False,
    )
```

```python
import functools
import math

import jax
import jax.numpy as jnp
from jax import lax
from jax.experimental import pallas as pl
from jax.experimental.pallas import tpu as pltpu
from jax.sharding import PartitionSpec as P

CAP_E = 32
SEG = 128
STEP = 10
LANE = 128

MARGIN = 0.1
EPS_DIST = 1e-06
BETA_ONE = 0.9
BETA_TWO = 0.999
RATE = 0.5
DECAY = 0.01
EPS_ADAM = 1e-08

F32 = jnp.float32
BF16 = jnp.bfloat16
I32 = jnp.int32


def mm(a, b):
    return lax.dot_general(a, b, (((1,), (0,)), ((), ())), preferred_element_type=F32)


def mm_nt(a, b):
    return lax.dot_general(a, b, (((1,), (1,)), ((), ())), preferred_element_type=F32)


def halves(x):
    hi = x.astype(BF16)
    return hi, (x - hi.astype(F32)).astype(BF16)


def up(n, m):
    return (n + m - 1) // m * m


def iota(shape, axis):
    return lax.broadcasted_iota(I32, shape, axis)


def padded(ref):
    *lead, rows, cols = ref.shape
    size = jnp.dtype(ref.dtype).itemsize
    return math.prod(lead) * up(rows, 32 // size) * up(cols, LANE) * size


def exchange_kernel(
    ns,
    ng,
    dims,
    keep,
    early,
    valid_ref,
    req_hbm,
    head_hbm,
    rslot_hbm,
    tail_hbm,
    neg_hbm,
    ent_hbm,
    rel_hbm,
    *refs,
):
    rest_hbm, refs = refs[: 4 * keep], refs[4 * keep :]
    ge_ref, gr_ref, stat_ref, ent_v, rel_v, *refs = refs
    rest_v, refs = refs[: 4 * keep], refs[4 * keep :]
    exchange(ns, ng, dims, early, valid_ref, (req_hbm, head_hbm, rslot_hbm, tail_hbm, neg_hbm), (ent_hbm, rel_hbm, *rest_hbm), ge_ref, gr_ref, stat_ref, (ent_v, rel_v, *rest_v), *refs)


def exchange(
    ns,
    ng,
    dims,
    early,
    valid_ref,
    small_hbm,
    tables_hbm,
    ge_ref,
    gr_ref,
    stat_ref,
    tables,
    req_v,
    slots_v,
    neg_v,
    eth,
    etl,
    rth,
    rtl,
    ids_all,
    idg,
    send_buf,
    recv_buf,
    rows_e,
    rows_r,
    oh_e,
    oh_r,
    hot_h,
    hot_t,
    hot_r,
    hotx,
    hott,
    wt,
    eh,
    el,
    rr,
    targets,
    anchors,
    folds,
    squares,
    edge_rows,
    form,
    y_h,
    y_l,
    gbuf,
    sgt_e,
    sgt_r,
    local_sem,
    ids_send,
    ids_recv,
    idg_send,
    idg_recv,
    f_send,
    f_recv,
    g_send,
    g_recv,
    core_send,
    y_send,
    turn_sem,
):
    d, ne, nr, cap, edges, neg = dims
    ent_v, rel_v = tables[:2]
    req_hbm, head_hbm, rslot_hbm, tail_hbm, neg_hbm = small_hbm
    ent_hbm, rel_hbm = tables_hbm[:2]
    cap_r = cap - CAP_E
    ke, kr = ns * CAP_E, ns * cap_r
    chunks = d // LANE
    rest = d - chunks * LANE
    dp = (chunks + 1) * LANE
    nrp = up(nr, LANE)
    segs = edges // SEG
    copies = LANE // rest
    subs = cap // 8
    ny = ng // 2

    g = lax.axis_index("grp")
    s = lax.axis_index("shard")
    parity = lax.rem(g, 2)
    mate = g + 1 - 2 * parity
    near = list(range(1, ns))
    order = near

    def shard_at(k):
        partner, bit = s, 1
        while bit < ns:
            if k & bit:
                partner = partner + bit * (1 - 2 * lax.rem(s // bit, 2))
            bit *= 2
        return partner

    shard_from = shard_at

    barrier = pltpu.get_barrier_semaphore()
    for k in range(1, ns):
        pl.semaphore_signal(barrier, inc=1, device_id={"shard": shard_at(k)})
    for k in range(1, ng):
        pl.semaphore_signal(barrier, inc=1, device_id={"grp": lax.rem(g + k, ng)})

    local = [
        pltpu.make_async_copy(src, dst, local_sem.at[i])
        for i, (src, dst) in enumerate(
            [
                (req_hbm, req_v),
                (ent_hbm, ent_v),
                (rel_hbm, rel_v),
                (head_hbm, slots_v.at[0]),
                (rslot_hbm, slots_v.at[1]),
                (tail_hbm, slots_v.at[2]),
                (neg_hbm, neg_v),
                *zip(tables_hbm[2:], tables[2:]),
            ]
        )
    ]
    for copy in local[:7]:
        copy.start()
    local[0].wait()
    pl.semaphore_wait(barrier, ns - 1 + ng - 1)

    def ids_copy(k):
        return pltpu.make_async_remote_copy(
            src_ref=req_v,
            dst_ref=ids_all.at[s],
            send_sem=ids_send.at[k],
            recv_sem=ids_recv.at[s],
            device_id={"shard": shard_at(k)},
        )

    def ids_arrival(k):
        return pltpu.make_async_remote_copy(
            src_ref=req_v,
            dst_ref=ids_all.at[shard_from(k)],
            send_sem=ids_send.at[k],
            recv_sem=ids_recv.at[shard_from(k)],
            device_id={"shard": shard_from(k)},
        )

    for k in order:
        ids_copy(k).start()
    ids_all[s] = req_v[...]

    local[1].wait()
    local[2].wait()

    for start in range(0, d, 80):
        at = slice(start, start + 80)
        eth[at, :], etl[at, :] = halves(ent_v[at, :])
        rth[at, 0:nr], rtl[at, 0:nr] = halves(rel_v[at, :])
    if nrp > nr:
        rth[:, nr:nrp] = jnp.zeros((dp, nrp - nr), BF16)
        rtl[:, nr:nrp] = jnp.zeros((dp, nrp - nr), BF16)
    for table in (eth, etl, rth, rtl):
        tail_rows = table[chunks * LANE : d, :]
        for c in range(1, copies):
            table[chunks * LANE + c * rest : chunks * LANE + (c + 1) * rest, :] = tail_rows

    for k in order:
        ids_arrival(k).wait_recv()
    for r in range(ns):
        idg[g, r : r + 1, :] = ids_all[r, pl.ds(s, 1), :]

    def idg_copy(k):
        return pltpu.make_async_remote_copy(
            src_ref=idg.at[g],
            dst_ref=idg.at[g],
            send_sem=idg_send.at[k],
            recv_sem=idg_recv.at[g],
            device_id={"grp": lax.rem(g + k, ng)},
        )

    def idg_arrival(k):
        other = lax.rem(g + ng - k, ng)
        return pltpu.make_async_remote_copy(
            src_ref=idg.at[other],
            dst_ref=idg.at[other],
            send_sem=idg_send.at[k],
            recv_sem=idg_recv.at[other],
            device_id={"grp": other},
        )

    lanes_e = iota((CAP_E, ne), 1).astype(F32)
    lanes_r = iota((cap_r, nrp), 1).astype(F32) + float(ne)

    def one_hots(at, blocks, columns):
        pieces = []
        for n, (grp, src) in enumerate(blocks):
            column = columns[grp][:, src : src + 1]
            hit = jnp.where(column[0:CAP_E] == lanes_e, 1.0, 0.0).astype(BF16)
            oh_e[at, n * CAP_E : (n + 1) * CAP_E, :] = hit
            pieces.append(jnp.where(column[CAP_E:cap] == lanes_r, 1.0, 0.0))
        hit = jnp.concatenate(pieces, axis=0).astype(BF16)
        oh_r[at, 0:kr, :] = hit
        oh_r[at, kr : 2 * kr, :] = hit

    def columns_of(grp):
        wide = jnp.concatenate([idg[grp].astype(F32), jnp.zeros((ns, LANE - cap), F32)], axis=1)
        return jnp.concatenate([wide, jnp.zeros((LANE - ns, LANE), F32)], axis=0).T

    one_hots(0, [(0, src) for src in range(ns)], [columns_of(g)])
    rows_e[...] = mm_nt(oh_e[0], eth[...]) + mm_nt(oh_e[0], etl[...])
    rows_r[...] = mm_nt(oh_r[0, 0:kr], rth[...]) + mm_nt(oh_r[0, 0:kr], rtl[...])

    lane8 = iota((8, LANE), 1)

    def pack(r, roll, extra):
        for c in range(chunks):
            at = slice(c * LANE, (c + 1) * LANE)
            send_buf[r, c * cap : c * cap + CAP_E, :] = rows_e[r * CAP_E : (r + 1) * CAP_E, at]
            send_buf[r, c * cap + CAP_E : (c + 1) * cap, :] = rows_r[r * cap_r : (r + 1) * cap_r, at]
        last = slice(chunks * LANE, dp)
        out = extra
        for j in range(subs):
            if j * 8 < CAP_E:
                piece = rows_e[r * CAP_E + j * 8 : r * CAP_E + j * 8 + 8, last]
            else:
                piece = rows_r[r * cap_r + j * 8 - CAP_E : r * cap_r + j * 8 - CAP_E + 8, last]
            if roll and j:
                piece = pltpu.roll(piece, j * rest, 1)
            out = jnp.where((lane8 >= j * rest) & (lane8 < (j + 1) * rest), piece, out)
        send_buf[r, chunks * cap : chunks * cap + 8, :] = out

    def last_columns(tile):
        pieces = []
        for j in range(subs):
            piece = pltpu.roll(tile, LANE - j * rest, 1) if j else tile
            pieces.append(jnp.where(lane8 < rest, piece, 0.0))
        return jnp.concatenate(pieces[: CAP_E // 8], axis=0), jnp.concatenate(pieces[CAP_E // 8 :], axis=0)

    def fetch_copy(k):
        peer = shard_at(k)
        return pltpu.make_async_remote_copy(
            src_ref=send_buf.at[peer],
            dst_ref=recv_buf.at[s],
            send_sem=f_send.at[k],
            recv_sem=f_recv.at[s],
            device_id={"shard": peer},
        )

    def fetch_arrival(k):
        peer = shard_from(k)
        return pltpu.make_async_remote_copy(
            src_ref=send_buf.at[peer],
            dst_ref=recv_buf.at[peer],
            send_sem=f_send.at[k],
            recv_sem=f_recv.at[peer],
            device_id={"shard": peer},
        )

    for r in range(ns):
        pack(r, False, jnp.zeros((8, LANE), F32))
    @pl.when(parity == 0)
    def _():
        for k in order:
            fetch_copy(k).start()

    recv_buf[s] = send_buf[s]
    for k in range(1, ng):
        idg_copy(k).start()
    for copy in local[7:]:
        copy.start()

    for copy in local[3:7]:
        copy.wait()
    slots = slots_v[...]
    owner = lax.shift_right_logical(slots * ((1 << 16) // cap + 1), 16)
    within = slots - owner * cap
    head_k = owner[0] * CAP_E + within[0]
    rel_k = owner[1] * cap_r + within[1] - CAP_E
    tail_k = owner[2] * CAP_E + within[2]
    for i in range(segs):
        at = slice(i * SEG, (i + 1) * SEG)
        head_row, rel_row, tail_row = (v[i : i + 1, :] for v in (head_k, rel_k, tail_k))
        hotx[0:ke, at] = jnp.where(iota((ke, SEG), 0) == head_row, 1.0, 0.0).astype(BF16)
        hott[:, at] = jnp.where(iota((ke, SEG), 0) == tail_row, 1.0, 0.0).astype(BF16)
        hotx[ke:, at] = jnp.where(iota((kr, SEG), 0) == rel_row, 1.0, 0.0).astype(BF16)
        head_col, rel_col, tail_col = (
            jnp.broadcast_to(v.astype(F32), (SEG, SEG)).T[:, 0:1] for v in (head_row, rel_row, tail_row)
        )
        slots_e = iota((SEG, ke), 1).astype(F32)
        slots_r = iota((SEG, kr), 1).astype(F32)
        hot_h[at, :] = jnp.where(slots_e == head_col, 1.0, 0.0).astype(BF16)
        hot_t[at, :] = jnp.where(slots_e == tail_col, 1.0, 0.0).astype(BF16)
        hit = jnp.where(slots_r == rel_col, 1.0, 0.0)
        hot_r[at, :] = jnp.concatenate([hit, hit], axis=1).astype(BF16)

    part = ns // 2
    batches = [
        ((core + 4 * pair_of, core + 4 * pair_of + 2), core, b * part)
        for core in range(2)
        for b in range(2)
        for pair_of in range(ny // 2)
    ]

    def batch_one_hots(n):
        groups, _, start = batches[n]
        columns = []
        for grp in groups:
            wide = jnp.concatenate([idg[grp, pl.ds(shard_at(k), 1), :].astype(F32) for k in range(start, start + part)], axis=0)
            wide = jnp.concatenate([wide, jnp.zeros((part, LANE - cap), F32)], axis=1)
            columns.append(jnp.concatenate([wide, jnp.zeros((LANE - part, LANE), F32)], axis=0).T)
        one_hots(n if early else 0, [(c, k) for c in range(2) for k in range(part)], columns)

    for k in range(1, ng):
        idg_arrival(k).wait_recv()
    if early:
        for n in range(len(batches)):
            batch_one_hots(n)

    valid = valid_ref[0]
    sub = iota((SEG, SEG), 0)
    lane = iota((SEG, SEG), 1)

    def count(i, total):
        start = pl.multiple_of(i * SEG, SEG)
        hits = jnp.zeros((SEG, SEG), F32)
        for k in range(neg):
            hits += jnp.where(neg_v[k : k + 1, pl.ds(start, SEG)] == sub, 1.0, 0.0)
        keep = (lane + start < valid) & (sub + start < valid) & (sub != lane)
        hits = jnp.where(keep, hits, 0.0)
        wt[i] = hits
        return total + hits

    pairs = jnp.sum(lax.fori_loop(0, segs, count, jnp.zeros((SEG, SEG), F32)))

    most = 4

    @pl.when(parity == 0)
    def _():
        for k in order[:most]:
            fetch_arrival(k).wait_recv()
        pl.semaphore_signal(turn_sem, inc=1, device_id={"grp": mate})
        for k in order[most:]:
            fetch_arrival(k).wait_recv()

    @pl.when(parity == 1)
    def _():
        pl.semaphore_wait(turn_sem, 1)
        for k in order:
            fetch_copy(k).start()
        for k in order:
            fetch_arrival(k).wait_recv()

    for p in range(ns):
        ends_e, ends_r = last_columns(recv_buf[p, chunks * cap : chunks * cap + 8, :])
        e = jnp.concatenate(
            [recv_buf[p, c * cap : c * cap + CAP_E, :] for c in range(chunks)] + [ends_e], axis=1
        )
        r = jnp.concatenate(
            [recv_buf[p, c * cap + CAP_E : (c + 1) * cap, :] for c in range(chunks)] + [ends_r], axis=1
        )
        at = slice(p * CAP_E, (p + 1) * CAP_E)
        eh[at, :], el[at, :] = halves(e)
        rows_r[p * cap_r : (p + 1) * cap_r, :] = r
    hi, lo = halves(rows_r[...])
    rr[0:kr, :] = hi
    rr[kr : 2 * kr, :] = lo

    def lane_fold(x):
        out = x[:, 0:LANE]
        for c in range(1, dp // LANE):
            out += x[:, c * LANE : (c + 1) * LANE]
        return out

    def seg(i):
        return slice(i * SEG, (i + 1) * SEG)

    def pair(i):
        return slice(2 * i * SEG, 2 * (i + 1) * SEG)

    for i in range(segs):
        hots = jnp.concatenate([hot_h[seg(i), :], hot_t[seg(i), :]], axis=0)
        both_h = mm(hots, eh[...])
        both_l = mm(hots, el[...])
        a = both_h[0:SEG] + both_l[0:SEG] + mm(hot_r[seg(i), :], rr[...])
        t = both_h[SEG:] + both_l[SEG:]
        targets[pair(i), :] = jnp.concatenate([both_h[SEG:].astype(BF16), both_l[SEG:].astype(BF16)], axis=0)
        anchors[pair(i), :] = jnp.concatenate(halves(a), axis=0)
        offset = a - t
        folds[0, i] = lane_fold(offset * offset)
        folds[1, i] = lane_fold(a * a)
        folds[2, i] = lane_fold(t * t)

    for i in range(segs):
        terms = mm_nt(targets[pair(i), :], anchors[pair(i), :])
        gram = terms[0:SEG, 0:SEG] + (terms[0:SEG, SEG:] + terms[SEG:, 0:SEG] + terms[SEG:, SEG:])
        square_pos = jnp.sum(folds[0, i].T, axis=0, keepdims=True)
        edge_rows[0:1, seg(i)] = jnp.sqrt(square_pos + EPS_DIST)
        anchor_sq = jnp.sum(folds[1, i].T, axis=0, keepdims=True)
        target_sq = jnp.sum(folds[2, i], axis=1, keepdims=True)
        squares[i] = anchor_sq + target_sq - 2.0 * gram

    loss = jnp.zeros((SEG, SEG), F32)
    for i in range(segs):
        square = jnp.maximum(squares[i], 0.0) + EPS_DIST
        dist_pos = edge_rows[0:1, seg(i)]
        inv = lax.rsqrt(square)
        m = MARGIN + dist_pos - square * inv
        w = wt[i]
        small = jnp.exp(-jnp.abs(m))
        loss += w * (jnp.maximum(m, 0.0) + jnp.log1p(small))
        slope = w * (jnp.where(m >= 0.0, 1.0, small) / (1.0 + small))
        ratio = jnp.sum(slope, axis=0, keepdims=True) / dist_pos
        pt = slope * inv - jnp.where(sub == lane, ratio, 0.0)
        pa = pt.T
        sum_a = jnp.sum(pt, axis=0, keepdims=True)
        edge_rows[1:2, seg(i)] = sum_a
        edge_rows[2:3, seg(i)] = jnp.sum(pa, axis=0, keepdims=True)
        own_h, own_l = halves(jnp.where(sub == lane, -sum_a, 0.0))
        pa_h, pa_l = halves(pa)
        form[pair(i), 0:SEG] = jnp.concatenate([pa_h, pa_l], axis=0)
        form[pair(i), SEG:] = jnp.concatenate([own_h, own_l], axis=0)
    loss = jnp.sum(loss)

    for i in range(segs):
        hots = jnp.concatenate([hot_t[seg(i), :], hot_h[seg(i), :]], axis=0)
        y = mm(form[pair(i), :], hots)
        y_h[seg(i), :], y_l[seg(i), :] = halves(y[0:SEG] + y[SEG:])
    crossed = mm(hotx[...], y_h[...]) + mm(hotx[...], y_l[...])
    form_re = crossed[ke:]
    own_e = jnp.zeros((ke, LANE), F32)
    own_r = jnp.zeros((kr, LANE), F32)
    for i in range(segs):
        sum_a = edge_rows[1:2, seg(i)]
        sum_t = edge_rows[2:3, seg(i)]
        own_e += hotx[0:ke, seg(i)].astype(F32) * sum_a - hott[:, seg(i)].astype(F32) * sum_t
        own_r -= hotx[ke:, seg(i)].astype(F32) * sum_a
    own_e = jnp.sum(own_e, axis=1, keepdims=True)
    own_r = jnp.sum(own_r, axis=1, keepdims=True)
    diagonal = iota((ke, ke), 0) == iota((ke, ke), 1)
    form_ee = crossed[0:ke] + crossed[0:ke].T + jnp.where(diagonal, own_e, 0.0)

    ee_h, ee_l = halves(form_ee)
    re_h, re_l = halves(form_re)
    er_h, er_l = halves(form_re.T)
    rows_e[...] = (
        mm(ee_h, eh[...])
        + (mm(ee_h, el[...]) + mm(ee_l, eh[...]))
        + (mm(jnp.concatenate([er_h, er_h], axis=1), rr[...]) + mm(er_l, rr[0:kr, :]))
    )
    rows_r[...] = (
        mm(re_h, eh[...])
        + (mm(re_h, el[...]) + mm(re_l, eh[...]))
        + own_r * (rr[0:kr, :].astype(F32) + rr[kr : 2 * kr, :].astype(F32))
    )
    at_loss = copies * rest - 2
    extra = jnp.where(lane8 == at_loss, loss, jnp.where(lane8 == at_loss + 1, pairs, 0.0))

    def grad_copy(k):
        peer = shard_at(k)
        return pltpu.make_async_remote_copy(
            src_ref=send_buf.at[peer],
            dst_ref=gbuf.at[g, s],
            send_sem=g_send.at[k],
            recv_sem=g_recv.at[g, s],
            device_id={"shard": peer},
        )

    def block_copy(grp, src, to, send_sem):
        return pltpu.make_async_remote_copy(
            src_ref=gbuf.at[grp, src],
            dst_ref=gbuf.at[grp, src],
            send_sem=send_sem,
            recv_sem=g_recv.at[grp, src],
            device_id={"grp": to},
        )

    def arrived(grp, src):
        block_copy(grp, src, mate, core_send.at[0, 0]).wait_recv()

    for k in order:
        fetch_copy(k).wait_send()
    for r in range(ns):
        pack(r, True, extra)
    for k in near:
        grad_copy(k).start()
    gbuf[g, s] = send_buf[s]

    def group_up(dy):
        return lax.rem(g + 2 * dy, ng)

    def group_down(dy):
        return lax.rem(g + ng - 2 * dy, ng)

    def forward(src):
        out = [block_copy(g, src, group_up(dy), y_send.at[dy - 1, src]) for dy in range(1, ny)]
        return out + [block_copy(g, src, mate, core_send.at[0, src])]

    def hand_over(dy, src):
        return block_copy(group_down(dy), src, mate, core_send.at[dy, src])

    sequence = [0] + near
    lag = 4
    handed = [0]

    def hand_over_to(end):
        end = max(end, handed[0])
        for k in sequence[handed[0] : end]:
            for dy in range(1, ny):
                arrived(group_down(dy), shard_at(k))
                hand_over(dy, shard_at(k)).start()
        handed[0] = end

    def hand_over_last():
        for dy in range(1, ny):
            arrived(group_down(dy), shard_at(sequence[-1]))
            hand_over(dy, shard_at(sequence[-1])).start()

    def add_batch(n):
        groups, core, start = batches[n]

        @pl.when(parity != core)
        def _():
            for k in range(start, start + part):
                for grp in groups:
                    arrived(grp, shard_at(k))

        if not early:
            batch_one_hots(n)
        at = n if early else 0
        blocks = [(grp, shard_at(k)) for grp in groups for k in range(start, start + part)]
        ends = [last_columns(gbuf[grp, src, chunks * cap : chunks * cap + 8, :]) for grp, src in blocks]
        for c in range(chunks + 1):
            size = LANE if c < chunks else rest
            put = slice(c * LANE, c * LANE + size)
            if c < chunks:
                e = [gbuf[grp, src, c * cap : c * cap + CAP_E, :] for grp, src in blocks]
                r = [gbuf[grp, src, c * cap + CAP_E : (c + 1) * cap, :] for grp, src in blocks]
            else:
                e, r = [x[0] for x in ends], [x[1] for x in ends]
            hi, lo = halves(jnp.concatenate(e, axis=0).T[0:size, :])
            sgt_e[put, 0:ke] = hi
            sgt_e[put, ke : 2 * ke] = lo
            hi, lo = halves(jnp.concatenate(r, axis=0).T[0:size, :])
            sgt_r[put, 0:kr] = hi
            sgt_r[put, kr : 2 * kr] = lo
        part_e = mm(sgt_e[:, 0:ke], oh_e[at]) + mm(sgt_e[:, ke : 2 * ke], oh_e[at])
        part_r = mm(sgt_r[...], oh_r[at])
        if n:
            ge_ref[...] += part_e
            gr_ref[...] += part_r[:, 0:nr]
        else:
            ge_ref[...] = part_e
            gr_ref[...] = part_r[:, 0:nr]

    def drain_sends(ks):
        for k in ks:
            for copy in forward(shard_at(k)):
                copy.wait_send()
            for dy in range(1, ny):
                hand_over(dy, shard_at(k)).wait_send()

    def pass_on(idx):
        k = sequence[idx]
        if k:
            arrived(g, shard_at(k))
        for copy in forward(shard_at(k)):
            copy.start()

    for idx in range(ns):
        pass_on(idx)
        hand_over_to(idx + 1 - lag)
    for copy in local[7:]:
        copy.wait()
    for k in near:
        ids_copy(k).wait_send()
        grad_copy(k).wait_send()
    for k in range(1, ng):
        idg_copy(k).wait_send()
    quarter = len(batches) // 4
    for n in range(quarter):
        add_batch(n)
    hand_over_to(ns - 1)

    @pl.when(parity == 0)
    def _():
        hand_over_last()

    for n in range(quarter, 2 * quarter):
        add_batch(n)

    @pl.when(parity == 1)
    def _():
        hand_over_last()

    drain_sends(sequence[:-2])
    for n in range(2 * quarter, 4 * quarter):
        add_batch(n)

    def stat(i, total):
        for r in range(ns):
            total += gbuf[i, r, chunks * cap : chunks * cap + 8, :]
        return total

    stat_ref[...] = lax.fori_loop(0, ng, stat, jnp.zeros((8, LANE), F32))

    drain_sends(sequence[-2:])


def adamw_kernel(
    at_loss,
    strip,
    stat_ref,
    ge_ref,
    gr_ref,
    w_e,
    one_e,
    two_e,
    w_r,
    one_r,
    two_r,
    e_new,
    e_one,
    e_two,
    e_low,
    r_new,
    r_one,
    r_two,
    r_low,
    loss_ref,
    pairs_ref,
    *scratch,
):
    d = ge_ref.shape[0]
    sems = scratch[-1]
    total = stat_ref[0:1, :]
    sums = [
        pltpu.make_async_copy(buf, out, sems.at[n, 0])
        for n, (buf, out) in enumerate(zip(scratch[8:10], (loss_ref, pairs_ref)), 8)
    ]
    for n, copy in enumerate(sums):
        scratch[8 + n][0] = total[0, at_loss + n]
        copy.start()
    factor = ((1.0 - BETA_ONE) / total)[0, at_loss + 1]
    square = (1.0 - BETA_TWO) / (1.0 - BETA_ONE) ** 2
    fix_two = 1.0 / (1.0 - BETA_TWO**STEP)
    rate = RATE / (1.0 - BETA_ONE**STEP)
    tables = (
        (ge_ref, w_e, one_e, two_e, (e_new, e_one, e_two, e_low), scratch[0:4]),
        (gr_ref, w_r, one_r, two_r, (r_new, r_one, r_two, r_low), scratch[4:8]),
    )

    def copies(i):
        at = pl.ds(pl.multiple_of(i * strip, strip), strip)
        out = []
        for n, (_, _, _, _, outs, bufs) in enumerate(tables):
            for m, (hbm, buf) in enumerate(zip(outs, bufs)):
                out.append(pltpu.make_async_copy(buf.at[at, :], hbm.at[at, :], sems.at[n * 4 + m, i]))
        return out

    def step(i, _):
        for g_ref, w_ref, one_ref, two_ref, _, bufs in tables:

            def rows(j, _):
                at = pl.ds(pl.multiple_of(i * strip, 16), strip)
                gradient = g_ref[at, :] * factor
                weight = w_ref[at, :]
                one = BETA_ONE * one_ref[at, :] + gradient
                two = BETA_TWO * two_ref[at, :] + square * gradient * gradient
                scaled = two * fix_two
                root = scaled * lax.rsqrt(scaled) + EPS_ADAM
                new = weight * (1.0 - RATE * DECAY) - rate * one / root
                bufs[0][at, :] = new
                bufs[1][at, :] = one
                bufs[2][at, :] = two
                bufs[3][at, :] = new.astype(BF16)
                return 0

            rows(0, 0)
        for copy in copies(i):
            copy.start()
        return 0

    steps = d // strip
    lax.fori_loop(0, steps, step, 0)
    for i in range(steps):
        for copy in copies(i):
            copy.wait()
    for copy in sums:
        copy.wait()


def per_device(
    ns,
    ng,
    entity_rows,
    entity_first,
    entity_second,
    relation_rows,
    relation_first,
    relation_second,
    requests,
    head_slots,
    relation_slots,
    tail_slots,
    neg_offsets,
    valid_counts,
):
    ne, d = entity_rows.shape
    nr = relation_rows.shape[0]
    cap = requests.shape[2]
    cap_r = cap - CAP_E
    edges, neg = neg_offsets.shape
    segs = edges // SEG
    ke, kr = ns * CAP_E, ns * cap_r
    chunks = d // LANE
    rest = d - chunks * LANE
    dp = (chunks + 1) * LANE
    nrp = up(nr, LANE)
    ny = ng // 2
    block = (LANE, LANE)
    any_space = pl.BlockSpec(memory_space=pl.ANY)
    vmem = pl.BlockSpec(memory_space=pltpu.VMEM)
    smem = pl.BlockSpec(memory_space=pltpu.SMEM)
    dma = pltpu.SemaphoreType.DMA
    hbm = functools.partial(pltpu.with_memory_space_constraint, memory_space=pltpu.HBM)
    batches = ng if ng <= 4 else 1
    scratch = [
        pltpu.VMEM((ns, cap), I32),
        pltpu.VMEM((3, segs, SEG), I32),
        pltpu.VMEM((neg, edges), I32),
        pltpu.VMEM((dp, ne), BF16),
        pltpu.VMEM((dp, ne), BF16),
        pltpu.VMEM((dp, nrp), BF16),
        pltpu.VMEM((dp, nrp), BF16),
        pltpu.VMEM((ns, ns, cap), I32),
        pltpu.VMEM((ng, ns, cap), I32),
        pltpu.VMEM((ns, *block), F32),
        pltpu.VMEM((ns, *block), F32),
        pltpu.VMEM((ke, dp), F32),
        pltpu.VMEM((kr, dp), F32),
        pltpu.VMEM((batches, ke, ne), BF16),
        pltpu.VMEM((batches, 2 * kr, nrp), BF16),
        pltpu.VMEM((edges, ke), BF16),
        pltpu.VMEM((edges, ke), BF16),
        pltpu.VMEM((edges, 2 * kr), BF16),
        pltpu.VMEM((ke + kr, edges), BF16),
        pltpu.VMEM((ke, edges), BF16),
        pltpu.VMEM((segs, SEG, SEG), F32),
        pltpu.VMEM((ke, dp), BF16),
        pltpu.VMEM((ke, dp), BF16),
        pltpu.VMEM((2 * kr, dp), BF16),
        pltpu.VMEM((2 * edges, dp), BF16),
        pltpu.VMEM((2 * edges, dp), BF16),
        pltpu.VMEM((3, segs, SEG, SEG), F32),
        pltpu.VMEM((segs, SEG, SEG), F32),
        pltpu.VMEM((8, edges), F32),
        pltpu.VMEM((2 * edges, 2 * SEG), BF16),
        pltpu.VMEM((edges, ke), BF16),
        pltpu.VMEM((edges, ke), BF16),
        pltpu.VMEM((ng, ns, *block), F32),
        pltpu.VMEM((d, 2 * ke), BF16),
        pltpu.VMEM((d, 2 * kr), BF16),
        dma((11,)),
        dma((ns,)),
        dma((ns,)),
        dma((ng,)),
        dma((ng,)),
        dma((ns,)),
        dma((ns,)),
        dma((ns,)),
        dma((ng, ns)),
        dma((ny, ns)),
        dma((max(ny - 1, 1), ns)),
        pltpu.SemaphoreType.REGULAR,
    ]
    small = [
        requests[0],
        head_slots.reshape(segs, SEG),
        relation_slots.reshape(segs, SEG),
        tail_slots.reshape(segs, SEG),
        neg_offsets.T,
    ]
    rows = [entity_rows.T, relation_rows.T]
    moments = [entity_first.T, entity_second.T, relation_first.T, relation_second.T]
    sums = [pltpu.VMEM((d, ne), F32), pltpu.VMEM((d, nr), F32), pltpu.VMEM((8, LANE), F32)]
    held_rows = [pltpu.VMEM(x.shape, F32) for x in rows]
    held_moments = [pltpu.VMEM(x.shape, F32) for x in moments]
    need = sum(padded(x) for x in scratch[: scratch.index(dma((11,)))]) + (2 << 20)
    keep = need + sum(padded(x) for x in sums + held_rows + held_moments) < (62 << 20)
    if keep:
        outs, held = sums + held_rows + held_moments, []
    else:
        outs, held = sums, held_rows
        need += sum(padded(x) for x in held)
    operands = small + rows + (moments if keep else [])
    ge, gr, stat, *passed = pl.pallas_call(
        functools.partial(exchange_kernel, ns, ng, (d, ne, nr, cap, edges, neg), int(keep), batches > 1),
        out_shape=outs,
        in_specs=[smem] + [any_space] * len(operands),
        out_specs=[vmem] * len(outs),
        scratch_shapes=held + scratch,
        compiler_params=pltpu.CompilerParams(
            collective_id=0, has_side_effects=True, vmem_limit_bytes=need
        ),
    )(valid_counts, *[hbm(x) for x in operands])
    if not keep:
        passed = rows + moments
    w_e, w_r, one_e, two_e, one_r, two_r = passed
    tables = (w_e, one_e, two_e, w_r, one_r, two_r)
    at_loss = LANE // rest * rest - 2
    strip = 80
    shapes = [(jax.ShapeDtypeStruct((d, n), t)) for n in (ne, nr) for t in (F32, F32, F32, BF16)]
    one = jax.ShapeDtypeStruct((1,), F32)
    *outs, loss, pairs = pl.pallas_call(
        functools.partial(adamw_kernel, at_loss, strip),
        out_shape=shapes + [one, one],
        in_specs=[vmem] * 9,
        out_specs=[any_space] * 10,
        scratch_shapes=[pltpu.VMEM(x.shape, x.dtype) for x in shapes] + [pltpu.SMEM((1,), F32)] * 2 + [dma((10, d // strip))],
        compiler_params=pltpu.CompilerParams(vmem_limit_bytes=32 * 1024 * 1024),
    )(stat, ge, gr, *tables)
    e_new, e_one, e_two, e_low, r_new, r_one, r_two, r_low = (x.T for x in outs)
    return (e_new, e_one, e_two, r_new, r_one, r_two, e_low, r_low, loss, pairs)


def solution(mesh):
    rows = P("shard", None)
    both = ("grp", "shard")
    return jax.shard_map(
        functools.partial(per_device, mesh.shape["shard"], mesh.shape["grp"]),
        mesh=mesh,
        in_specs=(
            rows,
            rows,
            rows,
            rows,
            rows,
            rows,
            P(both, None, None),
            P(both),
            P(both),
            P(both),
            P(both, None),
            P(both),
        ),
        out_specs=(rows,) * 8 + (P(), P()),
        check_vma=False,
    )
```

```python
import functools
import math

import jax
import jax.numpy as jnp
from jax import lax
from jax.experimental import pallas as pl
from jax.experimental.pallas import tpu as pltpu
from jax.sharding import PartitionSpec as P

CAP_E = 32
SEG = 128
STEP = 10
LANE = 128

MARGIN = 0.1
EPS_DIST = 1e-06
BETA_ONE = 0.9
BETA_TWO = 0.999
RATE = 0.5
DECAY = 0.01
EPS_ADAM = 1e-08

F32 = jnp.float32
BF16 = jnp.bfloat16
I32 = jnp.int32


def mm(a, b):
    return lax.dot_general(a, b, (((1,), (0,)), ((), ())), preferred_element_type=F32)


def mm_nt(a, b):
    return lax.dot_general(a, b, (((1,), (1,)), ((), ())), preferred_element_type=F32)


def halves(x):
    hi = x.astype(BF16)
    return hi, (x - hi.astype(F32)).astype(BF16)


def up(n, m):
    return (n + m - 1) // m * m


def iota(shape, axis):
    return lax.broadcasted_iota(I32, shape, axis)


def padded(ref):
    *lead, rows, cols = ref.shape
    size = jnp.dtype(ref.dtype).itemsize
    return math.prod(lead) * up(rows, 32 // size) * up(cols, LANE) * size


def exchange_kernel(
    ns,
    ng,
    dims,
    keep,
    early,
    valid_ref,
    req_hbm,
    head_hbm,
    rslot_hbm,
    tail_hbm,
    neg_hbm,
    ent_hbm,
    rel_hbm,
    *refs,
):
    rest_hbm, refs = refs[: 4 * keep], refs[4 * keep :]
    ge_ref, gr_ref, stat_ref, ent_v, rel_v, *refs = refs
    rest_v, refs = refs[: 4 * keep], refs[4 * keep :]
    exchange(ns, ng, dims, early, valid_ref, (req_hbm, head_hbm, rslot_hbm, tail_hbm, neg_hbm), (ent_hbm, rel_hbm, *rest_hbm), ge_ref, gr_ref, stat_ref, (ent_v, rel_v, *rest_v), *refs)


def exchange(
    ns,
    ng,
    dims,
    early,
    valid_ref,
    small_hbm,
    tables_hbm,
    ge_ref,
    gr_ref,
    stat_ref,
    tables,
    req_v,
    slots_v,
    neg_v,
    eth,
    etl,
    rth,
    rtl,
    ids_all,
    idg,
    send_buf,
    recv_buf,
    rows_e,
    rows_r,
    oh_e,
    oh_r,
    hot_h,
    hot_t,
    hot_r,
    hotx,
    hott,
    wt,
    eh,
    el,
    rr,
    targets,
    anchors,
    folds,
    squares,
    edge_rows,
    form,
    y_h,
    y_l,
    gbuf,
    sgt_e,
    sgt_r,
    local_sem,
    ids_send,
    ids_recv,
    idg_send,
    idg_recv,
    f_send,
    f_recv,
    g_send,
    g_recv,
    core_send,
    y_send,
    turn_sem,
):
    d, ne, nr, cap, edges, neg = dims
    ent_v, rel_v = tables[:2]
    req_hbm, head_hbm, rslot_hbm, tail_hbm, neg_hbm = small_hbm
    ent_hbm, rel_hbm = tables_hbm[:2]
    cap_r = cap - CAP_E
    ke, kr = ns * CAP_E, ns * cap_r
    chunks = d // LANE
    rest = d - chunks * LANE
    dp = (chunks + 1) * LANE
    nrp = up(nr, LANE)
    segs = edges // SEG
    copies = LANE // rest
    subs = cap // 8
    ny = ng // 2

    g = lax.axis_index("grp")
    s = lax.axis_index("shard")
    parity = lax.rem(g, 2)
    mate = g + 1 - 2 * parity
    near = list(range(1, ns))
    order = near

    def shard_at(k):
        partner, bit = s, 1
        while bit < ns:
            if k & bit:
                partner = partner + bit * (1 - 2 * lax.rem(s // bit, 2))
            bit *= 2
        return partner

    shard_from = shard_at

    barrier = pltpu.get_barrier_semaphore()
    for k in range(1, ns):
        pl.semaphore_signal(barrier, inc=1, device_id={"shard": shard_at(k)})
    for k in range(1, ng):
        pl.semaphore_signal(barrier, inc=1, device_id={"grp": lax.rem(g + k, ng)})

    local = [
        pltpu.make_async_copy(src, dst, local_sem.at[i])
        for i, (src, dst) in enumerate(
            [
                (req_hbm, req_v),
                (ent_hbm, ent_v),
                (rel_hbm, rel_v),
                (head_hbm, slots_v.at[0]),
                (rslot_hbm, slots_v.at[1]),
                (tail_hbm, slots_v.at[2]),
                (neg_hbm, neg_v),
                *zip(tables_hbm[2:], tables[2:]),
            ]
        )
    ]
    for copy in local[:7]:
        copy.start()
    local[0].wait()
    pl.semaphore_wait(barrier, ns - 1 + ng - 1)

    def ids_copy(k):
        return pltpu.make_async_remote_copy(
            src_ref=req_v,
            dst_ref=ids_all.at[s],
            send_sem=ids_send.at[k],
            recv_sem=ids_recv.at[s],
            device_id={"shard": shard_at(k)},
        )

    def ids_arrival(k):
        return pltpu.make_async_remote_copy(
            src_ref=req_v,
            dst_ref=ids_all.at[shard_from(k)],
            send_sem=ids_send.at[k],
            recv_sem=ids_recv.at[shard_from(k)],
            device_id={"shard": shard_from(k)},
        )

    for k in order:
        ids_copy(k).start()
    ids_all[s] = req_v[...]

    local[1].wait()
    local[2].wait()

    for start in range(0, d, 80):
        at = slice(start, start + 80)
        eth[at, :], etl[at, :] = halves(ent_v[at, :])
        rth[at, 0:nr], rtl[at, 0:nr] = halves(rel_v[at, :])
    if nrp > nr:
        rth[:, nr:nrp] = jnp.zeros((dp, nrp - nr), BF16)
        rtl[:, nr:nrp] = jnp.zeros((dp, nrp - nr), BF16)
    for table in (eth, etl, rth, rtl):
        tail_rows = table[chunks * LANE : d, :]
        for c in range(1, copies):
            table[chunks * LANE + c * rest : chunks * LANE + (c + 1) * rest, :] = tail_rows

    for k in order:
        ids_arrival(k).wait_recv()
    for r in range(ns):
        idg[g, r : r + 1, :] = ids_all[r, pl.ds(s, 1), :]

    def idg_copy(k):
        return pltpu.make_async_remote_copy(
            src_ref=idg.at[g],
            dst_ref=idg.at[g],
            send_sem=idg_send.at[k],
            recv_sem=idg_recv.at[g],
            device_id={"grp": lax.rem(g + k, ng)},
        )

    def idg_arrival(k):
        other = lax.rem(g + ng - k, ng)
        return pltpu.make_async_remote_copy(
            src_ref=idg.at[other],
            dst_ref=idg.at[other],
            send_sem=idg_send.at[k],
            recv_sem=idg_recv.at[other],
            device_id={"grp": other},
        )

    lanes_e = iota((CAP_E, ne), 1).astype(F32)
    lanes_r = iota((cap_r, nrp), 1).astype(F32) + float(ne)

    def one_hots(at, blocks, columns):
        pieces = []
        for n, (grp, src) in enumerate(blocks):
            column = columns[grp][:, src : src + 1]
            hit = jnp.where(column[0:CAP_E] == lanes_e, 1.0, 0.0).astype(BF16)
            oh_e[at, n * CAP_E : (n + 1) * CAP_E, :] = hit
            pieces.append(jnp.where(column[CAP_E:cap] == lanes_r, 1.0, 0.0))
        hit = jnp.concatenate(pieces, axis=0).astype(BF16)
        oh_r[at, 0:kr, :] = hit
        oh_r[at, kr : 2 * kr, :] = hit

    def columns_of(grp):
        wide = jnp.concatenate([idg[grp].astype(F32), jnp.zeros((ns, LANE - cap), F32)], axis=1)
        return jnp.concatenate([wide, jnp.zeros((LANE - ns, LANE), F32)], axis=0).T

    one_hots(0, [(0, src) for src in range(ns)], [columns_of(g)])
    rows_e[...] = mm_nt(oh_e[0], eth[...]) + mm_nt(oh_e[0], etl[...])
    rows_r[...] = mm_nt(oh_r[0, 0:kr], rth[...]) + mm_nt(oh_r[0, 0:kr], rtl[...])

    lane8 = iota((8, LANE), 1)

    def pack(r, roll, extra):
        for c in range(chunks):
            at = slice(c * LANE, (c + 1) * LANE)
            send_buf[r, c * cap : c * cap + CAP_E, :] = rows_e[r * CAP_E : (r + 1) * CAP_E, at]
            send_buf[r, c * cap + CAP_E : (c + 1) * cap, :] = rows_r[r * cap_r : (r + 1) * cap_r, at]
        last = slice(chunks * LANE, dp)
        out = extra
        for j in range(subs):
            if j * 8 < CAP_E:
                piece = rows_e[r * CAP_E + j * 8 : r * CAP_E + j * 8 + 8, last]
            else:
                piece = rows_r[r * cap_r + j * 8 - CAP_E : r * cap_r + j * 8 - CAP_E + 8, last]
            if roll and j:
                piece = pltpu.roll(piece, j * rest, 1)
            out = jnp.where((lane8 >= j * rest) & (lane8 < (j + 1) * rest), piece, out)
        send_buf[r, chunks * cap : chunks * cap + 8, :] = out

    def last_columns(tile):
        pieces = []
        for j in range(subs):
            piece = pltpu.roll(tile, LANE - j * rest, 1) if j else tile
            pieces.append(jnp.where(lane8 < rest, piece, 0.0))
        return jnp.concatenate(pieces[: CAP_E // 8], axis=0), jnp.concatenate(pieces[CAP_E // 8 :], axis=0)

    def fetch_copy(k):
        peer = shard_at(k)
        return pltpu.make_async_remote_copy(
            src_ref=send_buf.at[peer],
            dst_ref=recv_buf.at[s],
            send_sem=f_send.at[k],
            recv_sem=f_recv.at[s],
            device_id={"shard": peer},
        )

    def fetch_arrival(k):
        peer = shard_from(k)
        return pltpu.make_async_remote_copy(
            src_ref=send_buf.at[peer],
            dst_ref=recv_buf.at[peer],
            send_sem=f_send.at[k],
            recv_sem=f_recv.at[peer],
            device_id={"shard": peer},
        )

    for r in range(ns):
        pack(r, False, jnp.zeros((8, LANE), F32))
    @pl.when(parity == 0)
    def _():
        for k in order:
            fetch_copy(k).start()

    recv_buf[s] = send_buf[s]
    for k in range(1, ng):
        idg_copy(k).start()
    for copy in local[7:]:
        copy.start()

    for copy in local[3:7]:
        copy.wait()
    slots = slots_v[...]
    owner = lax.shift_right_logical(slots * ((1 << 16) // cap + 1), 16)
    within = slots - owner * cap
    head_k = owner[0] * CAP_E + within[0]
    rel_k = owner[1] * cap_r + within[1] - CAP_E
    tail_k = owner[2] * CAP_E + within[2]
    for i in range(segs):
        at = slice(i * SEG, (i + 1) * SEG)
        head_row, rel_row, tail_row = (v[i : i + 1, :] for v in (head_k, rel_k, tail_k))
        hotx[0:ke, at] = jnp.where(iota((ke, SEG), 0) == head_row, 1.0, 0.0).astype(BF16)
        hott[:, at] = jnp.where(iota((ke, SEG), 0) == tail_row, 1.0, 0.0).astype(BF16)
        hotx[ke:, at] = jnp.where(iota((kr, SEG), 0) == rel_row, 1.0, 0.0).astype(BF16)
        head_col, rel_col, tail_col = (
            jnp.broadcast_to(v.astype(F32), (SEG, SEG)).T[:, 0:1] for v in (head_row, rel_row, tail_row)
        )
        slots_e = iota((SEG, ke), 1).astype(F32)
        slots_r = iota((SEG, kr), 1).astype(F32)
        hot_h[at, :] = jnp.where(slots_e == head_col, 1.0, 0.0).astype(BF16)
        hot_t[at, :] = jnp.where(slots_e == tail_col, 1.0, 0.0).astype(BF16)
        hit = jnp.where(slots_r == rel_col, 1.0, 0.0)
        hot_r[at, :] = jnp.concatenate([hit, hit], axis=1).astype(BF16)

    part = ns // 2
    batches = [
        ((core + 4 * pair_of, core + 4 * pair_of + 2), core, b * part)
        for core in range(2)
        for b in range(2)
        for pair_of in range(ny // 2)
    ]

    def batch_one_hots(n):
        groups, _, start = batches[n]
        columns = []
        for grp in groups:
            wide = jnp.concatenate([idg[grp, pl.ds(shard_at(k), 1), :].astype(F32) for k in range(start, start + part)], axis=0)
            wide = jnp.concatenate([wide, jnp.zeros((part, LANE - cap), F32)], axis=1)
            columns.append(jnp.concatenate([wide, jnp.zeros((LANE - part, LANE), F32)], axis=0).T)
        one_hots(n if early else 0, [(c, k) for c in range(2) for k in range(part)], columns)

    for k in range(1, ng):
        idg_arrival(k).wait_recv()
    if early:
        for n in range(len(batches)):
            batch_one_hots(n)

    valid = valid_ref[0]
    sub = iota((SEG, SEG), 0)
    lane = iota((SEG, SEG), 1)

    def count(i, total):
        start = pl.multiple_of(i * SEG, SEG)
        hits = jnp.zeros((SEG, SEG), F32)
        for k in range(neg):
            hits += jnp.where(neg_v[k : k + 1, pl.ds(start, SEG)] == sub, 1.0, 0.0)
        keep = (lane + start < valid) & (sub + start < valid) & (sub != lane)
        hits = jnp.where(keep, hits, 0.0)
        wt[i] = hits
        return total + hits

    pairs = jnp.sum(lax.fori_loop(0, segs, count, jnp.zeros((SEG, SEG), F32)))

    most = 4

    @pl.when(parity == 0)
    def _():
        for k in order[:most]:
            fetch_arrival(k).wait_recv()
        pl.semaphore_signal(turn_sem, inc=1, device_id={"grp": mate})
        for k in order[most:]:
            fetch_arrival(k).wait_recv()

    @pl.when(parity == 1)
    def _():
        pl.semaphore_wait(turn_sem, 1)
        for k in order:
            fetch_copy(k).start()
        for k in order:
            fetch_arrival(k).wait_recv()

    for p in range(ns):
        ends_e, ends_r = last_columns(recv_buf[p, chunks * cap : chunks * cap + 8, :])
        e = jnp.concatenate(
            [recv_buf[p, c * cap : c * cap + CAP_E, :] for c in range(chunks)] + [ends_e], axis=1
        )
        r = jnp.concatenate(
            [recv_buf[p, c * cap + CAP_E : (c + 1) * cap, :] for c in range(chunks)] + [ends_r], axis=1
        )
        at = slice(p * CAP_E, (p + 1) * CAP_E)
        eh[at, :], el[at, :] = halves(e)
        rows_r[p * cap_r : (p + 1) * cap_r, :] = r
    hi, lo = halves(rows_r[...])
    rr[0:kr, :] = hi
    rr[kr : 2 * kr, :] = lo

    def lane_fold(x):
        out = x[:, 0:LANE]
        for c in range(1, dp // LANE):
            out += x[:, c * LANE : (c + 1) * LANE]
        return out

    def seg(i):
        return slice(i * SEG, (i + 1) * SEG)

    def pair(i):
        return slice(2 * i * SEG, 2 * (i + 1) * SEG)

    for i in range(segs):
        hots = jnp.concatenate([hot_h[seg(i), :], hot_t[seg(i), :]], axis=0)
        both_h = mm(hots, eh[...])
        both_l = mm(hots, el[...])
        a = both_h[0:SEG] + both_l[0:SEG] + mm(hot_r[seg(i), :], rr[...])
        t = both_h[SEG:] + both_l[SEG:]
        targets[pair(i), :] = jnp.concatenate([both_h[SEG:].astype(BF16), both_l[SEG:].astype(BF16)], axis=0)
        anchors[pair(i), :] = jnp.concatenate(halves(a), axis=0)
        offset = a - t
        folds[0, i] = lane_fold(offset * offset)
        folds[1, i] = lane_fold(a * a)
        folds[2, i] = lane_fold(t * t)

    for i in range(segs):
        terms = mm_nt(targets[pair(i), :], anchors[pair(i), :])
        gram = terms[0:SEG, 0:SEG] + (terms[0:SEG, SEG:] + terms[SEG:, 0:SEG] + terms[SEG:, SEG:])
        square_pos = jnp.sum(folds[0, i].T, axis=0, keepdims=True)
        edge_rows[0:1, seg(i)] = jnp.sqrt(square_pos + EPS_DIST)
        anchor_sq = jnp.sum(folds[1, i].T, axis=0, keepdims=True)
        target_sq = jnp.sum(folds[2, i], axis=1, keepdims=True)
        squares[i] = anchor_sq + target_sq - 2.0 * gram

    loss = jnp.zeros((SEG, SEG), F32)
    for i in range(segs):
        square = jnp.maximum(squares[i], 0.0) + EPS_DIST
        dist_pos = edge_rows[0:1, seg(i)]
        inv = lax.rsqrt(square)
        m = MARGIN + dist_pos - square * inv
        w = wt[i]
        small = jnp.exp(-jnp.abs(m))
        loss += w * (jnp.maximum(m, 0.0) + jnp.log1p(small))
        slope = w * (jnp.where(m >= 0.0, 1.0, small) / (1.0 + small))
        ratio = jnp.sum(slope, axis=0, keepdims=True) / dist_pos
        pt = slope * inv - jnp.where(sub == lane, ratio, 0.0)
        pa = pt.T
        sum_a = jnp.sum(pt, axis=0, keepdims=True)
        edge_rows[1:2, seg(i)] = sum_a
        edge_rows[2:3, seg(i)] = jnp.sum(pa, axis=0, keepdims=True)
        own_h, own_l = halves(jnp.where(sub == lane, -sum_a, 0.0))
        pa_h, pa_l = halves(pa)
        form[pair(i), 0:SEG] = jnp.concatenate([pa_h, pa_l], axis=0)
        form[pair(i), SEG:] = jnp.concatenate([own_h, own_l], axis=0)
    loss = jnp.sum(loss)

    for i in range(segs):
        hots = jnp.concatenate([hot_t[seg(i), :], hot_h[seg(i), :]], axis=0)
        y = mm(form[pair(i), :], hots)
        y_h[seg(i), :], y_l[seg(i), :] = halves(y[0:SEG] + y[SEG:])
    crossed = mm(hotx[...], y_h[...]) + mm(hotx[...], y_l[...])
    form_re = crossed[ke:]
    own_e = jnp.zeros((ke, LANE), F32)
    own_r = jnp.zeros((kr, LANE), F32)
    for i in range(segs):
        sum_a = edge_rows[1:2, seg(i)]
        sum_t = edge_rows[2:3, seg(i)]
        own_e += hotx[0:ke, seg(i)].astype(F32) * sum_a - hott[:, seg(i)].astype(F32) * sum_t
        own_r -= hotx[ke:, seg(i)].astype(F32) * sum_a
    own_e = jnp.sum(own_e, axis=1, keepdims=True)
    own_r = jnp.sum(own_r, axis=1, keepdims=True)
    diagonal = iota((ke, ke), 0) == iota((ke, ke), 1)
    form_ee = crossed[0:ke] + crossed[0:ke].T + jnp.where(diagonal, own_e, 0.0)

    ee_h, ee_l = halves(form_ee)
    re_h, re_l = halves(form_re)
    er_h, er_l = halves(form_re.T)
    rows_e[...] = (
        mm(ee_h, eh[...])
        + (mm(ee_h, el[...]) + mm(ee_l, eh[...]))
        + (mm(jnp.concatenate([er_h, er_h], axis=1), rr[...]) + mm(er_l, rr[0:kr, :]))
    )
    rows_r[...] = (
        mm(re_h, eh[...])
        + (mm(re_h, el[...]) + mm(re_l, eh[...]))
        + own_r * (rr[0:kr, :].astype(F32) + rr[kr : 2 * kr, :].astype(F32))
    )
    at_loss = copies * rest - 2
    extra = jnp.where(lane8 == at_loss, loss, jnp.where(lane8 == at_loss + 1, pairs, 0.0))

    def grad_copy(k):
        peer = shard_at(k)
        return pltpu.make_async_remote_copy(
            src_ref=send_buf.at[peer],
            dst_ref=gbuf.at[g, s],
            send_sem=g_send.at[k],
            recv_sem=g_recv.at[g, s],
            device_id={"shard": peer},
        )

    def block_copy(grp, src, to, send_sem):
        return pltpu.make_async_remote_copy(
            src_ref=gbuf.at[grp, src],
            dst_ref=gbuf.at[grp, src],
            send_sem=send_sem,
            recv_sem=g_recv.at[grp, src],
            device_id={"grp": to},
        )

    def arrived(grp, src):
        block_copy(grp, src, mate, core_send.at[0, 0]).wait_recv()

    for k in order:
        fetch_copy(k).wait_send()
    for r in range(ns):
        pack(r, True, extra)
    for k in near:
        grad_copy(k).start()
    gbuf[g, s] = send_buf[s]

    def group_up(dy):
        return lax.rem(g + 2 * dy, ng)

    def group_down(dy):
        return lax.rem(g + ng - 2 * dy, ng)

    def forward(src):
        out = [block_copy(g, src, group_up(dy), y_send.at[dy - 1, src]) for dy in range(1, ny)]
        return out + [block_copy(g, src, mate, core_send.at[0, src])]

    def hand_over(dy, src):
        return block_copy(group_down(dy), src, mate, core_send.at[dy, src])

    sequence = [0] + near
    lag = 4
    handed = [0]

    def hand_over_to(end):
        end = max(end, handed[0])
        for k in sequence[handed[0] : end]:
            for dy in range(1, ny):
                arrived(group_down(dy), shard_at(k))
                hand_over(dy, shard_at(k)).start()
        handed[0] = end

    def hand_over_last():
        for dy in range(1, ny):
            arrived(group_down(dy), shard_at(sequence[-1]))
            hand_over(dy, shard_at(sequence[-1])).start()

    def add_batch(n):
        groups, core, start = batches[n]

        @pl.when(parity != core)
        def _():
            for k in range(start, start + part):
                for grp in groups:
                    arrived(grp, shard_at(k))

        if not early:
            batch_one_hots(n)
        at = n if early else 0
        blocks = [(grp, shard_at(k)) for grp in groups for k in range(start, start + part)]
        ends = [last_columns(gbuf[grp, src, chunks * cap : chunks * cap + 8, :]) for grp, src in blocks]
        for c in range(chunks + 1):
            size = LANE if c < chunks else rest
            put = slice(c * LANE, c * LANE + size)
            if c < chunks:
                e = [gbuf[grp, src, c * cap : c * cap + CAP_E, :] for grp, src in blocks]
                r = [gbuf[grp, src, c * cap + CAP_E : (c + 1) * cap, :] for grp, src in blocks]
            else:
                e, r = [x[0] for x in ends], [x[1] for x in ends]
            terms = jnp.concatenate(halves(jnp.concatenate(e, axis=0).T[0:size, :]), axis=0)
            sums_e = mm(terms, oh_e[at])
            terms = jnp.concatenate(halves(jnp.concatenate(r, axis=0).T[0:size, :]), axis=1)
            sums_r = mm(terms, oh_r[at])
            if n:
                ge_ref[put, :] += sums_e[0:size] + sums_e[size:]
                gr_ref[put, :] += sums_r[:, 0:nr]
            else:
                ge_ref[put, :] = sums_e[0:size] + sums_e[size:]
                gr_ref[put, :] = sums_r[:, 0:nr]

    def drain_sends(ks):
        for k in ks:
            for copy in forward(shard_at(k)):
                copy.wait_send()
            for dy in range(1, ny):
                hand_over(dy, shard_at(k)).wait_send()

    def pass_on(idx):
        k = sequence[idx]
        if k:
            arrived(g, shard_at(k))
        for copy in forward(shard_at(k)):
            copy.start()

    for idx in range(ns):
        pass_on(idx)
        hand_over_to(idx + 1 - lag)
    for copy in local[7:]:
        copy.wait()
    for k in near:
        ids_copy(k).wait_send()
        grad_copy(k).wait_send()
    for k in range(1, ng):
        idg_copy(k).wait_send()
    quarter = len(batches) // 4
    for n in range(quarter):
        add_batch(n)
    hand_over_to(ns - 1)

    @pl.when(parity == 0)
    def _():
        hand_over_last()

    for n in range(quarter, 2 * quarter):
        add_batch(n)

    @pl.when(parity == 1)
    def _():
        hand_over_last()

    drain_sends(sequence[:-2])
    for n in range(2 * quarter, 4 * quarter):
        add_batch(n)

    def stat(i, total):
        for r in range(ns):
            total += gbuf[i, r, chunks * cap : chunks * cap + 8, :]
        return total

    stat_ref[...] = lax.fori_loop(0, ng, stat, jnp.zeros((8, LANE), F32))

    drain_sends(sequence[-2:])


def adamw_kernel(
    at_loss,
    strip,
    stat_ref,
    ge_ref,
    gr_ref,
    w_e,
    one_e,
    two_e,
    w_r,
    one_r,
    two_r,
    e_new,
    e_one,
    e_two,
    e_low,
    r_new,
    r_one,
    r_two,
    r_low,
    loss_ref,
    pairs_ref,
    *scratch,
):
    d = ge_ref.shape[0]
    sems = scratch[-1]
    total = stat_ref[0:1, :]
    sums = [
        pltpu.make_async_copy(buf, out, sems.at[n, 0])
        for n, (buf, out) in enumerate(zip(scratch[8:10], (loss_ref, pairs_ref)), 8)
    ]
    for n, copy in enumerate(sums):
        scratch[8 + n][0] = total[0, at_loss + n]
        copy.start()
    factor = ((1.0 - BETA_ONE) / total)[0, at_loss + 1]
    square = (1.0 - BETA_TWO) / (1.0 - BETA_ONE) ** 2
    fix_two = 1.0 / (1.0 - BETA_TWO**STEP)
    rate = RATE / (1.0 - BETA_ONE**STEP)
    tables = (
        (ge_ref, w_e, one_e, two_e, (e_new, e_one, e_two, e_low), scratch[0:4]),
        (gr_ref, w_r, one_r, two_r, (r_new, r_one, r_two, r_low), scratch[4:8]),
    )

    def copies(i):
        at = pl.ds(pl.multiple_of(i * strip, strip), strip)
        out = []
        for n, (_, _, _, _, outs, bufs) in enumerate(tables):
            for m, (hbm, buf) in enumerate(zip(outs, bufs)):
                out.append(pltpu.make_async_copy(buf.at[at, :], hbm.at[at, :], sems.at[n * 4 + m, i]))
        return out

    def step(i, _):
        for g_ref, w_ref, one_ref, two_ref, _, bufs in tables:

            def rows(j, _):
                at = pl.ds(pl.multiple_of(i * strip, 16), strip)
                gradient = g_ref[at, :] * factor
                weight = w_ref[at, :]
                one = BETA_ONE * one_ref[at, :] + gradient
                two = BETA_TWO * two_ref[at, :] + square * gradient * gradient
                scaled = two * fix_two
                root = scaled * lax.rsqrt(scaled) + EPS_ADAM
                new = weight * (1.0 - RATE * DECAY) - rate * one / root
                bufs[0][at, :] = new
                bufs[1][at, :] = one
                bufs[2][at, :] = two
                bufs[3][at, :] = new.astype(BF16)
                return 0

            rows(0, 0)
        for copy in copies(i):
            copy.start()
        return 0

    steps = d // strip
    lax.fori_loop(0, steps, step, 0)
    for i in range(steps):
        for copy in copies(i):
            copy.wait()
    for copy in sums:
        copy.wait()


def per_device(
    ns,
    ng,
    entity_rows,
    entity_first,
    entity_second,
    relation_rows,
    relation_first,
    relation_second,
    requests,
    head_slots,
    relation_slots,
    tail_slots,
    neg_offsets,
    valid_counts,
):
    ne, d = entity_rows.shape
    nr = relation_rows.shape[0]
    cap = requests.shape[2]
    cap_r = cap - CAP_E
    edges, neg = neg_offsets.shape
    segs = edges // SEG
    ke, kr = ns * CAP_E, ns * cap_r
    chunks = d // LANE
    rest = d - chunks * LANE
    dp = (chunks + 1) * LANE
    nrp = up(nr, LANE)
    ny = ng // 2
    block = (LANE, LANE)
    any_space = pl.BlockSpec(memory_space=pl.ANY)
    vmem = pl.BlockSpec(memory_space=pltpu.VMEM)
    smem = pl.BlockSpec(memory_space=pltpu.SMEM)
    dma = pltpu.SemaphoreType.DMA
    hbm = functools.partial(pltpu.with_memory_space_constraint, memory_space=pltpu.HBM)
    batches = ng if ng <= 4 else 1
    scratch = [
        pltpu.VMEM((ns, cap), I32),
        pltpu.VMEM((3, segs, SEG), I32),
        pltpu.VMEM((neg, edges), I32),
        pltpu.VMEM((dp, ne), BF16),
        pltpu.VMEM((dp, ne), BF16),
        pltpu.VMEM((dp, nrp), BF16),
        pltpu.VMEM((dp, nrp), BF16),
        pltpu.VMEM((ns, ns, cap), I32),
        pltpu.VMEM((ng, ns, cap), I32),
        pltpu.VMEM((ns, *block), F32),
        pltpu.VMEM((ns, *block), F32),
        pltpu.VMEM((ke, dp), F32),
        pltpu.VMEM((kr, dp), F32),
        pltpu.VMEM((batches, ke, ne), BF16),
        pltpu.VMEM((batches, 2 * kr, nrp), BF16),
        pltpu.VMEM((edges, ke), BF16),
        pltpu.VMEM((edges, ke), BF16),
        pltpu.VMEM((edges, 2 * kr), BF16),
        pltpu.VMEM((ke + kr, edges), BF16),
        pltpu.VMEM((ke, edges), BF16),
        pltpu.VMEM((segs, SEG, SEG), F32),
        pltpu.VMEM((ke, dp), BF16),
        pltpu.VMEM((ke, dp), BF16),
        pltpu.VMEM((2 * kr, dp), BF16),
        pltpu.VMEM((2 * edges, dp), BF16),
        pltpu.VMEM((2 * edges, dp), BF16),
        pltpu.VMEM((3, segs, SEG, SEG), F32),
        pltpu.VMEM((segs, SEG, SEG), F32),
        pltpu.VMEM((8, edges), F32),
        pltpu.VMEM((2 * edges, 2 * SEG), BF16),
        pltpu.VMEM((edges, ke), BF16),
        pltpu.VMEM((edges, ke), BF16),
        pltpu.VMEM((ng, ns, *block), F32),
        pltpu.VMEM((d, 2 * ke), BF16),
        pltpu.VMEM((d, 2 * kr), BF16),
        dma((11,)),
        dma((ns,)),
        dma((ns,)),
        dma((ng,)),
        dma((ng,)),
        dma((ns,)),
        dma((ns,)),
        dma((ns,)),
        dma((ng, ns)),
        dma((ny, ns)),
        dma((max(ny - 1, 1), ns)),
        pltpu.SemaphoreType.REGULAR,
    ]
    small = [
        requests[0],
        head_slots.reshape(segs, SEG),
        relation_slots.reshape(segs, SEG),
        tail_slots.reshape(segs, SEG),
        neg_offsets.T,
    ]
    rows = [entity_rows.T, relation_rows.T]
    moments = [entity_first.T, entity_second.T, relation_first.T, relation_second.T]
    sums = [pltpu.VMEM((d, ne), F32), pltpu.VMEM((d, nr), F32), pltpu.VMEM((8, LANE), F32)]
    held_rows = [pltpu.VMEM(x.shape, F32) for x in rows]
    held_moments = [pltpu.VMEM(x.shape, F32) for x in moments]
    need = sum(padded(x) for x in scratch[: scratch.index(dma((11,)))]) + (2 << 20)
    keep = need + sum(padded(x) for x in sums + held_rows + held_moments) < (62 << 20)
    if keep:
        outs, held = sums + held_rows + held_moments, []
    else:
        outs, held = sums, held_rows
        need += sum(padded(x) for x in held)
    operands = small + rows + (moments if keep else [])
    ge, gr, stat, *passed = pl.pallas_call(
        functools.partial(exchange_kernel, ns, ng, (d, ne, nr, cap, edges, neg), int(keep), batches > 1),
        out_shape=outs,
        in_specs=[smem] + [any_space] * len(operands),
        out_specs=[vmem] * len(outs),
        scratch_shapes=held + scratch,
        compiler_params=pltpu.CompilerParams(
            collective_id=0, has_side_effects=True, vmem_limit_bytes=need
        ),
    )(valid_counts, *[hbm(x) for x in operands])
    if not keep:
        passed = rows + moments
    w_e, w_r, one_e, two_e, one_r, two_r = passed
    tables = (w_e, one_e, two_e, w_r, one_r, two_r)
    at_loss = LANE // rest * rest - 2
    strip = 80
    shapes = [(jax.ShapeDtypeStruct((d, n), t)) for n in (ne, nr) for t in (F32, F32, F32, BF16)]
    one = jax.ShapeDtypeStruct((1,), F32)
    *outs, loss, pairs = pl.pallas_call(
        functools.partial(adamw_kernel, at_loss, strip),
        out_shape=shapes + [one, one],
        in_specs=[vmem] * 9,
        out_specs=[any_space] * 10,
        scratch_shapes=[pltpu.VMEM(x.shape, x.dtype) for x in shapes] + [pltpu.SMEM((1,), F32)] * 2 + [dma((10, d // strip))],
        compiler_params=pltpu.CompilerParams(vmem_limit_bytes=32 * 1024 * 1024),
    )(stat, ge, gr, *tables)
    e_new, e_one, e_two, e_low, r_new, r_one, r_two, r_low = (x.T for x in outs)
    return (e_new, e_one, e_two, r_new, r_one, r_two, e_low, r_low, loss, pairs)


def solution(mesh):
    rows = P("shard", None)
    both = ("grp", "shard")
    return jax.shard_map(
        functools.partial(per_device, mesh.shape["shard"], mesh.shape["grp"]),
        mesh=mesh,
        in_specs=(
            rows,
            rows,
            rows,
            rows,
            rows,
            rows,
            P(both, None, None),
            P(both),
            P(both),
            P(both),
            P(both, None),
            P(both),
        ),
        out_specs=(rows,) * 8 + (P(), P()),
        check_vma=False,
    )
```
